32 devices in a mesh: row: 8 (over y, x, core), col: 4 (over z).
Axes of the slice: x: 2, y: 2, z: 4, core: 2. Of those that a mesh axis runs over, the one named last changes fastest.
Arguments:
- noise: bfloat16 [1024, 16384], P('row', 'col'), as said below
- data: bfloat16 [1024, 16384], P('col', 'row'), may hold values from -5 to 5
Outputs:
- targets: bfloat16 [1024, 16384], P(('row', 'col'))
- noise_potential: float32 [1024], P('row')
- data_potential: float32 [1024], P('col')
The draws below stay inside these ranges and needn't reach their ends.
Inputs may be any that keep to these rules, and one draw needn't show every extreme that they name: noise latents, real values of order one.
All inputs are finite; a program needn't handle non-finite values.
Results may differ from the reference program's by a relative error of at most 0.022.
Values may be sent and summed in bfloat16 or wider, within the bound.
No kernel may reach another device: no remote copies, remote signals or barrier semaphores. Data moves between devices by JAX's collectives and lax.ppermute only.
A program may use at most 64 MiB of HBM per device.

```python
import math
import jax
import jax.numpy as jnp
from jax import lax

LATENT = 16384
ITERS = 3
DATA_DEV = 256
NOISE = 1024
DATA = 1024
N_COL = 4


def data_latents(key):
    return jnp.clip(jax.random.normal(key, (DATA, LATENT), jnp.float32), -5.0, 5.0)


def draw_data(key, part):
    shared = data_latents(key)
    return shared.astype(jnp.bfloat16)


def draw_noise(key, part):
    key = jax.random.fold_in(key, 7)
    first = jax.random.fold_in(key, 0)
    values = jnp.clip(jax.random.normal(first, (NOISE, LATENT), jnp.float32), -5.0, 5.0)
    return values.astype(jnp.bfloat16)


def setup_inputs(seed: int = 0) -> dict:
    splits = jax.random.split(jax.random.key(seed), 3)
    noise = draw_noise(jax.random.fold_in(splits[2], 71), 0)
    data = draw_data(jax.random.fold_in(splits[2], 71), 0)
    return dict(noise=noise, data=data)


def soft_max_log(scores, axis):
    peak = lax.optimization_barrier(jnp.max(scores, axis=axis, keepdims=True))
    return jnp.squeeze(peak, axis) + jnp.log(lax.optimization_barrier(jnp.sum(jnp.exp(scores - peak), axis=axis)))

def reference(noise, data):
    epsilon = 0.64 / math.sqrt(LATENT)
    noise_norm = lax.optimization_barrier(jnp.sum(jnp.square(noise.astype(jnp.float32)), axis=1)) / LATENT
    data_norm = lax.optimization_barrier(jnp.sum(jnp.square(data.astype(jnp.float32)), axis=1)) / LATENT
    cross = lax.dot_general(noise, data, (((1,), (1,)), ((), ())), preferred_element_type=jnp.float32)
    cost_tile = noise_norm[:, None] + data_norm[None, :] - 2.0 / LATENT * cross
    log_noise = math.log(NOISE)
    log_data = math.log(DATA)

    def row_update(data_pot):
        return -epsilon * (log_noise + soft_max_log((data_pot[None, :] - cost_tile) / epsilon, 1))

    def col_update(noise_pot):
        return -epsilon * (log_data + soft_max_log((noise_pot[:, None] - cost_tile) / epsilon, 0))
    data_pot = jnp.zeros((DATA,), jnp.float32)
    for step in range(ITERS):
        noise_pot = row_update(data_pot)
        data_pot = col_update(noise_pot)
    noise_pot = row_update(data_pot)
    weights = jnp.exp((noise_pot[:, None] + data_pot[None, :] - cost_tile) / epsilon + log_noise).astype(jnp.bfloat16)

    def add_block(index, summed):
        begin = (index * DATA_DEV).astype(jnp.int32)
        block_weights = lax.dynamic_slice_in_dim(weights, begin, DATA_DEV, 1)
        block_data = lax.dynamic_slice_in_dim(data, begin, DATA_DEV, 0)
        partial_sum = jnp.dot(block_weights, block_data, preferred_element_type=jnp.float32).astype(jnp.bfloat16)
        partial_sum = lax.optimization_barrier(partial_sum)
        return summed + partial_sum.astype(jnp.float32)
    summed = lax.fori_loop(0, N_COL, add_block, jnp.zeros((NOISE, LATENT), jnp.float32))
    return (summed.astype(jnp.bfloat16), noise_pot, data_pot)
```

```python
import functools
import math

import jax
import jax.numpy as jnp
from jax import lax
from jax.experimental import pallas as pl
from jax.experimental.pallas import tpu as pltpu
from jax.sharding import PartitionSpec as P

LATENT = 16384
ITERS = 3
EPSILON = 0.64 / math.sqrt(LATENT)
LOG2E = math.log2(math.e)
TO_LOG2 = LOG2E / EPSILON
CONTRACT = (((1,), (1,)), ((), ()))
LOCAL_COST_BYTES = 8 * 2**20


def noise_update(cost_tile, data_pot, epsilon, log_count):
    scores = (data_pot[None, :] - cost_tile) / epsilon
    local_peak = jnp.max(scores, axis=1)
    highest = lax.pmax(local_peak, "col")
    summed = lax.psum(jnp.sum(jnp.exp(scores - highest[:, None]), axis=1), "col")
    return -epsilon * (log_count + highest + jnp.log(summed))


def data_update(cost_tile, noise_pot, epsilon, log_count):
    scores = (noise_pot[:, None] - cost_tile) / epsilon
    local_peak = jnp.max(scores, axis=0)
    highest = lax.pmax(local_peak, "row")
    summed = lax.psum(jnp.sum(jnp.exp(scores - highest[None, :]), axis=0), "row")
    return -epsilon * (log_count + highest + jnp.log(summed))


def per_device_tiled(noise, data):
    epsilon = EPSILON
    noise_full = lax.all_gather(noise, "col", axis=1, tiled=True)
    noise_norm = jnp.sum(jnp.square(noise_full.astype(jnp.float32)), axis=1) / LATENT
    noise_rows = noise.shape[0]
    data_rows = data.shape[0]
    data_full = lax.all_gather(data, "row", axis=1, tiled=True)
    data_norm = jnp.sum(jnp.square(data_full.astype(jnp.float32)), axis=1) / LATENT
    cross = lax.dot_general(noise_full, data_full, CONTRACT, preferred_element_type=jnp.float32)
    cost_tile = noise_norm[:, None] + data_norm[None, :] - 2.0 / LATENT * cross
    log_noise = math.log(noise_rows * lax.axis_size("row"))
    log_data = math.log(data_rows * lax.axis_size("col"))
    data_pot = jnp.zeros((data_rows,), jnp.float32)
    for step in range(ITERS):
        noise_pot = noise_update(cost_tile, data_pot, epsilon, log_noise)
        data_pot = data_update(cost_tile, noise_pot, epsilon, log_data)
    noise_pot = noise_update(cost_tile, data_pot, epsilon, log_noise)
    weights = jnp.exp(
        (noise_pot[:, None] + data_pot[None, :] - cost_tile) / epsilon + log_noise
    ).astype(jnp.bfloat16)
    targets = lax.psum_scatter(
        jnp.dot(weights, data_full, preferred_element_type=jnp.float32).astype(jnp.bfloat16),
        "col",
        scatter_dimension=0,
        tiled=True,
    )
    return (targets, noise_pot, data_pot)


def swap_row(array, step):
    count = lax.axis_size("row")
    return lax.ppermute(array, "row", [(i, i ^ step) for i in range(count)])


def swap_col(array, step):
    count = lax.axis_size("col")
    return lax.ppermute(array, "col", [(i, i ^ step) for i in range(count)])


def plane_gather(pieces):
    half = len(pieces) // 2
    along_x = [swap_row(piece, 2) for piece in pieces]
    along_y = [swap_row(piece, 4) for piece in pieces]
    across = [swap_row(piece, 4) for piece in along_x[:half]]
    across += [swap_row(piece, 2) for piece in along_y[half:]]
    result = []
    for group in (pieces, along_x, along_y, across):
        result += [group, [swap_row(piece, 1) for piece in group]]
    return result


def place():
    return lax.axis_index("row"), lax.axis_index("col")


ANY = pl.BlockSpec(memory_space=pl.ANY)
VMEM = pl.BlockSpec(memory_space=pltpu.VMEM)


def run_copies(copies):
    for copy in copies:
        copy.start()
    for copy in copies:
        copy.wait()


def deal_kernel(data_ref, *refs):
    *outs, sems = refs
    row, _ = place()
    count = outs[0].shape[0]
    copies = []
    for k, out in enumerate(outs, 1):
        rows = pl.ds(pl.multiple_of((row ^ k) * count, count), count)
        copies.append(pltpu.make_async_copy(data_ref.at[rows], out, sems.at[k]))
    run_copies(copies)


def deal(data, n_row):
    share = data.shape[0] // n_row
    piece = jax.ShapeDtypeStruct((share, data.shape[1]), data.dtype)
    return pl.pallas_call(
        deal_kernel,
        in_specs=[ANY],
        out_specs=[ANY] * (n_row - 1),
        out_shape=[piece] * (n_row - 1),
        scratch_shapes=[pltpu.SemaphoreType.DMA((n_row,))],
    )(data)


def regroup_kernel(n_row, n_col, *refs):
    data_ref, noise_ref = refs[:2]
    received = refs[2 : 1 + n_row]
    outs = refs[1 + n_row : 1 + n_row + n_col]
    low_ref, high_ref, sems = refs[1 + n_row + n_col :]
    row, col = place()
    share, wide = received[0].shape
    per_plane = n_row // n_col
    own = pl.ds(pl.multiple_of(row * share, share), share)
    half = low_ref.shape[0]
    halves = [
        pltpu.make_async_copy(noise_ref.at[pl.ds(0, half)], low_ref, sems.at[n_row]),
        pltpu.make_async_copy(noise_ref.at[pl.ds(half, half)], high_ref, sems.at[n_row + 1]),
    ]
    for k in range(n_row):
        source = data_ref.at[own] if k == 0 else received[k - 1]
        origin = row ^ k
        lanes = pl.ds(pl.multiple_of(lax.rem(origin, per_plane) * wide, wide), wide)
        step = col ^ (origin // per_plane)
        for d in range(n_col):

            @pl.when(step == d)
            def _():
                pltpu.make_async_copy(source, outs[d].at[:, lanes], sems.at[k]).start()

    for copy in halves:
        copy.start()
    for k in range(n_row):
        source = data_ref.at[own] if k == 0 else received[k - 1]
        pltpu.make_async_copy(source, outs[0].at[:, pl.ds(0, wide)], sems.at[k]).wait()
    for copy in halves:
        copy.wait()


def regroup(data, noise, received, n_col):
    n_row = len(received) + 1
    share, wide = received[0].shape
    piece = jax.ShapeDtypeStruct((share, wide * (n_row // n_col)), data.dtype)
    half = jax.ShapeDtypeStruct((noise.shape[0] // 2, noise.shape[1]), noise.dtype)
    return pl.pallas_call(
        functools.partial(regroup_kernel, n_row, n_col),
        in_specs=[ANY] * (n_row + 1),
        out_specs=[ANY] * (n_col + 2),
        out_shape=[piece] * n_col + [half] * 2,
        scratch_shapes=[pltpu.SemaphoreType.DMA((n_row + 2,))],
    )(data, noise, *received)


def stack_kernel(*refs):
    *pieces, low_ref, high_ref, sems = refs
    _, col = place()
    half = low_ref.shape[0]
    for d, piece in enumerate(pieces):
        origin = col ^ d
        slot = lax.rem(origin, half)

        @pl.when(origin < half)
        def _():
            pltpu.make_async_copy(piece, low_ref.at[slot], sems.at[d]).start()

        @pl.when(origin >= half)
        def _():
            pltpu.make_async_copy(piece, high_ref.at[slot], sems.at[d]).start()

    for d, piece in enumerate(pieces):
        pltpu.make_async_copy(piece, low_ref.at[0], sems.at[d]).wait()


def stack(pieces):
    half = jax.ShapeDtypeStruct((len(pieces) // 2,) + pieces[0].shape, pieces[0].dtype)
    return pl.pallas_call(
        stack_kernel,
        in_specs=[ANY] * len(pieces),
        out_specs=[ANY] * 2,
        out_shape=[half] * 2,
        scratch_shapes=[pltpu.SemaphoreType.DMA((len(pieces),))],
    )(*pieces)


def cost_kernel(n_row, n_col, *refs):
    noise_refs = refs[: 2 * n_row]
    low_ref, high_ref = refs[2 * n_row : 2 * n_row + 2]
    parts = refs[2 * n_row + 2 : 2 * n_row + 2 + n_col]
    noise_all, data_all, noise_sems, data_sems = refs[2 * n_row + 2 + n_col :]
    row, col = place()
    per_part = n_row // n_col
    half = n_col // 2
    data_copies = [
        pltpu.make_async_copy(low_ref, data_all.at[pl.ds(0, half)], data_sems.at[0]),
        pltpu.make_async_copy(high_ref, data_all.at[pl.ds(half, half)], data_sems.at[1]),
    ]
    for copy in data_copies:
        copy.start()

    def noise_copy(k, h, origin):
        return pltpu.make_async_copy(
            noise_refs[2 * k + h], noise_all.at[origin, h], noise_sems.at[origin, h]
        )

    for k in range(n_row):
        for h in range(2):
            noise_copy(k, h, row ^ k).start()
    for copy in data_copies:
        copy.wait()
    depth = data_all.shape[-1]
    columns = data_all.shape[0] * data_all.shape[1]
    rows_data = data_all[...].reshape(columns, depth)
    values = rows_data.astype(jnp.float32)
    norm = jnp.sum(values * values, axis=1, keepdims=True)
    norm = jnp.broadcast_to(norm, (columns, columns)).T[0:1, :]
    for d in range(n_col):
        first = (col ^ d) * per_part
        for i in range(per_part):
            for h in range(2):
                noise_copy(0, h, first + i).wait()
        rows = noise_all[pl.ds(first, per_part)].reshape(-1, depth)
        cross = lax.dot_general(rows, rows_data, CONTRACT, preferred_element_type=jnp.float32)
        values = rows.astype(jnp.float32)
        part = jnp.sum(values * values, axis=1, keepdims=True)
        parts[d][...] = (part + norm - 2.0 * cross) * (TO_LOG2 / LATENT)


def partial_cost(noise_pieces, data_halves, n_col):
    n_row = len(noise_pieces)
    half, depth = noise_pieces[0][0].shape
    columns = 2 * data_halves[0].shape[0] * data_halves[0].shape[1]
    rows = 2 * half * n_row
    return pl.pallas_call(
        functools.partial(cost_kernel, n_row, n_col),
        in_specs=[ANY] * (2 * n_row + 2),
        out_specs=[VMEM] * n_col,
        out_shape=[jax.ShapeDtypeStruct((rows // n_col, columns), jnp.float32)] * n_col,
        scratch_shapes=[
            pltpu.VMEM((n_row, 2, half, depth), jnp.bfloat16),
            pltpu.VMEM((n_col,) + data_halves[0].shape[1:], jnp.bfloat16),
            pltpu.SemaphoreType.DMA((n_row, 2)),
            pltpu.SemaphoreType.DMA((2,)),
        ],
        compiler_params=pltpu.CompilerParams(vmem_limit_bytes=40 * 2**20),
        cost_estimate=pl.CostEstimate(
            flops=2 * rows * columns * depth, bytes_accessed=2 * rows * depth, transcendentals=0
        ),
    )(*[piece for pair in noise_pieces for piece in pair], *data_halves)


def sinkhorn_kernel(n_row, n_col, *refs):
    cost_refs = refs[: n_row * n_col]
    data_refs = refs[n_row * n_col : n_row * (n_col + 2)]
    refs = refs[n_row * (n_col + 2) :]
    target_refs, refs = refs[:n_col], refs[n_col:]
    noise_pot_ref, data_pot_ref, cost, data_all, f_ref, weights, product, cost_sems, data_sems = refs
    row, col = place()
    wide, tall, height, width = cost.shape
    log_noise = math.log2(tall * height)
    log_data = math.log2(wide * width)
    blocks = range(wide)
    half = n_col // 2
    cost_copies, data_copies = [], []
    for k in range(n_row):
        for d in range(n_col):
            slot = cost.at[row ^ k, col ^ d]
            cost_copies.append(
                pltpu.make_async_copy(cost_refs[k * n_col + d], slot, cost_sems.at[k, d])
            )
        for h in range(2):
            slot = data_all.at[row ^ k, pl.ds(h * half, half)]
            data_copies.append(pltpu.make_async_copy(data_refs[2 * k + h], slot, data_sems.at[k, h]))
    for copy in cost_copies + data_copies:
        copy.start()
    for copy in cost_copies:
        copy.wait()

    def row_update(tiles, g):
        peak = functools.reduce(jnp.maximum, [g[b] - tiles(b) for b in blocks])
        peak = jnp.max(peak, axis=1, keepdims=True)
        total = functools.reduce(jnp.add, [jnp.exp2(g[b] - tiles(b) - peak) for b in blocks])
        total = jnp.sum(total, axis=1, keepdims=True)
        return -(log_noise + peak + jnp.log2(total))

    def both_updates(chunk, carry, g):
        high, summed = carry
        f = row_update(lambda b: cost[b, chunk], g)
        new_high, new_summed = [], []
        for b in blocks:
            scores = f - cost[b, chunk]
            peak = jnp.max(scores, axis=0, keepdims=True)
            total = jnp.sum(jnp.exp2(scores - peak), axis=0, keepdims=True)
            top = jnp.maximum(high[b], peak)
            new_high.append(top)
            new_summed.append(summed[b] * jnp.exp2(high[b] - top) + total * jnp.exp2(peak - top))
        return tuple(new_high), tuple(new_summed)

    def iteration(_, g):
        first = (
            tuple(jnp.full((1, width), -jnp.inf, jnp.float32) for b in blocks),
            tuple(jnp.zeros((1, width), jnp.float32) for b in blocks),
        )
        high, summed = lax.fori_loop(0, tall, lambda i, carry: both_updates(i, carry, g), first)
        return tuple(-(log_data + high[b] + jnp.log2(summed[b])) for b in blocks)

    g = tuple(jnp.zeros((1, width), jnp.float32) for b in blocks)
    g = lax.fori_loop(0, ITERS, iteration, g)
    for b in blocks:
        data_pot_ref[b : b + 1, :] = g[b] * (1.0 / TO_LOG2)

    own = noise_pot_ref.shape[1]
    per_chunk = height // own
    chunk = row // per_chunk
    rows = pl.ds(pl.multiple_of(lax.rem(row, per_chunk) * own, own), own)
    f = row_update(lambda b: cost[b, chunk, rows, :], g)
    for b in blocks:
        scores = (f + g[b] - cost[b, chunk, rows, :]) + log_noise
        weights[:, b * width : (b + 1) * width] = jnp.exp2(scores).astype(jnp.bfloat16)
    f_ref[...] = jnp.broadcast_to(f, f_ref.shape)
    noise_pot_ref[...] = f_ref[...].T[0:1, :] * (1.0 / TO_LOG2)

    for copy in data_copies:
        copy.wait()
    depth = data_all.shape[-1]
    piece = min(depth, 512)
    share = own // n_col

    def multiply(i, _):
        lanes = pl.ds(pl.multiple_of(i * piece, piece), piece)
        latents = data_all[:, :, :, lanes].reshape(wide * width, piece)
        product[...] = jnp.dot(weights[...], latents, preferred_element_type=jnp.float32)
        for d in range(n_col):
            rows = pl.ds(pl.multiple_of((col ^ d) * share, share), share)
            target_refs[d][:, lanes] = product[rows, :].astype(jnp.bfloat16)
        return 0

    lax.fori_loop(0, depth // piece, multiply, 0)


def sinkhorn(tiles, latents, own):
    n_row, n_col = len(tiles), len(tiles[0])
    height, width = tiles[0][0].shape
    half, share, depth = latents[0][0].shape
    size = n_row * n_col * height * width
    return pl.pallas_call(
        functools.partial(sinkhorn_kernel, n_row, n_col),
        in_specs=[ANY] * (n_row * (n_col + 2)),
        out_specs=[VMEM] * (n_col + 2),
        out_shape=[jax.ShapeDtypeStruct((own // n_col, depth), jnp.bfloat16)] * n_col
        + [
            jax.ShapeDtypeStruct((1, own), jnp.float32),
            jax.ShapeDtypeStruct((n_row, width), jnp.float32),
        ],
        scratch_shapes=[
            pltpu.VMEM((n_row, n_col, height, width), jnp.float32),
            pltpu.VMEM((n_row, n_col, share, depth), jnp.bfloat16),
            pltpu.VMEM((own, own), jnp.float32),
            pltpu.VMEM((own, n_row * width), jnp.bfloat16),
            pltpu.VMEM((own, min(depth, 512)), jnp.float32),
            pltpu.SemaphoreType.DMA((n_row, n_col)),
            pltpu.SemaphoreType.DMA((n_row, 2)),
        ],
        compiler_params=pltpu.CompilerParams(vmem_limit_bytes=48 * 2**20),
        cost_estimate=pl.CostEstimate(
            flops=60 * size, bytes_accessed=8 * size, transcendentals=8 * size
        ),
    )(*[tile for group in tiles for tile in group], *[piece for group in latents for piece in group])


def join_kernel(*refs):
    *pieces, out_ref, sems = refs
    _, col = place()
    depth = pieces[0].shape[1]
    copies = []
    for d, piece in enumerate(pieces):
        lanes = pl.ds(pl.multiple_of((col ^ d) * depth, depth), depth)
        copies.append(pltpu.make_async_copy(piece, out_ref.at[:, lanes], sems.at[d]))
    run_copies(copies)


def join(pieces):
    share, depth = pieces[0].shape
    return pl.pallas_call(
        join_kernel,
        in_specs=[ANY] * len(pieces),
        out_specs=ANY,
        out_shape=jax.ShapeDtypeStruct((share, depth * len(pieces)), pieces[0].dtype),
        scratch_shapes=[pltpu.SemaphoreType.DMA((len(pieces),))],
    )(*pieces)


def col_exchange(pieces):
    return [pieces[0]] + [swap_col(piece, d) for d, piece in enumerate(pieces) if d]


def per_device_local(noise, data):
    n_row, n_col = lax.axis_size("row"), lax.axis_size("col")
    own, own_data = noise.shape[0], data.shape[0]
    received = [swap_row(piece, k) for k, piece in enumerate(deal(data, n_row), 1)]
    *spread, low, high = regroup(data, noise, received, n_col)
    mine = stack(col_exchange(spread))
    noise_plane = plane_gather([low, high])
    parts = partial_cost(noise_plane, mine, n_col)
    data_plane = plane_gather(mine)
    tile = functools.reduce(jnp.add, col_exchange(parts))
    tiles = plane_gather([tile] + [swap_col(tile, d) for d in range(1, n_col)])
    *products, noise_pot, pots = sinkhorn(tiles, data_plane, own)
    share = own_data // n_row
    data_pot = lax.dynamic_slice_in_dim(pots, lax.axis_index("col") * share, share, 1)
    targets = join(col_exchange(products))
    return (targets, noise_pot.reshape((own,)), data_pot.reshape((own_data,)))


def per_device(noise, data):
    n_row, n_col = lax.axis_size("row"), lax.axis_size("col")
    whole = 4 * noise.shape[0] * n_row * data.shape[0] * n_col
    if whole <= LOCAL_COST_BYTES and n_row == 8 and n_col == 4:
        return per_device_local(noise, data)
    return per_device_tiled(noise, data)


def solution(mesh):
    placed = (P("row", "col"), P("col", "row"))
    return jax.shard_map(
        per_device,
        mesh=mesh,
        in_specs=placed,
        out_specs=(P(("row", "col"), None), P("row"), P("col")),
        check_vma=False,
    )
```

```python
import functools
import math

import jax
import jax.numpy as jnp
from jax import lax
from jax.experimental import pallas as pl
from jax.experimental.pallas import tpu as pltpu
from jax.sharding import PartitionSpec as P

LATENT = 16384
ITERS = 3
EPSILON = 0.64 / math.sqrt(LATENT)
LOG2E = math.log2(math.e)
TO_LOG2 = LOG2E / EPSILON
CONTRACT = (((1,), (1,)), ((), ()))
LOCAL_COST_BYTES = 8 * 2**20


def noise_update(cost_tile, data_pot, epsilon, log_count):
    scores = (data_pot[None, :] - cost_tile) / epsilon
    local_peak = jnp.max(scores, axis=1)
    highest = lax.pmax(local_peak, "col")
    summed = lax.psum(jnp.sum(jnp.exp(scores - highest[:, None]), axis=1), "col")
    return -epsilon * (log_count + highest + jnp.log(summed))


def data_update(cost_tile, noise_pot, epsilon, log_count):
    scores = (noise_pot[:, None] - cost_tile) / epsilon
    local_peak = jnp.max(scores, axis=0)
    highest = lax.pmax(local_peak, "row")
    summed = lax.psum(jnp.sum(jnp.exp(scores - highest[None, :]), axis=0), "row")
    return -epsilon * (log_count + highest + jnp.log(summed))


def per_device_tiled(noise, data):
    epsilon = EPSILON
    noise_full = lax.all_gather(noise, "col", axis=1, tiled=True)
    noise_norm = jnp.sum(jnp.square(noise_full.astype(jnp.float32)), axis=1) / LATENT
    noise_rows = noise.shape[0]
    data_rows = data.shape[0]
    data_full = lax.all_gather(data, "row", axis=1, tiled=True)
    data_norm = jnp.sum(jnp.square(data_full.astype(jnp.float32)), axis=1) / LATENT
    cross = lax.dot_general(noise_full, data_full, CONTRACT, preferred_element_type=jnp.float32)
    cost_tile = noise_norm[:, None] + data_norm[None, :] - 2.0 / LATENT * cross
    log_noise = math.log(noise_rows * lax.axis_size("row"))
    log_data = math.log(data_rows * lax.axis_size("col"))
    data_pot = jnp.zeros((data_rows,), jnp.float32)
    for step in range(ITERS):
        noise_pot = noise_update(cost_tile, data_pot, epsilon, log_noise)
        data_pot = data_update(cost_tile, noise_pot, epsilon, log_data)
    noise_pot = noise_update(cost_tile, data_pot, epsilon, log_noise)
    weights = jnp.exp(
        (noise_pot[:, None] + data_pot[None, :] - cost_tile) / epsilon + log_noise
    ).astype(jnp.bfloat16)
    targets = lax.psum_scatter(
        jnp.dot(weights, data_full, preferred_element_type=jnp.float32).astype(jnp.bfloat16),
        "col",
        scatter_dimension=0,
        tiled=True,
    )
    return (targets, noise_pot, data_pot)


VMEM = pl.BlockSpec(memory_space=pltpu.VMEM)
WIDTH = 128


def place():
    return lax.axis_index("row"), lax.axis_index("col")


def swap(array, axis, step):
    count = lax.axis_size(axis)
    return lax.ppermute(array, axis, [(i, i ^ step) for i in range(count)])


def swap_core(array):
    return swap(array, "row", 1)


def swap_x(array):
    return swap(array, "row", 2)


def swap_y(array):
    return swap(array, "row", 4)


def col_exchange(pieces):
    return [pieces[0]] + [swap(piece, "col", d) for d, piece in enumerate(pieces) if d]


def chip_gather(pieces):
    along_x, along_y, across = [], [], []
    for i, piece in enumerate(pieces):
        along_x.append(swap_x(piece))
        along_y.append(swap_y(piece))
        across.append(swap_x(along_y[i]) if i % 2 else swap_y(along_x[i]))
    return [pieces, along_x, along_y, across]


def block(index, size):
    return pl.ds(pl.multiple_of(index * size, size), size)


def kernel_call(kernel, outs, scratch, vmem, *operands, flops=0):
    moved = sum(a.size * a.dtype.itemsize for a in operands)
    return pl.pallas_call(
        kernel,
        in_specs=[VMEM] * len(operands),
        out_specs=[VMEM] * len(outs),
        out_shape=[jax.ShapeDtypeStruct(shape, dtype) for shape, dtype in outs],
        scratch_shapes=scratch,
        compiler_params=pltpu.CompilerParams(vmem_limit_bytes=vmem * 2**20),
        cost_estimate=pl.CostEstimate(flops=flops, bytes_accessed=moved, transcendentals=0),
    )(*operands)


def chip_swap(piece, k):
    return swap(piece, "row", 2 * k) if k else piece


def deal_kernel(n_chip, data_ref, noise_ref, *outs):
    row, _ = place()
    core, chip = lax.rem(row, 2), row // 2
    share = data_ref.shape[0] // n_chip
    for k in range(n_chip):
        outs[k][...] = data_ref[block(chip ^ k, share), :]
    half = noise_ref.shape[1] // 2
    outs[n_chip][...] = noise_ref[:, block(core, half)]
    outs[n_chip + 1][...] = noise_ref[:, block(1 - core, half)]


def deal(data, noise, n_chip):
    piece = (data.shape[0] // n_chip, data.shape[1])
    half = (noise.shape[0], noise.shape[1] // 2)
    return kernel_call(
        functools.partial(deal_kernel, n_chip),
        [(piece, data.dtype)] * n_chip + [(half, noise.dtype)] * 2,
        [],
        12,
        data,
        noise,
    )


def regroup_kernel(n_col, *refs):
    row, col = place()
    pieces, outs = refs[:n_col], refs[n_col:]
    for d in range(n_col):
        for k in range(n_col):

            @pl.when((row // 2) ^ col ^ d == k)
            def _():
                outs[d][...] = pieces[k][...]


def regroup(pieces):
    n_col = len(pieces)
    out = (pieces[0].shape, pieces[0].dtype)
    return kernel_call(functools.partial(regroup_kernel, n_col), [out] * n_col, [], 8, *pieces)


def cost_kernel(n_col, *refs):
    noise_refs, latent_refs = refs[:4], refs[4 : 4 + 2 * n_col]
    own_ref, other_ref, latents, noise = refs[4 + 2 * n_col :]
    row, col = place()
    x, y = lax.rem(row // 2, 2), row // 4
    own, depth = noise_refs[0].shape
    share = latent_refs[0].shape[0]
    height = 2 * share
    for i in range(4):
        core, far = i % 2, i // 2
        noise[block(2 * core + (x ^ far), own), :] = noise_refs[i][...]
    for far in range(2):
        for d in range(n_col):
            rows = block((col ^ d) * 2 + (y ^ far), share)
            latents[rows, :] = latent_refs[far * n_col + d][...]
    lanes = [slice(i, i + WIDTH) for i in range(0, depth, WIDTH)]
    squares = jnp.zeros((4 * own, WIDTH), jnp.float32)
    for part in lanes:
        values = noise[:, part].astype(jnp.float32)
        squares += values * values
    noise_norm = jnp.sum(squares, axis=1, keepdims=True)
    step = 2 * height
    for first in range(0, n_col * height, step):
        rows = slice(first, first + step)
        cross = lax.dot_general(
            noise[...], latents[rows, :], CONTRACT, preferred_element_type=jnp.float32
        )
        squares = jnp.zeros((step, WIDTH), jnp.float32)
        for part in lanes:
            values = latents[rows, part].astype(jnp.float32)
            squares += values * values
        norm = jnp.sum(squares, axis=1, keepdims=True)
        norm = jnp.broadcast_to(norm, (step, WIDTH)).T[0:1, :]
        cost = (noise_norm + norm - 2.0 * cross) * (TO_LOG2 / LATENT)
        for i in range(2):
            own_ref[i, :, rows] = cost[i * own : (i + 1) * own]
            other_ref[i, :, rows] = cost[(2 + i) * own : (3 + i) * own]


def partial_cost(noise_parts, latents):
    n_col = len(latents) // 2
    own, depth = noise_parts[0].shape
    width = 2 * n_col * latents[0].shape[0]
    return kernel_call(
        functools.partial(cost_kernel, n_col),
        [((2, own, width), jnp.float32)] * 2 + [((width, depth), jnp.bfloat16)],
        [pltpu.VMEM((4 * own, depth), jnp.bfloat16)],
        24,
        *noise_parts,
        *latents,
        flops=8 * own * width * depth,
    )


def core_sum_kernel(n_col, own_ref, other_ref, *outs):
    _, col = place()
    share = own_ref.shape[1] // n_col
    for d in range(n_col):
        rows = block(col ^ d, share)
        outs[d][...] = own_ref[:, rows, :] + other_ref[:, rows, :]


def core_sum(own, other, n_col):
    shape = (2, own.shape[1] // n_col, own.shape[2])
    return kernel_call(
        functools.partial(core_sum_kernel, n_col), [(shape, own.dtype)] * n_col, [], 8, own, other
    )


def sinkhorn_kernel(n_col, n_half, *refs):
    n_cost = 8 * n_half
    cost_refs, latent_refs, refs = refs[:n_cost], refs[n_cost : n_cost + 2], refs[n_cost + 2 :]
    target_refs, refs = refs[:n_col], refs[n_col:]
    noise_pot_ref, data_pot_ref, cost, own_cost, pots, weights = refs
    row, col = place()
    x = lax.rem(row // 2, 2)
    tall, height, wide = cost.shape
    log_noise = math.log2(tall * height)
    log_data = math.log2(wide)
    blocks = range(wide // WIDTH)
    half_wide = wide // 2
    pieces, share = cost_refs[0].shape[0], cost_refs[0].shape[2]
    for i, ref in enumerate(cost_refs):
        chip, core, half = i // (2 * n_half), i // n_half % 2, i % n_half
        rows = slice(half * pieces * 2 * share, (half + 1) * pieces * 2 * share)
        part = slice((chip % 2) * half_wide, (chip % 2 + 1) * half_wide)
        cost[(chip // 2) * 2 + core, rows, part] = ref[...].reshape(pieces * 2 * share, half_wide)

    def lanes(b):
        return pl.ds(b * WIDTH, WIDTH)

    def row_update(tile, g):
        peak = functools.reduce(jnp.maximum, [g[b] - tile(b) for b in blocks])
        peak = jnp.max(peak, axis=1, keepdims=True)
        total = functools.reduce(jnp.add, [jnp.exp2(g[b] - tile(b) - peak) for b in blocks])
        total = jnp.sum(total, axis=1, keepdims=True)
        return -(log_noise + peak + jnp.log2(total))

    def both_updates(chunk, carry, g):
        high, summed = carry
        f = row_update(lambda b: cost[chunk, :, lanes(b)], g)
        new_high, new_summed = [], []
        for b in blocks:
            scores = f - cost[chunk, :, lanes(b)]
            peak = jnp.max(scores, axis=0, keepdims=True)
            total = jnp.sum(jnp.exp2(scores - peak), axis=0, keepdims=True)
            top = jnp.maximum(high[b], peak)
            new_high.append(top)
            new_summed.append(summed[b] * jnp.exp2(high[b] - top) + total * jnp.exp2(peak - top))
        return tuple(new_high), tuple(new_summed)

    def iteration(_, g):
        first = (
            tuple(jnp.full((1, WIDTH), -jnp.inf, jnp.float32) for b in blocks),
            tuple(jnp.zeros((1, WIDTH), jnp.float32) for b in blocks),
        )
        high, summed = lax.fori_loop(0, tall, lambda i, carry: both_updates(i, carry, g), first)
        return tuple(-(log_data + high[b] + jnp.log2(summed[b])) for b in blocks)

    g = tuple(jnp.zeros((1, WIDTH), jnp.float32) for b in blocks)
    g = lax.fori_loop(0, ITERS, iteration, g)
    for b in blocks:
        pots[:, lanes(b)] = g[b] * (1.0 / TO_LOG2)
    width = half_wide // n_col
    for far in range(2):
        data_pot_ref[pl.ds(x ^ far, 1), :] = pots[:, block(far * n_col + col, width)]

    for core in range(2):
        for d in range(n_col):
            rows = slice((core * n_col + d) * share, (core * n_col + d + 1) * share)
            own_cost[rows, :] = cost[core, block(2 * d + x, share), :]
    f = row_update(lambda b: own_cost[:, lanes(b)], g)
    for b in blocks:
        scores = (f + g[b] - own_cost[:, lanes(b)]) + log_noise
        weights[:, lanes(b)] = jnp.exp2(scores).astype(jnp.bfloat16)
    own = share * n_col
    f = jnp.broadcast_to(f[:own], (own, WIDTH)).T[0:1, :] * (1.0 / TO_LOG2)
    for d in range(n_col):
        noise_pot_ref[pl.ds(col ^ d, 1), :] = f[:, d * share : (d + 1) * share]

    depth = latent_refs[0].shape[1]
    step = min(depth, 512)
    for i in range(0, depth, step):
        part = slice(i, i + step)
        product = jnp.dot(
            weights[:, :half_wide], latent_refs[0][:, part], preferred_element_type=jnp.float32
        )
        product += jnp.dot(
            weights[:, half_wide:], latent_refs[1][:, part], preferred_element_type=jnp.float32
        )
        product = product.astype(jnp.bfloat16)
        for d in range(n_col):
            target_refs[d][0, :, part] = product[d * share : (d + 1) * share]
            target_refs[d][1, :, part] = product[own + d * share : own + (d + 1) * share]


def sinkhorn(tiles, latents, n_col):
    n_half = len(tiles[0]) // 2
    pieces, _, share, half_wide = tiles[0][0].shape
    height = n_half * pieces * 2 * share
    wide = 2 * half_wide
    own = n_col * share
    return kernel_call(
        functools.partial(sinkhorn_kernel, n_col, n_half),
        [((2, share, latents[0].shape[1]), jnp.bfloat16)] * n_col
        + [((n_col, share), jnp.float32), ((2, half_wide // n_col), jnp.float32)],
        [
            pltpu.VMEM((4, height, wide), jnp.float32),
            pltpu.VMEM((2 * own, wide), jnp.float32),
            pltpu.VMEM((1, wide), jnp.float32),
            pltpu.VMEM((2 * own, wide), jnp.bfloat16),
        ],
        32,
        *[tile for group in tiles for tile in group],
        *latents,
        flops=240 * height * wide,
    )


def join_kernel(n_col, *refs):
    *pieces, out_ref = refs
    row, col = place()
    depth = pieces[0].shape[2]
    for d in range(n_col):
        for other in range(2):
            lanes = block(2 * (col ^ d) + (lax.rem(row, 2) ^ other), depth)
            out_ref[:, lanes] = pieces[other * n_col + d][other]


def join(pieces, n_col):
    _, share, depth = pieces[0].shape
    shape = (share, depth * len(pieces))
    (out,) = kernel_call(
        functools.partial(join_kernel, n_col), [(shape, pieces[0].dtype)], [], 12, *pieces
    )
    return out


def per_device_local(noise, data):
    n_row, n_col = lax.axis_size("row"), lax.axis_size("col")
    n_chip = n_row // 2
    own, own_data = noise.shape[0], data.shape[0]
    *dealt, own_half, other_half = deal(data, noise, n_chip)
    spread = regroup([chip_swap(piece, k) for k, piece in enumerate(dealt)])
    latents = col_exchange(spread)
    latents = latents + [swap_y(piece) for piece in latents]
    halves = [own_half, swap_core(other_half)]
    halves = halves + [swap_x(half) for half in halves]
    own_part, other_part, near = partial_cost(halves, latents)
    far = swap_x(near)
    parts = col_exchange(core_sum(own_part, swap_core(other_part), n_col))
    tile = functools.reduce(jnp.add, parts)
    rows = [tile] + [swap(tile, "col", d) for d in range(1, n_col)]
    halves = [jnp.stack(rows[: n_col // 2]), jnp.stack(rows[n_col // 2 :])]
    tiles = [group + [swap_core(half) for half in group] for group in chip_gather(halves)]
    *products, noise_pot, data_pot = sinkhorn(tiles, [near, far], n_col)
    products = col_exchange(products)
    targets = join(products + [swap_core(piece) for piece in products], n_col)
    data_pot = data_pot.reshape((2, 2, own_data // 4)).transpose((1, 0, 2))
    return (targets, noise_pot.reshape((own,)), data_pot.reshape((own_data,)))


def per_device(noise, data):
    n_row, n_col = lax.axis_size("row"), lax.axis_size("col")
    whole = 4 * noise.shape[0] * n_row * data.shape[0] * n_col
    if whole <= LOCAL_COST_BYTES and n_row == 8 and n_col == 4:
        return per_device_local(noise, data)
    return per_device_tiled(noise, data)


def solution(mesh):
    placed = (P("row", "col"), P("col", "row"))
    return jax.shard_map(
        per_device,
        mesh=mesh,
        in_specs=placed,
        out_specs=(P(("row", "col"), None), P("row"), P("col")),
        check_vma=False,
    )
```

```python
import functools
import math

import jax
import jax.numpy as jnp
from jax import lax
from jax.experimental import pallas as pl
from jax.experimental.pallas import tpu as pltpu
from jax.sharding import PartitionSpec as P

LATENT = 16384
ITERS = 3
EPSILON = 0.64 / math.sqrt(LATENT)
LOG2E = math.log2(math.e)
TO_LOG2 = LOG2E / EPSILON
CONTRACT = (((1,), (1,)), ((), ()))
LOCAL_COST_BYTES = 8 * 2**20


def noise_update(cost_tile, data_pot, epsilon, log_count):
    scores = (data_pot[None, :] - cost_tile) / epsilon
    local_peak = jnp.max(scores, axis=1)
    highest = lax.pmax(local_peak, "col")
    summed = lax.psum(jnp.sum(jnp.exp(scores - highest[:, None]), axis=1), "col")
    return -epsilon * (log_count + highest + jnp.log(summed))


def data_update(cost_tile, noise_pot, epsilon, log_count):
    scores = (noise_pot[:, None] - cost_tile) / epsilon
    local_peak = jnp.max(scores, axis=0)
    highest = lax.pmax(local_peak, "row")
    summed = lax.psum(jnp.sum(jnp.exp(scores - highest[None, :]), axis=0), "row")
    return -epsilon * (log_count + highest + jnp.log(summed))


def per_device_tiled(noise, data):
    epsilon = EPSILON
    noise_full = lax.all_gather(noise, "col", axis=1, tiled=True)
    noise_norm = jnp.sum(jnp.square(noise_full.astype(jnp.float32)), axis=1) / LATENT
    noise_rows = noise.shape[0]
    data_rows = data.shape[0]
    data_full = lax.all_gather(data, "row", axis=1, tiled=True)
    data_norm = jnp.sum(jnp.square(data_full.astype(jnp.float32)), axis=1) / LATENT
    cross = lax.dot_general(noise_full, data_full, CONTRACT, preferred_element_type=jnp.float32)
    cost_tile = noise_norm[:, None] + data_norm[None, :] - 2.0 / LATENT * cross
    log_noise = math.log(noise_rows * lax.axis_size("row"))
    log_data = math.log(data_rows * lax.axis_size("col"))
    data_pot = jnp.zeros((data_rows,), jnp.float32)
    for step in range(ITERS):
        noise_pot = noise_update(cost_tile, data_pot, epsilon, log_noise)
        data_pot = data_update(cost_tile, noise_pot, epsilon, log_data)
    noise_pot = noise_update(cost_tile, data_pot, epsilon, log_noise)
    weights = jnp.exp(
        (noise_pot[:, None] + data_pot[None, :] - cost_tile) / epsilon + log_noise
    ).astype(jnp.bfloat16)
    targets = lax.psum_scatter(
        jnp.dot(weights, data_full, preferred_element_type=jnp.float32).astype(jnp.bfloat16),
        "col",
        scatter_dimension=0,
        tiled=True,
    )
    return (targets, noise_pot, data_pot)


VMEM = pl.BlockSpec(memory_space=pltpu.VMEM)
WIDTH = 128


def place():
    return lax.axis_index("row"), lax.axis_index("col")


def swap(array, axis, step):
    count = lax.axis_size(axis)
    return lax.ppermute(array, axis, [(i, i ^ step) for i in range(count)])


def swap_core(array):
    return swap(array, "row", 1)


def swap_x(array):
    return swap(array, "row", 2)


def swap_y(array):
    return swap(array, "row", 4)


def after(array, *others):
    return lax.optimization_barrier((array,) + others)[0]


def col_exchange(pieces):
    return [pieces[0]] + [swap(piece, "col", d) for d, piece in enumerate(pieces) if d]


def chip_gather(pieces):
    along_x, along_y, across = [], [], []
    for i, piece in enumerate(pieces):
        along_x.append(swap_x(piece))
        along_y.append(swap_y(piece))
        across.append(swap_x(along_y[i]) if i % 2 else swap_y(along_x[i]))
    return [pieces, along_x, along_y, across]


def block(index, size):
    return pl.ds(pl.multiple_of(index * size, size), size)


def kernel_call(kernel, outs, scratch, vmem, *operands, flops=0):
    moved = sum(a.size * a.dtype.itemsize for a in operands)
    return pl.pallas_call(
        kernel,
        in_specs=[VMEM] * len(operands),
        out_specs=[VMEM] * len(outs),
        out_shape=[jax.ShapeDtypeStruct(shape, dtype) for shape, dtype in outs],
        scratch_shapes=scratch,
        compiler_params=pltpu.CompilerParams(vmem_limit_bytes=vmem * 2**20),
        cost_estimate=pl.CostEstimate(flops=flops, bytes_accessed=moved, transcendentals=0),
    )(*operands)


def deal_kernel(n_col, data_ref, noise_ref, *outs):
    row, col = place()
    core = lax.rem(row, 2)
    part = data_ref.shape[1] // n_col
    for d in range(n_col):
        outs[d][...] = data_ref[:, block(col ^ d, part)]
    half = noise_ref.shape[1] // 2
    outs[n_col][...] = noise_ref[:, block(core, half)]
    outs[n_col + 1][...] = noise_ref[:, block(1 - core, half)]


def deal(data, noise, n_col):
    piece = (data.shape[0], data.shape[1] // n_col)
    half = (noise.shape[0], noise.shape[1] // 2)
    return kernel_call(
        functools.partial(deal_kernel, n_col),
        [(piece, data.dtype)] * n_col + [(half, noise.dtype)] * 2,
        [],
        12,
        data,
        noise,
    )


def deal_noise_kernel(n_col, own_ref, other_ref, *outs):
    _, col = place()
    part = own_ref.shape[1] // n_col
    for d in range(n_col):
        outs[d][0] = own_ref[:, block(col ^ d, part)]
        outs[d][1] = other_ref[:, block(col ^ d, part)]


def deal_noise(own, other, n_col):
    shape = (2, own.shape[0], own.shape[1] // n_col)
    return kernel_call(
        functools.partial(deal_noise_kernel, n_col), [(shape, own.dtype)] * n_col, [], 8, own, other
    )


def cost_kernel(n_col, n_chip, *refs):
    noise_refs, latent_refs = refs[:n_col], refs[n_col : n_col + n_chip * n_col]
    own_ref, other_ref, noise_all = refs[n_col + n_chip * n_col :]
    row, col = place()
    _, own, part = noise_refs[0].shape
    height = latent_refs[0].shape[0]
    for d in range(n_col):
        noise_all[(row // 2) ^ col ^ d] = noise_refs[d][...].reshape(2 * own, part)
    noise_norm = jnp.zeros((2 * own, 1), jnp.float32)
    for k in range(n_chip):
        values = noise_all[k].astype(jnp.float32)
        noise_norm += jnp.sum(values * values, axis=1, keepdims=True)
    for d in range(n_col):
        cross = jnp.zeros((2 * own, height), jnp.float32)
        squares = jnp.zeros((height, part), jnp.float32)
        for k in range(n_chip):
            rows = latent_refs[k * n_col + d][...]
            cross += lax.dot_general(noise_all[k], rows, CONTRACT, preferred_element_type=jnp.float32)
            values = rows.astype(jnp.float32)
            squares += values * values
        norm = jnp.sum(squares, axis=1, keepdims=True)
        norm = jnp.broadcast_to(norm, (height, WIDTH)).T[0:1, :]
        cost = (noise_norm + norm - 2.0 * cross) * (TO_LOG2 / LATENT)
        lanes = block(col ^ d, height)
        own_ref[:, lanes] = cost[:own]
        other_ref[:, lanes] = cost[own:]


def partial_cost(noise_pieces, latents):
    n_chip, n_col = len(latents), len(noise_pieces)
    _, own, part = noise_pieces[0].shape
    width = n_col * latents[0][0].shape[0]
    return kernel_call(
        functools.partial(cost_kernel, n_col, n_chip),
        [((own, width), jnp.float32)] * 2,
        [pltpu.VMEM((n_chip, 2 * own, part), jnp.bfloat16)],
        24,
        *noise_pieces,
        *[piece for group in latents for piece in group],
        flops=4 * own * width * n_chip * part,
    )


def core_sum_kernel(n_col, own_ref, other_ref, *outs):
    _, col = place()
    share = own_ref.shape[0] // n_col
    for d in range(n_col):
        rows = block(col ^ d, share)
        outs[d][...] = own_ref[rows, :] + other_ref[rows, :]


def core_sum(own, other, n_col):
    shape = (own.shape[0] // n_col, own.shape[1])
    return kernel_call(
        functools.partial(core_sum_kernel, n_col), [(shape, own.dtype)] * n_col, [], 8, own, other
    )


def sinkhorn_kernel(n_col, n_chip, n_half, *refs):
    n_cost = 2 * n_chip * n_half
    cost_refs, latent_refs = refs[:n_cost], refs[n_cost : n_cost + n_chip * n_col]
    refs = refs[n_cost + n_chip * n_col :]
    target_refs, refs = refs[:n_col], refs[n_col:]
    noise_pot_ref, data_pot_ref, cost, pots, weights = refs
    _, col = place()
    tall, height, wide = cost.shape
    log_noise = math.log2(tall * height)
    log_data = math.log2(wide)
    blocks = range(wide // WIDTH)
    rows_of_one = height // (2 * n_half)
    for i, ref in enumerate(cost_refs):
        k, place_in = divmod(i, 2 * n_half)
        cost[k, place_in * rows_of_one : (place_in + 1) * rows_of_one, :] = ref[...]

    def lanes(b):
        return pl.ds(b * WIDTH, WIDTH)

    def row_update(chunk, g):
        peak = functools.reduce(jnp.maximum, [g[b] - cost[chunk, :, lanes(b)] for b in blocks])
        peak = jnp.max(peak, axis=1, keepdims=True)
        total = functools.reduce(
            jnp.add, [jnp.exp2(g[b] - cost[chunk, :, lanes(b)] - peak) for b in blocks]
        )
        total = jnp.sum(total, axis=1, keepdims=True)
        return -(log_noise + peak + jnp.log2(total))

    def both_updates(chunk, carry, g):
        high, summed = carry
        f = row_update(chunk, g)
        new_high, new_summed = [], []
        for b in blocks:
            scores = f - cost[chunk, :, lanes(b)]
            peak = jnp.max(scores, axis=0, keepdims=True)
            total = jnp.sum(jnp.exp2(scores - peak), axis=0, keepdims=True)
            top = jnp.maximum(high[b], peak)
            new_high.append(top)
            new_summed.append(summed[b] * jnp.exp2(high[b] - top) + total * jnp.exp2(peak - top))
        return tuple(new_high), tuple(new_summed)

    def iteration(_, g):
        first = (
            tuple(jnp.full((1, WIDTH), -jnp.inf, jnp.float32) for b in blocks),
            tuple(jnp.zeros((1, WIDTH), jnp.float32) for b in blocks),
        )
        high, summed = lax.fori_loop(0, tall, lambda i, carry: both_updates(i, carry, g), first)
        return tuple(-(log_data + high[b] + jnp.log2(summed[b])) for b in blocks)

    g = tuple(jnp.zeros((1, WIDTH), jnp.float32) for b in blocks)
    g = lax.fori_loop(0, ITERS, iteration, g)
    for b in blocks:
        pots[:, lanes(b)] = g[b] * (1.0 / TO_LOG2)
    data_pot_ref[...] = pots[:, block(col, wide // n_col)]

    f = row_update(0, g)
    for b in blocks:
        scores = (f + g[b] - cost[0, :, lanes(b)]) + log_noise
        weights[:, lanes(b)] = jnp.exp2(scores).astype(jnp.bfloat16)
    own = height // 2
    share = own // n_col
    f = jnp.broadcast_to(f[:own], (own, WIDTH)).T[0:1, :] * (1.0 / TO_LOG2)
    for d in range(n_col):
        noise_pot_ref[pl.ds(col ^ d, 1), :] = f[:, d * share : (d + 1) * share]

    rows_of_one, part = latent_refs[0].shape
    for k in range(n_chip):
        product = jnp.zeros((height, part), jnp.float32)
        for d in range(n_col):
            product += jnp.dot(
                weights[:, block(col ^ d, rows_of_one)],
                latent_refs[k * n_col + d][...],
                preferred_element_type=jnp.float32,
            )
        product = product.astype(jnp.bfloat16)
        for d in range(n_col):
            target_refs[d][0, k] = product[d * share : (d + 1) * share]
            target_refs[d][1, k] = product[own + d * share : own + (d + 1) * share]


def sinkhorn(tiles, latents, n_col):
    n_chip, n_half = len(latents), len(tiles[0]) // 2
    share_rows, width = tiles[0][0].shape
    height = 2 * n_half * share_rows
    part = latents[0][0].shape[1]
    share = height // (2 * n_col)
    size = n_chip * height * width
    piece = ((2, n_chip, share, part), jnp.bfloat16)
    return kernel_call(
        functools.partial(sinkhorn_kernel, n_col, n_chip, n_half),
        [piece] * n_col
        + [((n_col, share), jnp.float32), ((1, width // n_col), jnp.float32)],
        [
            pltpu.VMEM((n_chip, height, width), jnp.float32),
            pltpu.VMEM((1, width), jnp.float32),
            pltpu.VMEM((height, width), jnp.bfloat16),
        ],
        32,
        *[tile for group in tiles for tile in group],
        *[piece for group in latents for piece in group],
        flops=60 * size,
    )


def join_kernel(n_col, *refs):
    *pieces, out_ref = refs
    row, col = place()
    _, n_chip, _, part = pieces[0].shape
    for i, piece in enumerate(pieces):
        other, d = divmod(i, n_col)
        for k in range(n_chip):
            out_ref[:, block((row ^ other ^ (2 * k)) * n_col + (col ^ d), part)] = piece[other, k]


def join(pieces, n_col):
    _, n_chip, share, part = pieces[0].shape
    shape = (share, n_chip * part * len(pieces))
    (out,) = kernel_call(
        functools.partial(join_kernel, n_col), [(shape, pieces[0].dtype)], [], 12, *pieces
    )
    return out


def per_device_local(noise, data):
    n_col = lax.axis_size("col")
    own, own_data = noise.shape[0], data.shape[0]
    *dealt, own_half, other_half = deal(data, noise, n_col)
    swapped = swap_core(other_half)
    data_0 = dealt[0]
    data_1, data_2, data_3 = [swap(dealt[d], "col", d) for d in (1, 2, 3)]
    x_0, y_0 = swap_x(data_0), swap_y(data_0)
    across_0 = swap_y(x_0)
    x_1, y_1 = swap_x(data_1), swap_y(data_1)
    across_1 = swap_x(y_1)
    swapped = after(swapped, across_0, x_1, y_1, data_2)
    noise_pieces = list(deal_noise(own_half, swapped, n_col))
    noise_pieces[1] = swap(noise_pieces[1], "col", 1)
    noise_pieces[2] = swap(noise_pieces[2], "col", 2)
    x_2, y_2 = swap_x(data_2), swap_y(data_2)
    across_2 = swap_y(x_2)
    x_3, y_3 = swap_x(data_3), swap_y(data_3)
    noise_pieces[3] = swap(after(noise_pieces[3], noise_pieces[1], x_2, y_2), "col", 3)
    across_3 = swap_x(y_3)
    latents = [
        [data_0, data_1, data_2, data_3],
        [x_0, x_1, x_2, x_3],
        [y_0, y_1, y_2, y_3],
        [across_0, across_1, across_2, across_3],
    ]
    own_part, other_part = partial_cost(noise_pieces, latents)
    parts = col_exchange(core_sum(own_part, swap_core(other_part), n_col))
    tile = functools.reduce(jnp.add, parts)
    rows = [tile] + [swap(tile, "col", d) for d in range(1, n_col)]
    halves = [jnp.concatenate(rows[: n_col // 2]), jnp.concatenate(rows[n_col // 2 :])]
    tiles = [group + [swap_core(half) for half in group] for group in chip_gather(halves)]
    *products, noise_pot, data_pot = sinkhorn(tiles, latents, n_col)
    products = col_exchange(products)
    targets = join(products + [swap_core(piece) for piece in products], n_col)
    return (targets, noise_pot.reshape((own,)), data_pot.reshape((own_data,)))


def per_device(noise, data):
    n_row, n_col = lax.axis_size("row"), lax.axis_size("col")
    whole = 4 * noise.shape[0] * n_row * data.shape[0] * n_col
    if whole <= LOCAL_COST_BYTES and n_row == 8 and n_col == 4:
        return per_device_local(noise, data)
    return per_device_tiled(noise, data)


def solution(mesh):
    placed = (P("row", "col"), P("col", "row"))
    return jax.shard_map(
        per_device,
        mesh=mesh,
        in_specs=placed,
        out_specs=(P(("row", "col"), None), P("row"), P("col")),
        check_vma=False,
    )
```

```python
import functools
import math

import jax
import jax.numpy as jnp
from jax import lax
from jax.experimental import pallas as pl
from jax.experimental.pallas import tpu as pltpu
from jax.sharding import PartitionSpec as P

LATENT = 16384
ITERS = 3
EPSILON = 0.64 / math.sqrt(LATENT)
LOG2E = math.log2(math.e)
TO_LOG2 = LOG2E / EPSILON
CONTRACT = (((1,), (1,)), ((), ()))
LOCAL_COST_BYTES = 8 * 2**20


def noise_update(cost_tile, data_pot, epsilon, log_count):
    scores = (data_pot[None, :] - cost_tile) / epsilon
    local_peak = jnp.max(scores, axis=1)
    highest = lax.pmax(local_peak, "col")
    summed = lax.psum(jnp.sum(jnp.exp(scores - highest[:, None]), axis=1), "col")
    return -epsilon * (log_count + highest + jnp.log(summed))


def data_update(cost_tile, noise_pot, epsilon, log_count):
    scores = (noise_pot[:, None] - cost_tile) / epsilon
    local_peak = jnp.max(scores, axis=0)
    highest = lax.pmax(local_peak, "row")
    summed = lax.psum(jnp.sum(jnp.exp(scores - highest[None, :]), axis=0), "row")
    return -epsilon * (log_count + highest + jnp.log(summed))


def per_device_tiled(noise, data):
    epsilon = EPSILON
    noise_full = lax.all_gather(noise, "col", axis=1, tiled=True)
    noise_norm = jnp.sum(jnp.square(noise_full.astype(jnp.float32)), axis=1) / LATENT
    noise_rows = noise.shape[0]
    data_rows = data.shape[0]
    data_full = lax.all_gather(data, "row", axis=1, tiled=True)
    data_norm = jnp.sum(jnp.square(data_full.astype(jnp.float32)), axis=1) / LATENT
    cross = lax.dot_general(noise_full, data_full, CONTRACT, preferred_element_type=jnp.float32)
    cost_tile = noise_norm[:, None] + data_norm[None, :] - 2.0 / LATENT * cross
    log_noise = math.log(noise_rows * lax.axis_size("row"))
    log_data = math.log(data_rows * lax.axis_size("col"))
    data_pot = jnp.zeros((data_rows,), jnp.float32)
    for step in range(ITERS):
        noise_pot = noise_update(cost_tile, data_pot, epsilon, log_noise)
        data_pot = data_update(cost_tile, noise_pot, epsilon, log_data)
    noise_pot = noise_update(cost_tile, data_pot, epsilon, log_noise)
    weights = jnp.exp(
        (noise_pot[:, None] + data_pot[None, :] - cost_tile) / epsilon + log_noise
    ).astype(jnp.bfloat16)
    targets = lax.psum_scatter(
        jnp.dot(weights, data_full, preferred_element_type=jnp.float32).astype(jnp.bfloat16),
        "col",
        scatter_dimension=0,
        tiled=True,
    )
    return (targets, noise_pot, data_pot)


VMEM = pl.BlockSpec(memory_space=pltpu.VMEM)
WIDTH = 128


def place():
    return lax.axis_index("row"), lax.axis_index("col")


def swap(array, axis, step):
    count = lax.axis_size(axis)
    return lax.ppermute(array, axis, [(i, i ^ step) for i in range(count)])


def swap_core(array):
    return swap(array, "row", 1)


def swap_x(array):
    return swap(array, "row", 2)


def swap_y(array):
    return swap(array, "row", 4)


def after(array, *others):
    return lax.optimization_barrier((array,) + others)[0]


def col_exchange(pieces):
    return [pieces[0]] + [swap(piece, "col", d) for d, piece in enumerate(pieces) if d]


def chip_gather(pieces):
    along_x, along_y, across = [], [], []
    for i, piece in enumerate(pieces):
        along_x.append(swap_x(piece))
        along_y.append(swap_y(piece))
        across.append(swap_x(along_y[i]) if i % 2 else swap_y(along_x[i]))
    return [pieces, along_x, along_y, across]


def block(index, size):
    return pl.ds(pl.multiple_of(index * size, size), size)


def kernel_call(kernel, outs, scratch, vmem, *operands, flops=0):
    moved = sum(a.size * a.dtype.itemsize for a in operands)
    return pl.pallas_call(
        kernel,
        in_specs=[VMEM] * len(operands),
        out_specs=[VMEM] * len(outs),
        out_shape=[jax.ShapeDtypeStruct(shape, dtype) for shape, dtype in outs],
        scratch_shapes=scratch,
        compiler_params=pltpu.CompilerParams(vmem_limit_bytes=vmem * 2**20),
        cost_estimate=pl.CostEstimate(flops=flops, bytes_accessed=moved, transcendentals=0),
    )(*operands)


def chip_swap(piece, k):
    return swap(piece, "row", 2 * k) if k else piece


def deal_kernel(n_chip, data_ref, noise_ref, *outs):
    row, _ = place()
    core, chip = lax.rem(row, 2), row // 2
    share = data_ref.shape[0] // n_chip
    for k in range(n_chip):
        outs[k][...] = data_ref[block(chip ^ k, share), :]
    half = noise_ref.shape[1] // 2
    outs[n_chip][...] = noise_ref[:, block(core, half)]
    outs[n_chip + 1][...] = noise_ref[:, block(1 - core, half)]


def deal(data, noise, n_chip):
    piece = (data.shape[0] // n_chip, data.shape[1])
    half = (noise.shape[0], noise.shape[1] // 2)
    return kernel_call(
        functools.partial(deal_kernel, n_chip),
        [(piece, data.dtype)] * n_chip + [(half, noise.dtype)] * 2,
        [],
        12,
        data,
        noise,
    )


def regroup_kernel(n_col, *refs):
    row, col = place()
    pieces, outs = refs[:n_col], refs[n_col:]
    for d in range(n_col):
        for k in range(n_col):

            @pl.when((row // 2) ^ col ^ d == k)
            def _():
                outs[d][...] = pieces[k][...]


def regroup(pieces):
    n_col = len(pieces)
    out = (pieces[0].shape, pieces[0].dtype)
    return kernel_call(functools.partial(regroup_kernel, n_col), [out] * n_col, [], 8, *pieces)


def cost_kernel(n_col, *refs):
    noise_refs, latent_refs, refs = refs[:4], refs[4 : 4 + 2 * n_col], refs[4 + 2 * n_col :]
    own_ref, other_ref, *half_refs, latents, noise = refs
    row, col = place()
    x, y = lax.rem(row // 2, 2), row // 4
    own, depth = noise_refs[0].shape
    share = latent_refs[0].shape[0]
    quarter = n_col * share
    for i in range(4):
        core, far = i % 2, i // 2
        noise[block(2 * core + (x ^ far), own), :] = noise_refs[i][...]
    for far in range(2):
        for d in range(n_col):
            rows = block((y ^ far) * n_col + (col ^ d), share)
            latents[rows, :] = latent_refs[far * n_col + d][...]
    for far in range(2):
        for i in range(2):
            half_refs[2 * far + i][...] = latents[block(2 * (y ^ far) + i, quarter // 2), :]
    lanes = [slice(i, i + WIDTH) for i in range(0, depth, WIDTH)]
    squares = jnp.zeros((4 * own, WIDTH), jnp.float32)
    for part in lanes:
        values = noise[:, part].astype(jnp.float32)
        squares += values * values
    noise_norm = jnp.sum(squares, axis=1, keepdims=True)
    for first in range(0, 2 * quarter, quarter):
        rows = slice(first, first + quarter)
        cross = lax.dot_general(
            noise[...], latents[rows, :], CONTRACT, preferred_element_type=jnp.float32
        )
        squares = jnp.zeros((quarter, WIDTH), jnp.float32)
        for part in lanes:
            values = latents[rows, part].astype(jnp.float32)
            squares += values * values
        norm = jnp.sum(squares, axis=1, keepdims=True)
        norm = jnp.broadcast_to(norm, (quarter, WIDTH)).T[0:1, :]
        cost = (noise_norm + norm - 2.0 * cross) * (TO_LOG2 / LATENT)
        for i in range(2):
            own_ref[i, :, rows] = cost[i * own : (i + 1) * own]
            other_ref[i, :, rows] = cost[(2 + i) * own : (3 + i) * own]


def partial_cost(noise_parts, latents):
    n_col = len(latents) // 2
    own, depth = noise_parts[0].shape
    quarter = n_col * latents[0].shape[0]
    return kernel_call(
        functools.partial(cost_kernel, n_col),
        [((2, own, 2 * quarter), jnp.float32)] * 2 + [((quarter // 2, depth), jnp.bfloat16)] * 4,
        [pltpu.VMEM((2 * quarter, depth), jnp.bfloat16), pltpu.VMEM((4 * own, depth), jnp.bfloat16)],
        24,
        *noise_parts,
        *latents,
        flops=16 * own * quarter * depth,
    )


def core_sum_kernel(n_col, own_ref, other_ref, *outs):
    _, col = place()
    share = own_ref.shape[1] // n_col
    for d in range(n_col):
        rows = block(col ^ d, share)
        outs[d][...] = own_ref[:, rows, :] + other_ref[:, rows, :]


def core_sum(own, other, n_col):
    shape = (2, own.shape[1] // n_col, own.shape[2])
    return kernel_call(
        functools.partial(core_sum_kernel, n_col), [(shape, own.dtype)] * n_col, [], 8, own, other
    )


def sinkhorn_kernel(n_col, n_half, *refs):
    n_cost = 8 * n_half
    cost_refs, latent_refs, refs = refs[:n_cost], refs[n_cost : n_cost + 8], refs[n_cost + 8 :]
    target_refs, refs = refs[:n_col], refs[n_col:]
    noise_pot_ref, data_pot_ref, cost, own_cost, weights = refs
    row, col = place()
    x, y = lax.rem(row // 2, 2), row // 4
    tall, height, wide = cost.shape
    log_noise = math.log2(tall * height)
    log_data = math.log2(wide)
    blocks = range(wide // WIDTH)
    half_wide = wide // 2
    pieces, share = cost_refs[0].shape[0], cost_refs[0].shape[2]
    for i, ref in enumerate(cost_refs):
        chip, core, half = i // (2 * n_half), i // n_half % 2, i % n_half
        rows = slice(half * pieces * 2 * share, (half + 1) * pieces * 2 * share)
        part = slice((chip % 2) * half_wide, (chip % 2 + 1) * half_wide)
        cost[(chip // 2) * 2 + core, rows, part] = ref[...].reshape(pieces * 2 * share, half_wide)

    def lanes(b):
        return pl.ds(b * WIDTH, WIDTH)

    def row_update(tile, g):
        peak = functools.reduce(jnp.maximum, [g[b] - tile(b) for b in blocks])
        peak = jnp.max(peak, axis=1, keepdims=True)
        total = functools.reduce(jnp.add, [jnp.exp2(g[b] - tile(b) - peak) for b in blocks])
        total = jnp.sum(total, axis=1, keepdims=True)
        return -(log_noise + peak + jnp.log2(total))

    def both_updates(chunk, carry, g):
        high, summed = carry
        f = row_update(lambda b: cost[chunk, :, lanes(b)], g)
        new_high, new_summed = [], []
        for b in blocks:
            scores = f - cost[chunk, :, lanes(b)]
            peak = jnp.max(scores, axis=0, keepdims=True)
            total = jnp.sum(jnp.exp2(scores - peak), axis=0, keepdims=True)
            top = jnp.maximum(high[b], peak)
            new_high.append(top)
            new_summed.append(summed[b] * jnp.exp2(high[b] - top) + total * jnp.exp2(peak - top))
        return tuple(new_high), tuple(new_summed)

    def iteration(_, g):
        first = (
            tuple(jnp.full((1, WIDTH), -jnp.inf, jnp.float32) for b in blocks),
            tuple(jnp.zeros((1, WIDTH), jnp.float32) for b in blocks),
        )
        high, summed = lax.fori_loop(0, tall, lambda i, carry: both_updates(i, carry, g), first)
        return tuple(-(log_data + high[b] + jnp.log2(summed[b])) for b in blocks)

    g = tuple(jnp.zeros((1, WIDTH), jnp.float32) for b in blocks)
    g = lax.fori_loop(0, ITERS, iteration, g)
    for b in blocks:
        far, first = divmod(b * WIDTH, half_wide)
        data_pot_ref[x ^ far, :, first : first + WIDTH] = g[b] * (1.0 / TO_LOG2)

    for core in range(2):
        for d in range(n_col):
            rows = slice((core * n_col + d) * share, (core * n_col + d + 1) * share)
            own_cost[rows, :] = cost[core, block(2 * d + x, share), :]
    f = row_update(lambda b: own_cost[:, lanes(b)], g)
    for b in blocks:
        scores = (f + g[b] - own_cost[:, lanes(b)]) + log_noise
        weights[:, lanes(b)] = jnp.exp2(scores).astype(jnp.bfloat16)
    own = share * n_col
    f = jnp.broadcast_to(f[:own], (own, WIDTH)).T[0:1, :] * (1.0 / TO_LOG2)
    for d in range(n_col):
        noise_pot_ref[pl.ds(col ^ d, 1), :] = f[:, d * share : (d + 1) * share]

    depth = latent_refs[0].shape[1]
    step = min(depth, 512)
    for i in range(0, depth, step):
        part = slice(i, i + step)
        product = jnp.zeros((2 * own, step), jnp.float32)
        for j, ref in enumerate(latent_refs):
            far_x, far_y, half = j // 4, j // 2 % 2, j % 2
            columns = block(4 * far_x + 2 * (y ^ far_y) + half, ref.shape[0])
            product += jnp.dot(weights[:, columns], ref[:, part], preferred_element_type=jnp.float32)
        product = product.astype(jnp.bfloat16)
        for d in range(n_col):
            target_refs[d][0, :, part] = product[d * share : (d + 1) * share]
            target_refs[d][1, :, part] = product[own + d * share : own + (d + 1) * share]


def sinkhorn(tiles, latents, n_col):
    n_half = len(tiles[0]) // 2
    pieces, _, share, half_wide = tiles[0][0].shape
    height = n_half * pieces * 2 * share
    wide = 2 * half_wide
    own = n_col * share
    return kernel_call(
        functools.partial(sinkhorn_kernel, n_col, n_half),
        [((2, share, latents[0].shape[1]), jnp.bfloat16)] * n_col
        + [((n_col, share), jnp.float32), ((2, 1, half_wide), jnp.float32)],
        [
            pltpu.VMEM((4, height, wide), jnp.float32),
            pltpu.VMEM((2 * own, wide), jnp.float32),
            pltpu.VMEM((2 * own, wide), jnp.bfloat16),
        ],
        32,
        *[tile for group in tiles for tile in group],
        *latents,
        flops=240 * height * wide,
    )


def join_kernel(n_col, *refs):
    *pieces, out_ref = refs
    row, col = place()
    depth = pieces[0].shape[2]
    for d in range(n_col):
        for other in range(2):
            lanes = block(2 * (col ^ d) + (lax.rem(row, 2) ^ other), depth)
            out_ref[:, lanes] = pieces[other * n_col + d][other]


def join(pieces, n_col):
    _, share, depth = pieces[0].shape
    shape = (share, depth * len(pieces))
    (out,) = kernel_call(
        functools.partial(join_kernel, n_col), [(shape, pieces[0].dtype)], [], 12, *pieces
    )
    return out


def per_device_local(noise, data):
    n_row, n_col = lax.axis_size("row"), lax.axis_size("col")
    n_chip = n_row // 2
    own, own_data = noise.shape[0], data.shape[0]
    *dealt, own_half, other_half = deal(data, noise, n_chip)
    spread = regroup([chip_swap(piece, k) for k, piece in enumerate(dealt)])
    data_0, data_1, data_2 = spread[0], swap(spread[1], "col", 1), swap(spread[2], "col", 2)
    data_3 = swap(after(spread[3], data_1), "col", 3)
    latents = [data_0, data_1, data_2, data_3]
    latents = latents + [swap_y(piece) for piece in latents]
    halves = [own_half, swap_core(other_half)]
    halves = halves + [swap_x(after(halves[0], spread[0])), swap_x(after(halves[1], data_1))]
    own_part, other_part, *near = partial_cost(halves, latents)
    over_x = [swap_x(near[0]), swap_x(near[1])]
    across = [swap_y(over_x[0]), swap_x(near[3])]
    parts = col_exchange(core_sum(own_part, swap_core(other_part), n_col))
    tile = functools.reduce(jnp.add, parts)
    tile_1, tile_2 = swap(tile, "col", 1), swap(tile, "col", 2)
    halves = [jnp.stack([tile, tile_1]), jnp.stack([tile_2, swap(tile_2, "col", 1)])]
    tiles = [group + [swap_core(half) for half in group] for group in chip_gather(halves)]
    *products, noise_pot, pots = sinkhorn(tiles, list(near) + over_x + across, n_col)
    products = col_exchange(products)
    targets = join(products + [swap_core(piece) for piece in products], n_col)
    pots = pots.reshape((2, 2, n_col, own_data // 4))
    data_pot = lax.dynamic_index_in_dim(pots, lax.axis_index("col"), 2, keepdims=False)
    data_pot = data_pot.transpose((1, 0, 2)).reshape((own_data,))
    return (targets, noise_pot.reshape((own,)), data_pot)


def per_device(noise, data):
    n_row, n_col = lax.axis_size("row"), lax.axis_size("col")
    whole = 4 * noise.shape[0] * n_row * data.shape[0] * n_col
    if whole <= LOCAL_COST_BYTES and n_row == 8 and n_col == 4:
        return per_device_local(noise, data)
    return per_device_tiled(noise, data)


def solution(mesh):
    placed = (P("row", "col"), P("col", "row"))
    return jax.shard_map(
        per_device,
        mesh=mesh,
        in_specs=placed,
        out_specs=(P(("row", "col"), None), P("row"), P("col")),
        check_vma=False,
    )
```

```python
import functools
import math

import jax
import jax.numpy as jnp
from jax import lax
from jax.experimental import pallas as pl
from jax.experimental.pallas import tpu as pltpu
from jax.sharding import PartitionSpec as P

LATENT = 16384
ITERS = 3
EPSILON = 0.64 / math.sqrt(LATENT)
LOG2E = math.log2(math.e)
TO_LOG2 = LOG2E / EPSILON
CONTRACT = (((1,), (1,)), ((), ()))
LOCAL_COST_BYTES = 8 * 2**20


def noise_update(cost_tile, data_pot, epsilon, log_count):
    scores = (data_pot[None, :] - cost_tile) / epsilon
    local_peak = jnp.max(scores, axis=1)
    highest = lax.pmax(local_peak, "col")
    summed = lax.psum(jnp.sum(jnp.exp(scores - highest[:, None]), axis=1), "col")
    return -epsilon * (log_count + highest + jnp.log(summed))


def data_update(cost_tile, noise_pot, epsilon, log_count):
    scores = (noise_pot[:, None] - cost_tile) / epsilon
    local_peak = jnp.max(scores, axis=0)
    highest = lax.pmax(local_peak, "row")
    summed = lax.psum(jnp.sum(jnp.exp(scores - highest[None, :]), axis=0), "row")
    return -epsilon * (log_count + highest + jnp.log(summed))


def per_device_tiled(noise, data):
    epsilon = EPSILON
    noise_full = lax.all_gather(noise, "col", axis=1, tiled=True)
    noise_norm = jnp.sum(jnp.square(noise_full.astype(jnp.float32)), axis=1) / LATENT
    noise_rows = noise.shape[0]
    data_rows = data.shape[0]
    data_full = lax.all_gather(data, "row", axis=1, tiled=True)
    data_norm = jnp.sum(jnp.square(data_full.astype(jnp.float32)), axis=1) / LATENT
    cross = lax.dot_general(noise_full, data_full, CONTRACT, preferred_element_type=jnp.float32)
    cost_tile = noise_norm[:, None] + data_norm[None, :] - 2.0 / LATENT * cross
    log_noise = math.log(noise_rows * lax.axis_size("row"))
    log_data = math.log(data_rows * lax.axis_size("col"))
    data_pot = jnp.zeros((data_rows,), jnp.float32)
    for step in range(ITERS):
        noise_pot = noise_update(cost_tile, data_pot, epsilon, log_noise)
        data_pot = data_update(cost_tile, noise_pot, epsilon, log_data)
    noise_pot = noise_update(cost_tile, data_pot, epsilon, log_noise)
    weights = jnp.exp(
        (noise_pot[:, None] + data_pot[None, :] - cost_tile) / epsilon + log_noise
    ).astype(jnp.bfloat16)
    targets = lax.psum_scatter(
        jnp.dot(weights, data_full, preferred_element_type=jnp.float32).astype(jnp.bfloat16),
        "col",
        scatter_dimension=0,
        tiled=True,
    )
    return (targets, noise_pot, data_pot)


VMEM = pl.BlockSpec(memory_space=pltpu.VMEM)
WIDTH = 128


def place():
    return lax.axis_index("row"), lax.axis_index("col")


def swap(array, axis, step):
    count = lax.axis_size(axis)
    return lax.ppermute(array, axis, [(i, i ^ step) for i in range(count)])


def swap_core(array):
    return swap(array, "row", 1)


def swap_x(array):
    return swap(array, "row", 2)


def swap_y(array):
    return swap(array, "row", 4)


def after(array, *others):
    return lax.optimization_barrier((array,) + others)[0]


def col_exchange(pieces):
    return [pieces[0]] + [swap(piece, "col", d) for d, piece in enumerate(pieces) if d]


def chip_gather(pieces):
    along_x, along_y, across = [], [], []
    for i, piece in enumerate(pieces):
        along_x.append(swap_x(piece))
        along_y.append(swap_y(piece))
        across.append(swap_x(along_y[i]) if i % 2 else swap_y(along_x[i]))
    return [pieces, along_x, along_y, across]


def block(index, size):
    return pl.ds(pl.multiple_of(index * size, size), size)


def kernel_call(kernel, outs, scratch, vmem, *operands, flops=0):
    moved = sum(a.size * a.dtype.itemsize for a in operands)
    return pl.pallas_call(
        kernel,
        in_specs=[VMEM] * len(operands),
        out_specs=[VMEM] * len(outs),
        out_shape=[jax.ShapeDtypeStruct(shape, dtype) for shape, dtype in outs],
        scratch_shapes=scratch,
        compiler_params=pltpu.CompilerParams(vmem_limit_bytes=vmem * 2**20),
        cost_estimate=pl.CostEstimate(flops=flops, bytes_accessed=moved, transcendentals=0),
    )(*operands)


def deal_kernel(n_col, data_ref, *outs):
    _, col = place()
    part = data_ref.shape[1] // n_col
    for d in range(n_col):
        outs[d][...] = data_ref[:, block(col ^ d, part)]


def deal(data, n_col):
    piece = (data.shape[0], data.shape[1] // n_col)
    return kernel_call(functools.partial(deal_kernel, n_col), [(piece, data.dtype)] * n_col, [], 8, data)


def halve_kernel(noise_ref, own_ref, other_ref):
    row, _ = place()
    core = lax.rem(row, 2)
    half = own_ref.shape[1]
    own_ref[...] = noise_ref[:, block(core, half)]
    other_ref[...] = noise_ref[:, block(1 - core, half)]


def halve(noise):
    half = (noise.shape[0], noise.shape[1] // 2)
    return kernel_call(halve_kernel, [(half, noise.dtype)] * 2, [], 8, noise)


def deal_noise_kernel(n_col, own_ref, other_ref, *outs):
    _, col = place()
    part = own_ref.shape[1] // n_col
    for d in range(n_col):
        outs[d][0] = own_ref[:, block(col ^ d, part)]
        outs[d][1] = other_ref[:, block(col ^ d, part)]


def deal_noise(own, other, n_col):
    shape = (2, own.shape[0], own.shape[1] // n_col)
    return kernel_call(
        functools.partial(deal_noise_kernel, n_col), [(shape, own.dtype)] * n_col, [], 8, own, other
    )


def cost_kernel(n_col, n_chip, *refs):
    noise_refs, latent_refs = refs[:n_col], refs[n_col : n_col + n_chip * n_col]
    own_ref, other_ref, noise_all = refs[n_col + n_chip * n_col :]
    row, col = place()
    _, own, part = noise_refs[0].shape
    height = latent_refs[0].shape[0]
    for d in range(n_col):
        noise_all[(row // 2) ^ col ^ d] = noise_refs[d][...].reshape(2 * own, part)
    noise_norm = jnp.zeros((2 * own, 1), jnp.float32)
    for k in range(n_chip):
        values = noise_all[k].astype(jnp.float32)
        noise_norm += jnp.sum(values * values, axis=1, keepdims=True)
    for d in range(n_col):
        cross = jnp.zeros((2 * own, height), jnp.float32)
        squares = jnp.zeros((height, part), jnp.float32)
        for k in range(n_chip):
            rows = latent_refs[k * n_col + d][...]
            cross += lax.dot_general(noise_all[k], rows, CONTRACT, preferred_element_type=jnp.float32)
            values = rows.astype(jnp.float32)
            squares += values * values
        norm = jnp.sum(squares, axis=1, keepdims=True)
        norm = jnp.broadcast_to(norm, (height, WIDTH)).T[0:1, :]
        cost = (noise_norm + norm - 2.0 * cross) * (TO_LOG2 / LATENT)
        lanes = block(col ^ d, height)
        own_ref[:, lanes] = cost[:own]
        other_ref[:, lanes] = cost[own:]


def partial_cost(noise_pieces, latents):
    n_chip, n_col = len(latents), len(noise_pieces)
    _, own, part = noise_pieces[0].shape
    width = n_col * latents[0][0].shape[0]
    return kernel_call(
        functools.partial(cost_kernel, n_col, n_chip),
        [((own, width), jnp.float32)] * 2,
        [pltpu.VMEM((n_chip, 2 * own, part), jnp.bfloat16)],
        24,
        *noise_pieces,
        *[piece for group in latents for piece in group],
        flops=4 * own * width * n_chip * part,
    )


def core_sum_kernel(n_col, own_ref, other_ref, *outs):
    _, col = place()
    share = own_ref.shape[0] // n_col
    for d in range(n_col):
        rows = block(col ^ d, share)
        outs[d][...] = own_ref[rows, :] + other_ref[rows, :]


def core_sum(own, other, n_col):
    shape = (own.shape[0] // n_col, own.shape[1])
    return kernel_call(
        functools.partial(core_sum_kernel, n_col), [(shape, own.dtype)] * n_col, [], 8, own, other
    )


def rows_of(refs, b):
    lanes = slice(b * WIDTH, (b + 1) * WIDTH)
    parts = []
    for ref in refs:
        if len(ref.shape) == 2:
            parts.append(ref[:, lanes])
        else:
            parts += [ref[i, :, lanes] for i in range(ref.shape[0])]
    return jnp.concatenate(parts)


def row_update(refs, g, log_noise):
    blocks = range(len(g))
    peak = functools.reduce(jnp.maximum, [g[b] - rows_of(refs, b) for b in blocks])
    peak = jnp.max(peak, axis=1, keepdims=True)
    total = functools.reduce(jnp.add, [jnp.exp2(g[b] - rows_of(refs, b) - peak) for b in blocks])
    total = jnp.sum(total, axis=1, keepdims=True)
    return -(log_noise + peak + jnp.log2(total))


def data_potentials(stats, wide):
    if not stats:
        return [jnp.zeros((1, WIDTH), jnp.float32)] * (wide // WIDTH)
    own, other = stats
    result = []
    for first in range(0, wide, WIDTH):
        lanes = slice(first, first + WIDTH)
        peak = jnp.maximum(own[0:1, lanes], other[0:1, lanes])
        total = own[1:2, lanes] * jnp.exp2(own[0:1, lanes] - peak)
        total += other[1:2, lanes] * jnp.exp2(other[0:1, lanes] - peak)
        result.append(-(math.log2(wide) + peak + jnp.log2(total)))
    return result


def iteration_kernel(n_groups, log_noise, *refs):
    *refs, out_ref = refs
    wide = out_ref.shape[1]
    chips = [refs[i : i + 3] for i in range(0, 3 * n_groups, 3)]
    g = data_potentials(refs[3 * n_groups :], wide)
    potentials = [row_update(chip, g, log_noise) for chip in chips]
    for b in range(len(g)):
        scores = [f - rows_of(chip, b) for f, chip in zip(potentials, chips)]
        peak = functools.reduce(jnp.maximum, [jnp.max(s, axis=0, keepdims=True) for s in scores])
        total = functools.reduce(jnp.add, [jnp.sum(jnp.exp2(s - peak), axis=0, keepdims=True) for s in scores])
        out_ref[0:1, b * WIDTH : (b + 1) * WIDTH] = peak
        out_ref[1:2, b * WIDTH : (b + 1) * WIDTH] = total


def iteration(tiles, stats, log_noise):
    wide = tiles[0][0].shape[1]
    operands = [piece for group in tiles for piece in group] + list(stats)
    (own,) = kernel_call(
        functools.partial(iteration_kernel, len(tiles), log_noise),
        [((2, wide), jnp.float32)],
        [],
        16,
        *operands,
        flops=16 * sum(piece.size for piece in operands),
    )
    return own, swap_core(own)


def target_kernel(n_col, n_chip, log_noise, *refs):
    tiles, stats, latent_refs = refs[:6], refs[6:8], refs[8 : 8 + n_chip * n_col]
    refs = refs[8 + n_chip * n_col :]
    target_refs, refs = refs[:n_col], refs[n_col:]
    noise_pot_ref, data_pot_ref, pots, weights = refs
    _, col = place()
    height, wide = weights.shape
    g = data_potentials(stats, wide)
    f = row_update(tiles, g, log_noise)
    for b in range(len(g)):
        lanes = slice(b * WIDTH, (b + 1) * WIDTH)
        pots[:, lanes] = g[b] * (1.0 / TO_LOG2)
        scores = (f + g[b] - rows_of(tiles, b)) + log_noise
        weights[:, lanes] = jnp.exp2(scores).astype(jnp.bfloat16)
    data_pot_ref[...] = pots[:, block(col, wide // n_col)]
    own = height // 2
    share = own // n_col
    f = jnp.broadcast_to(f[:own], (own, WIDTH)).T[0:1, :] * (1.0 / TO_LOG2)
    for d in range(n_col):
        noise_pot_ref[pl.ds(col ^ d, 1), :] = f[:, d * share : (d + 1) * share]

    rows_of_one, part = latent_refs[0].shape
    for k in range(n_chip):
        product = jnp.zeros((height, part), jnp.float32)
        for d in range(n_col):
            product += jnp.dot(
                weights[:, block(col ^ d, rows_of_one)],
                latent_refs[k * n_col + d][...],
                preferred_element_type=jnp.float32,
            )
        product = product.astype(jnp.bfloat16)
        for d in range(n_col):
            target_refs[d][0, k] = product[d * share : (d + 1) * share]
            target_refs[d][1, k] = product[own + d * share : own + (d + 1) * share]


def make_targets(own_tiles, other_tiles, stats, latents, n_col, log_noise):
    n_chip = len(latents)
    share, wide = own_tiles[0].shape
    own = n_col * share
    part = latents[0][0].shape[1]
    return kernel_call(
        functools.partial(target_kernel, n_col, n_chip, log_noise),
        [((2, n_chip, share, part), jnp.bfloat16)] * n_col
        + [((n_col, share), jnp.float32), ((1, wide // n_col), jnp.float32)],
        [pltpu.VMEM((1, wide), jnp.float32), pltpu.VMEM((2 * own, wide), jnp.bfloat16)],
        24,
        *own_tiles,
        *other_tiles,
        *stats,
        *[piece for group in latents for piece in group],
        flops=4 * own * wide * n_chip * part,
    )


def join_kernel(n_col, *refs):
    *pieces, out_ref = refs
    row, col = place()
    _, n_chip, _, part = pieces[0].shape
    for i, piece in enumerate(pieces):
        other, d = divmod(i, n_col)
        for k in range(n_chip):
            out_ref[:, block((row ^ other ^ (2 * k)) * n_col + (col ^ d), part)] = piece[other, k]


def join(pieces, n_col):
    _, n_chip, share, part = pieces[0].shape
    shape = (share, n_chip * part * len(pieces))
    (out,) = kernel_call(
        functools.partial(join_kernel, n_col), [(shape, pieces[0].dtype)], [], 12, *pieces
    )
    return out


def per_device_local(noise, data):
    n_col = lax.axis_size("col")
    own, own_data = noise.shape[0], data.shape[0]
    data_0, *dealt = deal(data, n_col)
    own_half, other_half = halve(noise)
    data_1, data_2 = swap(dealt[0], "col", 1), swap(dealt[1], "col", 2)
    x_0, y_0 = swap_x(data_0), swap_y(data_0)
    noise_0, *dealt_noise = deal_noise(own_half, after(swap_core(other_half), x_0, y_0), n_col)
    data_3 = swap(dealt[2], "col", 3)
    across_0 = swap_y(after(x_0, noise_0))
    x_1, y_1 = swap_x(after(data_1, noise_0)), swap_y(after(data_1, noise_0))
    noise_1 = swap(after(dealt_noise[0], data_2), "col", 1)
    across_1 = swap_x(y_1)
    x_2, y_2 = swap_x(after(data_2, x_1)), swap_y(after(data_2, y_1, across_0))
    noise_2 = swap(after(dealt_noise[1], data_2), "col", 2)
    across_2 = swap_y(x_2)
    x_3, y_3 = swap_x(after(data_3, across_1, x_2, noise_1)), swap_y(after(data_3, y_2, noise_1))
    noise_3 = swap(after(dealt_noise[2], data_3, noise_1), "col", 3)
    across_3 = swap_x(y_3)
    noise_pieces = [noise_0, noise_1, noise_2, noise_3]
    latents = [
        [data_0, data_1, data_2, data_3],
        [x_0, x_1, x_2, x_3],
        [y_0, y_1, y_2, y_3],
        [across_0, across_1, across_2, across_3],
    ]
    own_part, other_part = partial_cost(noise_pieces, latents)
    parts = col_exchange(core_sum(own_part, swap_core(other_part), n_col))
    tile = functools.reduce(jnp.add, parts)
    tile_1, tile_2 = swap(tile, "col", 1), swap(tile, "col", 2)
    tile_3 = swap(tile_2, "col", 1)
    x_tile, y_tile = swap_x(tile), swap_y(tile)
    pair = jnp.stack([after(tile_1, x_tile, y_tile), tile_2])
    x_pair, y_pair = swap_x(pair), swap_y(pair)
    x_last, y_last = swap_x(tile_3), swap_y(tile_3)
    tiles = [
        [tile, pair, tile_3],
        [x_tile, x_pair, x_last],
        [y_tile, y_pair, y_last],
        [swap_x(y_tile), swap_y(x_pair), swap_x(y_last)],
    ]
    other_tiles = [swap_core(piece) for piece in tiles[0]]
    log_noise = math.log2(own * lax.axis_size("row"))
    stats = ()
    for _ in range(ITERS):
        stats = iteration(tiles, stats, log_noise)
    *products, noise_pot, data_pot = make_targets(tiles[0], other_tiles, stats, latents, n_col, log_noise)
    products = col_exchange(products)
    targets = join(products + [swap_core(piece) for piece in products], n_col)
    return (targets, noise_pot.reshape((own,)), data_pot.reshape((own_data,)))


def per_device(noise, data):
    n_row, n_col = lax.axis_size("row"), lax.axis_size("col")
    whole = 4 * noise.shape[0] * n_row * data.shape[0] * n_col
    if whole <= LOCAL_COST_BYTES and n_row == 8 and n_col == 4:
        return per_device_local(noise, data)
    return per_device_tiled(noise, data)


def solution(mesh):
    placed = (P("row", "col"), P("col", "row"))
    return jax.shard_map(
        per_device,
        mesh=mesh,
        in_specs=placed,
        out_specs=(P(("row", "col"), None), P("row"), P("col")),
        check_vma=False,
    )
```

```python
import functools
import math

import jax
import jax.numpy as jnp
from jax import lax
from jax.experimental import pallas as pl
from jax.experimental.pallas import tpu as pltpu
from jax.sharding import PartitionSpec as P

LATENT = 16384
ITERS = 3
EPSILON = 0.64 / math.sqrt(LATENT)
LOG2E = math.log2(math.e)
TO_LOG2 = LOG2E / EPSILON
CONTRACT = (((1,), (1,)), ((), ()))
LOCAL_COST_BYTES = 8 * 2**20


def noise_update(cost_tile, data_pot, epsilon, log_count):
    scores = (data_pot[None, :] - cost_tile) / epsilon
    local_peak = jnp.max(scores, axis=1)
    highest = lax.pmax(local_peak, "col")
    summed = lax.psum(jnp.sum(jnp.exp(scores - highest[:, None]), axis=1), "col")
    return -epsilon * (log_count + highest + jnp.log(summed))


def data_update(cost_tile, noise_pot, epsilon, log_count):
    scores = (noise_pot[:, None] - cost_tile) / epsilon
    local_peak = jnp.max(scores, axis=0)
    highest = lax.pmax(local_peak, "row")
    summed = lax.psum(jnp.sum(jnp.exp(scores - highest[None, :]), axis=0), "row")
    return -epsilon * (log_count + highest + jnp.log(summed))


def per_device_tiled(noise, data):
    epsilon = EPSILON
    noise_full = lax.all_gather(noise, "col", axis=1, tiled=True)
    noise_norm = jnp.sum(jnp.square(noise_full.astype(jnp.float32)), axis=1) / LATENT
    noise_rows = noise.shape[0]
    data_rows = data.shape[0]
    data_full = lax.all_gather(data, "row", axis=1, tiled=True)
    data_norm = jnp.sum(jnp.square(data_full.astype(jnp.float32)), axis=1) / LATENT
    cross = lax.dot_general(noise_full, data_full, CONTRACT, preferred_element_type=jnp.float32)
    cost_tile = noise_norm[:, None] + data_norm[None, :] - 2.0 / LATENT * cross
    log_noise = math.log(noise_rows * lax.axis_size("row"))
    log_data = math.log(data_rows * lax.axis_size("col"))
    data_pot = jnp.zeros((data_rows,), jnp.float32)
    for step in range(ITERS):
        noise_pot = noise_update(cost_tile, data_pot, epsilon, log_noise)
        data_pot = data_update(cost_tile, noise_pot, epsilon, log_data)
    noise_pot = noise_update(cost_tile, data_pot, epsilon, log_noise)
    weights = jnp.exp(
        (noise_pot[:, None] + data_pot[None, :] - cost_tile) / epsilon + log_noise
    ).astype(jnp.bfloat16)
    targets = lax.psum_scatter(
        jnp.dot(weights, data_full, preferred_element_type=jnp.float32).astype(jnp.bfloat16),
        "col",
        scatter_dimension=0,
        tiled=True,
    )
    return (targets, noise_pot, data_pot)


VMEM = pl.BlockSpec(memory_space=pltpu.VMEM)
WIDTH = 128


def place():
    return lax.axis_index("row"), lax.axis_index("col")


def swap(array, axis, step):
    count = lax.axis_size(axis)
    return lax.ppermute(array, axis, [(i, i ^ step) for i in range(count)])


def swap_core(array):
    return swap(array, "row", 1)


def swap_x(array):
    return swap(array, "row", 2)


def swap_y(array):
    return swap(array, "row", 4)


def after(array, *others):
    return lax.optimization_barrier((array,) + others)[0]


def col_exchange(pieces):
    return [pieces[0]] + [swap(piece, "col", d) for d, piece in enumerate(pieces) if d]


def chip_gather(pieces):
    along_x, along_y, across = [], [], []
    for i, piece in enumerate(pieces):
        along_x.append(swap_x(piece))
        along_y.append(swap_y(piece))
        across.append(swap_x(along_y[i]) if i % 2 else swap_y(along_x[i]))
    return [pieces, along_x, along_y, across]


def block(index, size):
    return pl.ds(pl.multiple_of(index * size, size), size)


def kernel_call(kernel, outs, scratch, vmem, *operands, flops=0):
    moved = sum(a.size * a.dtype.itemsize for a in operands)
    return pl.pallas_call(
        kernel,
        in_specs=[VMEM] * len(operands),
        out_specs=[VMEM] * len(outs),
        out_shape=[jax.ShapeDtypeStruct(shape, dtype) for shape, dtype in outs],
        scratch_shapes=scratch,
        compiler_params=pltpu.CompilerParams(vmem_limit_bytes=vmem * 2**20),
        cost_estimate=pl.CostEstimate(flops=flops, bytes_accessed=moved, transcendentals=0),
    )(*operands)


def deal_kernel(n_col, data_ref, *outs):
    _, col = place()
    part = data_ref.shape[1] // n_col
    for d in range(n_col):
        outs[d][...] = data_ref[:, block(col ^ d, part)]


def deal(data, n_col):
    piece = (data.shape[0], data.shape[1] // n_col)
    return kernel_call(functools.partial(deal_kernel, n_col), [(piece, data.dtype)] * n_col, [], 8, data)


def halve_kernel(noise_ref, own_ref, other_ref):
    row, _ = place()
    core = lax.rem(row, 2)
    half = own_ref.shape[1]
    own_ref[...] = noise_ref[:, block(core, half)]
    other_ref[...] = noise_ref[:, block(1 - core, half)]


def halve(noise):
    half = (noise.shape[0], noise.shape[1] // 2)
    return kernel_call(halve_kernel, [(half, noise.dtype)] * 2, [], 8, noise)


def deal_noise_kernel(n_col, own_ref, other_ref, *outs):
    _, col = place()
    part = own_ref.shape[1] // n_col
    for d in range(n_col):
        outs[d][0] = own_ref[:, block(col ^ d, part)]
        outs[d][1] = other_ref[:, block(col ^ d, part)]


def deal_noise(own, other, n_col):
    shape = (2, own.shape[0], own.shape[1] // n_col)
    return kernel_call(
        functools.partial(deal_noise_kernel, n_col), [(shape, own.dtype)] * n_col, [], 8, own, other
    )


def cost_kernel(n_col, n_chip, *refs):
    noise_refs, latent_refs = refs[:n_col], refs[n_col : n_col + n_chip * n_col]
    own_ref, other_ref, noise_all = refs[n_col + n_chip * n_col :]
    row, col = place()
    _, own, part = noise_refs[0].shape
    height = latent_refs[0].shape[0]
    for d in range(n_col):
        noise_all[(row // 2) ^ col ^ d] = noise_refs[d][...].reshape(2 * own, part)
    noise_norm = jnp.zeros((2 * own, 1), jnp.float32)
    for k in range(n_chip):
        values = noise_all[k].astype(jnp.float32)
        noise_norm += jnp.sum(values * values, axis=1, keepdims=True)
    for d in range(n_col):
        cross = jnp.zeros((2 * own, height), jnp.float32)
        squares = jnp.zeros((height, part), jnp.float32)
        for k in range(n_chip):
            rows = latent_refs[k * n_col + d][...]
            cross += lax.dot_general(noise_all[k], rows, CONTRACT, preferred_element_type=jnp.float32)
            values = rows.astype(jnp.float32)
            squares += values * values
        norm = jnp.sum(squares, axis=1, keepdims=True)
        norm = jnp.broadcast_to(norm, (height, WIDTH)).T[0:1, :]
        cost = (noise_norm + norm - 2.0 * cross) * (TO_LOG2 / LATENT)
        lanes = block(col ^ d, height)
        own_ref[:, lanes] = cost[:own]
        other_ref[:, lanes] = cost[own:]


def partial_cost(noise_pieces, latents):
    n_chip, n_col = len(latents), len(noise_pieces)
    _, own, part = noise_pieces[0].shape
    width = n_col * latents[0][0].shape[0]
    return kernel_call(
        functools.partial(cost_kernel, n_col, n_chip),
        [((own, width), jnp.float32)] * 2,
        [pltpu.VMEM((n_chip, 2 * own, part), jnp.bfloat16)],
        24,
        *noise_pieces,
        *[piece for group in latents for piece in group],
        flops=4 * own * width * n_chip * part,
    )


def core_sum_kernel(n_col, own_ref, other_ref, *outs):
    _, col = place()
    share = own_ref.shape[0] // n_col
    for d in range(n_col):
        rows = block(col ^ d, share)
        outs[d][...] = own_ref[rows, :] + other_ref[rows, :]


def core_sum(own, other, n_col):
    shape = (own.shape[0] // n_col, own.shape[1])
    return kernel_call(
        functools.partial(core_sum_kernel, n_col), [(shape, own.dtype)] * n_col, [], 8, own, other
    )


def rows_of(refs, b):
    lanes = slice(b * WIDTH, (b + 1) * WIDTH)
    parts = []
    for ref in refs:
        if len(ref.shape) == 2:
            parts.append(ref[:, lanes])
        else:
            parts += [ref[i, :, lanes] for i in range(ref.shape[0])]
    return jnp.concatenate(parts)


def row_update(refs, g, log_noise):
    blocks = range(len(g))
    peak = functools.reduce(jnp.maximum, [g[b] - rows_of(refs, b) for b in blocks])
    peak = jnp.max(peak, axis=1, keepdims=True)
    total = functools.reduce(jnp.add, [jnp.exp2(g[b] - rows_of(refs, b) - peak) for b in blocks])
    total = jnp.sum(total, axis=1, keepdims=True)
    return -(log_noise + peak + jnp.log2(total))


def data_potentials(stats, wide):
    if not stats:
        return [jnp.zeros((1, WIDTH), jnp.float32)] * (wide // WIDTH)
    own, other = stats
    result = []
    for first in range(0, wide, WIDTH):
        lanes = slice(first, first + WIDTH)
        peak = jnp.maximum(own[0:1, lanes], other[0:1, lanes])
        total = own[1:2, lanes] * jnp.exp2(own[0:1, lanes] - peak)
        total += other[1:2, lanes] * jnp.exp2(other[0:1, lanes] - peak)
        result.append(-(math.log2(wide) + peak + jnp.log2(total)))
    return result


def iteration_kernel(n_groups, log_noise, *refs):
    *refs, out_ref = refs
    wide = out_ref.shape[1]
    chips = [refs[i : i + 3] for i in range(0, 3 * n_groups, 3)]
    g = data_potentials(refs[3 * n_groups :], wide)
    potentials = [row_update(chip, g, log_noise) for chip in chips]
    for b in range(len(g)):
        scores = [f - rows_of(chip, b) for f, chip in zip(potentials, chips)]
        peak = functools.reduce(jnp.maximum, [jnp.max(s, axis=0, keepdims=True) for s in scores])
        total = functools.reduce(jnp.add, [jnp.sum(jnp.exp2(s - peak), axis=0, keepdims=True) for s in scores])
        out_ref[0:1, b * WIDTH : (b + 1) * WIDTH] = peak
        out_ref[1:2, b * WIDTH : (b + 1) * WIDTH] = total


def iteration(tiles, stats, log_noise):
    wide = tiles[0][0].shape[1]
    operands = [piece for group in tiles for piece in group] + list(stats)
    (own,) = kernel_call(
        functools.partial(iteration_kernel, len(tiles), log_noise),
        [((2, wide), jnp.float32)],
        [],
        16,
        *operands,
        flops=16 * sum(piece.size for piece in operands),
    )
    return own, swap_core(own)


def target_kernel(n_col, n_chip, log_noise, *refs):
    tiles, stats, latent_refs = refs[:6], refs[6:8], refs[8 : 8 + n_chip * n_col]
    refs = refs[8 + n_chip * n_col :]
    target_refs, refs = refs[:n_col], refs[n_col:]
    noise_pot_ref, data_pot_ref, pots, weights = refs
    _, col = place()
    height, wide = weights.shape
    g = data_potentials(stats, wide)
    f = row_update(tiles, g, log_noise)
    for b in range(len(g)):
        lanes = slice(b * WIDTH, (b + 1) * WIDTH)
        pots[:, lanes] = g[b] * (1.0 / TO_LOG2)
        scores = (f + g[b] - rows_of(tiles, b)) + log_noise
        weights[:, lanes] = jnp.exp2(scores).astype(jnp.bfloat16)
    data_pot_ref[...] = pots[:, block(col, wide // n_col)]
    own = height // 2
    share = own // n_col
    f = jnp.broadcast_to(f[:own], (own, WIDTH)).T[0:1, :] * (1.0 / TO_LOG2)
    for d in range(n_col):
        noise_pot_ref[pl.ds(col ^ d, 1), :] = f[:, d * share : (d + 1) * share]

    rows_of_one, part = latent_refs[0].shape
    for k in range(n_chip):
        product = jnp.zeros((height, part), jnp.float32)
        for d in range(n_col):
            product += jnp.dot(
                weights[:, block(col ^ d, rows_of_one)],
                latent_refs[k * n_col + d][...],
                preferred_element_type=jnp.float32,
            )
        product = product.astype(jnp.bfloat16)
        for d in range(n_col):
            target_refs[d][0, k] = product[d * share : (d + 1) * share]
            target_refs[d][1, k] = product[own + d * share : own + (d + 1) * share]


def make_targets(own_tiles, other_tiles, stats, latents, n_col, log_noise):
    n_chip = len(latents)
    share, wide = own_tiles[0].shape
    own = n_col * share
    part = latents[0][0].shape[1]
    return kernel_call(
        functools.partial(target_kernel, n_col, n_chip, log_noise),
        [((2, n_chip, share, part), jnp.bfloat16)] * n_col
        + [((n_col, share), jnp.float32), ((1, wide // n_col), jnp.float32)],
        [pltpu.VMEM((1, wide), jnp.float32), pltpu.VMEM((2 * own, wide), jnp.bfloat16)],
        24,
        *own_tiles,
        *other_tiles,
        *stats,
        *[piece for group in latents for piece in group],
        flops=4 * own * wide * n_chip * part,
    )


def join_kernel(n_col, *refs):
    *pieces, out_ref = refs
    row, col = place()
    _, n_chip, _, part = pieces[0].shape
    for i, piece in enumerate(pieces):
        other, d = divmod(i, n_col)
        for k in range(n_chip):
            out_ref[:, block((row ^ other ^ (2 * k)) * n_col + (col ^ d), part)] = piece[other, k]


def join(pieces, n_col):
    _, n_chip, share, part = pieces[0].shape
    shape = (share, n_chip * part * len(pieces))
    (out,) = kernel_call(
        functools.partial(join_kernel, n_col), [(shape, pieces[0].dtype)], [], 12, *pieces
    )
    return out


def per_device_local(noise, data):
    n_col = lax.axis_size("col")
    own, own_data = noise.shape[0], data.shape[0]
    data_0, *dealt = deal(data, n_col)
    own_half, other_half = halve(noise)
    data_1, data_2 = swap(dealt[0], "col", 1), swap(dealt[1], "col", 2)
    x_0, y_0 = swap_x(data_0), swap_y(data_0)
    noise_0, *dealt_noise = deal_noise(own_half, after(swap_core(other_half), x_0, y_0), n_col)
    data_3 = swap(dealt[2], "col", 3)
    across_0 = swap_y(after(x_0, noise_0))
    x_1, y_1 = swap_x(after(data_1, noise_0)), swap_y(after(data_1, noise_0))
    noise_1 = swap(after(dealt_noise[0], data_2), "col", 1)
    across_1 = swap_x(y_1)
    x_2, y_2 = swap_x(after(data_2, x_1)), swap_y(after(data_2, y_1, across_0))
    noise_2 = swap(after(dealt_noise[1], data_2), "col", 2)
    across_2 = swap_y(x_2)
    x_3 = swap_x(after(data_3, across_1, x_2, noise_1, noise_2))
    y_3 = swap_y(after(data_3, y_2, noise_1, noise_2))
    noise_3 = swap(after(dealt_noise[2], data_3, noise_1), "col", 3)
    across_3 = swap_x(y_3)
    noise_pieces = [noise_0, noise_1, noise_2, noise_3]
    latents = [
        [data_0, data_1, data_2, data_3],
        [x_0, x_1, x_2, x_3],
        [y_0, y_1, y_2, y_3],
        [across_0, across_1, across_2, across_3],
    ]
    own_part, other_part = partial_cost(noise_pieces, latents)
    parts = col_exchange(core_sum(own_part, swap_core(other_part), n_col))
    tile = functools.reduce(jnp.add, parts)
    tile_1, tile_2 = swap(tile, "col", 1), swap(tile, "col", 2)
    tile_3 = swap(tile_2, "col", 1)
    x_tile, y_tile = swap_x(after(tile, tile_1)), swap_y(after(tile, tile_1))
    pair = jnp.stack([tile_1, after(tile_2, x_tile)])
    x_pair, y_pair = swap_x(pair), swap_y(pair)
    x_last, y_last = swap_x(tile_3), swap_y(tile_3)
    tiles = [
        [tile, pair, tile_3],
        [x_tile, x_pair, x_last],
        [y_tile, y_pair, y_last],
        [swap_x(y_tile), swap_y(x_pair), swap_x(y_last)],
    ]
    other_tiles = [swap_core(piece) for piece in tiles[0]]
    log_noise = math.log2(own * lax.axis_size("row"))
    stats = ()
    for _ in range(ITERS):
        stats = iteration(tiles, stats, log_noise)
    *products, noise_pot, data_pot = make_targets(tiles[0], other_tiles, stats, latents, n_col, log_noise)
    products = col_exchange(products)
    targets = join(products + [swap_core(piece) for piece in products], n_col)
    return (targets, noise_pot.reshape((own,)), data_pot.reshape((own_data,)))


def per_device(noise, data):
    n_row, n_col = lax.axis_size("row"), lax.axis_size("col")
    whole = 4 * noise.shape[0] * n_row * data.shape[0] * n_col
    if whole <= LOCAL_COST_BYTES and n_row == 8 and n_col == 4:
        return per_device_local(noise, data)
    return per_device_tiled(noise, data)


def solution(mesh):
    placed = (P("row", "col"), P("col", "row"))
    return jax.shard_map(
        per_device,
        mesh=mesh,
        in_specs=placed,
        out_specs=(P(("row", "col"), None), P("row"), P("col")),
        check_vma=False,
    )
```

```python
import functools
import math

import jax
import jax.numpy as jnp
from jax import lax
from jax.experimental import pallas as pl
from jax.experimental.pallas import tpu as pltpu
from jax.sharding import PartitionSpec as P

LATENT = 16384
ITERS = 3
EPSILON = 0.64 / math.sqrt(LATENT)
LOG2E = math.log2(math.e)
TO_LOG2 = LOG2E / EPSILON
CONTRACT = (((1,), (1,)), ((), ()))
LOCAL_COST_BYTES = 8 * 2**20


def noise_update(cost_tile, data_pot, epsilon, log_count):
    scores = (data_pot[None, :] - cost_tile) / epsilon
    local_peak = jnp.max(scores, axis=1)
    highest = lax.pmax(local_peak, "col")
    summed = lax.psum(jnp.sum(jnp.exp(scores - highest[:, None]), axis=1), "col")
    return -epsilon * (log_count + highest + jnp.log(summed))


def data_update(cost_tile, noise_pot, epsilon, log_count):
    scores = (noise_pot[:, None] - cost_tile) / epsilon
    local_peak = jnp.max(scores, axis=0)
    highest = lax.pmax(local_peak, "row")
    summed = lax.psum(jnp.sum(jnp.exp(scores - highest[None, :]), axis=0), "row")
    return -epsilon * (log_count + highest + jnp.log(summed))


def per_device_tiled(noise, data):
    epsilon = EPSILON
    noise_full = lax.all_gather(noise, "col", axis=1, tiled=True)
    noise_norm = jnp.sum(jnp.square(noise_full.astype(jnp.float32)), axis=1) / LATENT
    noise_rows = noise.shape[0]
    data_rows = data.shape[0]
    data_full = lax.all_gather(data, "row", axis=1, tiled=True)
    data_norm = jnp.sum(jnp.square(data_full.astype(jnp.float32)), axis=1) / LATENT
    cross = lax.dot_general(noise_full, data_full, CONTRACT, preferred_element_type=jnp.float32)
    cost_tile = noise_norm[:, None] + data_norm[None, :] - 2.0 / LATENT * cross
    log_noise = math.log(noise_rows * lax.axis_size("row"))
    log_data = math.log(data_rows * lax.axis_size("col"))
    data_pot = jnp.zeros((data_rows,), jnp.float32)
    for step in range(ITERS):
        noise_pot = noise_update(cost_tile, data_pot, epsilon, log_noise)
        data_pot = data_update(cost_tile, noise_pot, epsilon, log_data)
    noise_pot = noise_update(cost_tile, data_pot, epsilon, log_noise)
    weights = jnp.exp(
        (noise_pot[:, None] + data_pot[None, :] - cost_tile) / epsilon + log_noise
    ).astype(jnp.bfloat16)
    targets = lax.psum_scatter(
        jnp.dot(weights, data_full, preferred_element_type=jnp.float32).astype(jnp.bfloat16),
        "col",
        scatter_dimension=0,
        tiled=True,
    )
    return (targets, noise_pot, data_pot)


VMEM = pl.BlockSpec(memory_space=pltpu.VMEM)
WIDTH = 128


def place():
    return lax.axis_index("row"), lax.axis_index("col")


def swap(array, axis, step):
    count = lax.axis_size(axis)
    return lax.ppermute(array, axis, [(i, i ^ step) for i in range(count)])


def swap_core(array):
    return swap(array, "row", 1)


def swap_x(array):
    return swap(array, "row", 2)


def swap_y(array):
    return swap(array, "row", 4)


def after(array, *others):
    return lax.optimization_barrier((array,) + others)[0]


def col_exchange(pieces):
    count = len(pieces)
    moved = [swap(pieces[d], "col", d) for d in reversed(range(1, count))]
    return [pieces[0]] + moved[::-1]


def chip_gather(pieces):
    along_x, along_y, across = [], [], []
    for i, piece in enumerate(pieces):
        along_x.append(swap_x(piece))
        along_y.append(swap_y(piece))
        across.append(swap_x(along_y[i]) if i % 2 else swap_y(along_x[i]))
    return [pieces, along_x, along_y, across]


def block(index, size):
    return pl.ds(pl.multiple_of(index * size, size), size)


def kernel_call(kernel, outs, scratch, vmem, *operands, flops=0):
    moved = sum(a.size * a.dtype.itemsize for a in operands)
    return pl.pallas_call(
        kernel,
        in_specs=[VMEM] * len(operands),
        out_specs=[VMEM] * len(outs),
        out_shape=[jax.ShapeDtypeStruct(shape, dtype) for shape, dtype in outs],
        scratch_shapes=scratch,
        compiler_params=pltpu.CompilerParams(vmem_limit_bytes=vmem * 2**20),
        cost_estimate=pl.CostEstimate(flops=flops, bytes_accessed=moved, transcendentals=0),
    )(*operands)


def deal_kernel(n_col, data_ref, *outs):
    _, col = place()
    part = data_ref.shape[1] // n_col
    for d in range(n_col):
        outs[d][...] = data_ref[:, block(col ^ d, part)]


def deal(data, n_col):
    piece = (data.shape[0], data.shape[1] // n_col)
    return kernel_call(functools.partial(deal_kernel, n_col), [(piece, data.dtype)] * n_col, [], 8, data)


def halve_kernel(noise_ref, own_ref, other_ref):
    row, _ = place()
    core = lax.rem(row, 2)
    half = own_ref.shape[1]
    own_ref[...] = noise_ref[:, block(core, half)]
    other_ref[...] = noise_ref[:, block(1 - core, half)]


def halve(noise):
    half = (noise.shape[0], noise.shape[1] // 2)
    return kernel_call(halve_kernel, [(half, noise.dtype)] * 2, [], 8, noise)


def deal_noise_kernel(n_col, own_ref, other_ref, *outs):
    _, col = place()
    part = own_ref.shape[1] // n_col
    for d in range(n_col):
        outs[d][0] = own_ref[:, block(col ^ d, part)]
        outs[d][1] = other_ref[:, block(col ^ d, part)]


def deal_noise(own, other, n_col):
    shape = (2, own.shape[0], own.shape[1] // n_col)
    return kernel_call(
        functools.partial(deal_noise_kernel, n_col), [(shape, own.dtype)] * n_col, [], 8, own, other
    )


def cost_kernel(n_col, n_chip, *refs):
    noise_refs, latent_refs = refs[:n_col], refs[n_col : n_col + n_chip * n_col]
    own_ref, other_ref, noise_all = refs[n_col + n_chip * n_col :]
    row, col = place()
    _, own, part = noise_refs[0].shape
    height = latent_refs[0].shape[0]
    for d in range(n_col):
        noise_all[(row // 2) ^ col ^ d] = noise_refs[d][...].reshape(2 * own, part)
    noise_norm = jnp.zeros((2 * own, 1), jnp.float32)
    for k in range(n_chip):
        values = noise_all[k].astype(jnp.float32)
        noise_norm += jnp.sum(values * values, axis=1, keepdims=True)
    for d in range(n_col):
        cross = jnp.zeros((2 * own, height), jnp.float32)
        squares = jnp.zeros((height, part), jnp.float32)
        for k in range(n_chip):
            rows = latent_refs[k * n_col + d][...]
            cross += lax.dot_general(noise_all[k], rows, CONTRACT, preferred_element_type=jnp.float32)
            values = rows.astype(jnp.float32)
            squares += values * values
        norm = jnp.sum(squares, axis=1, keepdims=True)
        norm = jnp.broadcast_to(norm, (height, WIDTH)).T[0:1, :]
        cost = (noise_norm + norm - 2.0 * cross) * (TO_LOG2 / LATENT)
        lanes = block(col ^ d, height)
        own_ref[:, lanes] = cost[:own]
        other_ref[:, lanes] = cost[own:]


def partial_cost(noise_pieces, latents):
    n_chip, n_col = len(latents), len(noise_pieces)
    _, own, part = noise_pieces[0].shape
    width = n_col * latents[0][0].shape[0]
    return kernel_call(
        functools.partial(cost_kernel, n_col, n_chip),
        [((own, width), jnp.float32)] * 2,
        [pltpu.VMEM((n_chip, 2 * own, part), jnp.bfloat16)],
        24,
        *noise_pieces,
        *[piece for group in latents for piece in group],
        flops=4 * own * width * n_chip * part,
    )


def core_sum_kernel(n_col, own_ref, other_ref, *outs):
    _, col = place()
    share = own_ref.shape[0] // n_col
    for d in range(n_col):
        rows = block(col ^ d, share)
        outs[d][...] = own_ref[rows, :] + other_ref[rows, :]


def core_sum(own, other, n_col):
    shape = (own.shape[0] // n_col, own.shape[1])
    return kernel_call(
        functools.partial(core_sum_kernel, n_col), [(shape, own.dtype)] * n_col, [], 8, own, other
    )


def rows_of(refs, b):
    lanes = slice(b * WIDTH, (b + 1) * WIDTH)
    parts = []
    for ref in refs:
        if len(ref.shape) == 2:
            parts.append(ref[:, lanes])
        else:
            parts += [ref[i, :, lanes] for i in reversed(range(ref.shape[0]))]
    return jnp.concatenate(parts)


def row_update(refs, g, log_noise):
    blocks = range(len(g))
    peak = functools.reduce(jnp.maximum, [g[b] - rows_of(refs, b) for b in blocks])
    peak = jnp.max(peak, axis=1, keepdims=True)
    total = functools.reduce(jnp.add, [jnp.exp2(g[b] - rows_of(refs, b) - peak) for b in blocks])
    total = jnp.sum(total, axis=1, keepdims=True)
    return -(log_noise + peak + jnp.log2(total))


def data_potentials(stats, wide):
    if not stats:
        return [jnp.zeros((1, WIDTH), jnp.float32)] * (wide // WIDTH)
    own, other = stats
    result = []
    for first in range(0, wide, WIDTH):
        lanes = slice(first, first + WIDTH)
        peak = jnp.maximum(own[0:1, lanes], other[0:1, lanes])
        total = own[1:2, lanes] * jnp.exp2(own[0:1, lanes] - peak)
        total += other[1:2, lanes] * jnp.exp2(other[0:1, lanes] - peak)
        result.append(-(math.log2(wide) + peak + jnp.log2(total)))
    return result


def iteration_kernel(n_groups, log_noise, *refs):
    *refs, out_ref = refs
    wide = out_ref.shape[1]
    chips = [refs[i : i + 3] for i in range(0, 3 * n_groups, 3)]
    g = data_potentials(refs[3 * n_groups :], wide)
    potentials = [row_update(chip, g, log_noise) for chip in chips]
    for b in range(len(g)):
        scores = [f - rows_of(chip, b) for f, chip in zip(potentials, chips)]
        peak = functools.reduce(jnp.maximum, [jnp.max(s, axis=0, keepdims=True) for s in scores])
        total = functools.reduce(jnp.add, [jnp.sum(jnp.exp2(s - peak), axis=0, keepdims=True) for s in scores])
        out_ref[0:1, b * WIDTH : (b + 1) * WIDTH] = peak
        out_ref[1:2, b * WIDTH : (b + 1) * WIDTH] = total


def iteration(tiles, stats, log_noise):
    wide = tiles[0][0].shape[1]
    operands = [piece for group in tiles for piece in group] + list(stats)
    (own,) = kernel_call(
        functools.partial(iteration_kernel, len(tiles), log_noise),
        [((2, wide), jnp.float32)],
        [],
        16,
        *operands,
        flops=16 * sum(piece.size for piece in operands),
    )
    return own, swap_core(own)


def target_kernel(n_col, n_chip, log_noise, *refs):
    tiles, stats, latent_refs = refs[:6], refs[6:8], refs[8 : 8 + n_chip * n_col]
    refs = refs[8 + n_chip * n_col :]
    target_refs, refs = refs[:n_col], refs[n_col:]
    noise_pot_ref, data_pot_ref, pots, weights = refs
    _, col = place()
    height, wide = weights.shape
    g = data_potentials(stats, wide)
    f = row_update(tiles, g, log_noise)
    for b in range(len(g)):
        lanes = slice(b * WIDTH, (b + 1) * WIDTH)
        pots[:, lanes] = g[b] * (1.0 / TO_LOG2)
        scores = (f + g[b] - rows_of(tiles, b)) + log_noise
        weights[:, lanes] = jnp.exp2(scores).astype(jnp.bfloat16)
    data_pot_ref[...] = pots[:, block(col, wide // n_col)]
    own = height // 2
    share = own // n_col
    f = jnp.broadcast_to(f[:own], (own, WIDTH)).T[0:1, :] * (1.0 / TO_LOG2)
    for d in range(n_col):
        noise_pot_ref[pl.ds(col ^ d, 1), :] = f[:, d * share : (d + 1) * share]

    rows_of_one, part = latent_refs[0].shape
    for k in range(n_chip):
        product = jnp.zeros((height, part), jnp.float32)
        for d in range(n_col):
            product += jnp.dot(
                weights[:, block(col ^ d, rows_of_one)],
                latent_refs[k * n_col + d][...],
                preferred_element_type=jnp.float32,
            )
        product = product.astype(jnp.bfloat16)
        for d in range(n_col):
            target_refs[d][0, k] = product[d * share : (d + 1) * share]
            target_refs[d][1, k] = product[own + d * share : own + (d + 1) * share]


def make_targets(own_tiles, other_tiles, stats, latents, n_col, log_noise):
    n_chip = len(latents)
    share, wide = own_tiles[0].shape
    own = n_col * share
    part = latents[0][0].shape[1]
    return kernel_call(
        functools.partial(target_kernel, n_col, n_chip, log_noise),
        [((2, n_chip, share, part), jnp.bfloat16)] * n_col
        + [((n_col, share), jnp.float32), ((1, wide // n_col), jnp.float32)],
        [pltpu.VMEM((1, wide), jnp.float32), pltpu.VMEM((2 * own, wide), jnp.bfloat16)],
        24,
        *own_tiles,
        *other_tiles,
        *stats,
        *[piece for group in latents for piece in group],
        flops=4 * own * wide * n_chip * part,
    )


def join_kernel(n_col, *refs):
    *pieces, out_ref = refs
    row, col = place()
    _, n_chip, _, part = pieces[0].shape
    for i, piece in enumerate(pieces):
        other, d = i // n_col, n_col - 1 - i % n_col
        for k in range(n_chip):
            out_ref[:, block((row ^ other ^ (2 * k)) * n_col + (col ^ d), part)] = piece[other, k]


def join(pieces, n_col):
    _, n_chip, share, part = pieces[0].shape
    shape = (share, n_chip * part * len(pieces))
    (out,) = kernel_call(
        functools.partial(join_kernel, n_col), [(shape, pieces[0].dtype)], [], 12, *pieces
    )
    return out


def per_device_local(noise, data):
    n_col = lax.axis_size("col")
    own, own_data = noise.shape[0], data.shape[0]
    data_0, *dealt = deal(data, n_col)
    own_half, other_half = halve(noise)
    data_1, data_2 = swap(dealt[0], "col", 1), swap(dealt[1], "col", 2)
    x_0, y_0 = swap_x(data_0), swap_y(data_0)
    noise_0, *dealt_noise = deal_noise(own_half, after(swap_core(other_half), x_0, y_0), n_col)
    data_3 = swap(dealt[2], "col", 3)
    across_0 = swap_y(after(x_0, noise_0))
    x_1, y_1 = swap_x(after(data_1, noise_0)), swap_y(after(data_1, noise_0))
    noise_1 = swap(after(dealt_noise[0], data_2), "col", 1)
    across_1 = swap_x(y_1)
    x_2, y_2 = swap_x(after(data_2, x_1)), swap_y(after(data_2, y_1, across_0))
    noise_2 = swap(after(dealt_noise[1], data_2), "col", 2)
    across_2 = swap_y(x_2)
    x_3, y_3 = swap_x(after(data_3, across_1, x_2, noise_1)), swap_y(after(data_3, y_2, noise_1))
    noise_3 = swap(after(dealt_noise[2], data_3, noise_1), "col", 3)
    across_3 = swap_x(y_3)
    noise_pieces = [noise_0, noise_1, noise_2, noise_3]
    latents = [
        [data_0, data_1, data_2, data_3],
        [x_0, x_1, x_2, x_3],
        [y_0, y_1, y_2, y_3],
        [across_0, across_1, across_2, across_3],
    ]
    own_part, other_part = partial_cost(noise_pieces, latents)
    parts = col_exchange(core_sum(own_part, swap_core(other_part), n_col))
    tile = functools.reduce(jnp.add, parts[::-1])
    tile_2, tile_1 = swap(tile, "col", 2), swap(tile, "col", 1)
    tile_3 = swap(tile_2, "col", 1)
    x_tile, y_tile = swap_x(tile), swap_y(tile)
    pair = jnp.stack([after(tile_2, y_tile), after(tile_1, x_tile)])
    x_pair, y_pair = swap_x(pair), swap_y(pair)
    x_last, y_last = swap_x(tile_3), swap_y(tile_3)
    tiles = [
        [tile, pair, tile_3],
        [x_tile, x_pair, x_last],
        [y_tile, y_pair, y_last],
        [swap_x(y_tile), swap_y(x_pair), swap_x(y_last)],
    ]
    other_tiles = [swap_core(piece) for piece in tiles[0]]
    log_noise = math.log2(own * lax.axis_size("row"))
    stats = ()
    for _ in range(ITERS):
        stats = iteration(tiles, stats, log_noise)
    *products, noise_pot, data_pot = make_targets(tiles[0], other_tiles, stats, latents, n_col, log_noise)
    products = col_exchange(products)
    products = products[::-1]
    targets = join(products + [swap_core(piece) for piece in products], n_col)
    return (targets, noise_pot.reshape((own,)), data_pot.reshape((own_data,)))


def per_device(noise, data):
    n_row, n_col = lax.axis_size("row"), lax.axis_size("col")
    whole = 4 * noise.shape[0] * n_row * data.shape[0] * n_col
    if whole <= LOCAL_COST_BYTES and n_row == 8 and n_col == 4:
        return per_device_local(noise, data)
    return per_device_tiled(noise, data)


def solution(mesh):
    placed = (P("row", "col"), P("col", "row"))
    return jax.shard_map(
        per_device,
        mesh=mesh,
        in_specs=placed,
        out_specs=(P(("row", "col"), None), P("row"), P("col")),
        check_vma=False,
    )
```

```python
import functools
import math

import jax
import jax.numpy as jnp
from jax import lax
from jax.experimental import pallas as pl
from jax.experimental.pallas import tpu as pltpu
from jax.sharding import PartitionSpec as P

LATENT = 16384
ITERS = 3
EPSILON = 0.64 / math.sqrt(LATENT)
LOG2E = math.log2(math.e)
TO_LOG2 = LOG2E / EPSILON
CONTRACT = (((1,), (1,)), ((), ()))
LOCAL_COST_BYTES = 8 * 2**20


def noise_update(cost_tile, data_pot, epsilon, log_count):
    scores = (data_pot[None, :] - cost_tile) / epsilon
    local_peak = jnp.max(scores, axis=1)
    highest = lax.pmax(local_peak, "col")
    summed = lax.psum(jnp.sum(jnp.exp(scores - highest[:, None]), axis=1), "col")
    return -epsilon * (log_count + highest + jnp.log(summed))


def data_update(cost_tile, noise_pot, epsilon, log_count):
    scores = (noise_pot[:, None] - cost_tile) / epsilon
    local_peak = jnp.max(scores, axis=0)
    highest = lax.pmax(local_peak, "row")
    summed = lax.psum(jnp.sum(jnp.exp(scores - highest[None, :]), axis=0), "row")
    return -epsilon * (log_count + highest + jnp.log(summed))


def per_device_tiled(noise, data):
    epsilon = EPSILON
    noise_full = lax.all_gather(noise, "col", axis=1, tiled=True)
    noise_norm = jnp.sum(jnp.square(noise_full.astype(jnp.float32)), axis=1) / LATENT
    noise_rows = noise.shape[0]
    data_rows = data.shape[0]
    data_full = lax.all_gather(data, "row", axis=1, tiled=True)
    data_norm = jnp.sum(jnp.square(data_full.astype(jnp.float32)), axis=1) / LATENT
    cross = lax.dot_general(noise_full, data_full, CONTRACT, preferred_element_type=jnp.float32)
    cost_tile = noise_norm[:, None] + data_norm[None, :] - 2.0 / LATENT * cross
    log_noise = math.log(noise_rows * lax.axis_size("row"))
    log_data = math.log(data_rows * lax.axis_size("col"))
    data_pot = jnp.zeros((data_rows,), jnp.float32)
    for step in range(ITERS):
        noise_pot = noise_update(cost_tile, data_pot, epsilon, log_noise)
        data_pot = data_update(cost_tile, noise_pot, epsilon, log_data)
    noise_pot = noise_update(cost_tile, data_pot, epsilon, log_noise)
    weights = jnp.exp(
        (noise_pot[:, None] + data_pot[None, :] - cost_tile) / epsilon + log_noise
    ).astype(jnp.bfloat16)
    targets = lax.psum_scatter(
        jnp.dot(weights, data_full, preferred_element_type=jnp.float32).astype(jnp.bfloat16),
        "col",
        scatter_dimension=0,
        tiled=True,
    )
    return (targets, noise_pot, data_pot)


VMEM = pl.BlockSpec(memory_space=pltpu.VMEM)
WIDTH = 128


def place():
    return lax.axis_index("row"), lax.axis_index("col")


def swap(array, axis, step):
    count = lax.axis_size(axis)
    return lax.ppermute(array, axis, [(i, i ^ step) for i in range(count)])


def swap_core(array):
    return swap(array, "row", 1)


def swap_x(array):
    return swap(array, "row", 2)


def swap_y(array):
    return swap(array, "row", 4)


def after(array, *others):
    return lax.optimization_barrier((array,) + others)[0]


def col_exchange(pieces):
    count = len(pieces)
    moved = [swap(pieces[d], "col", d) for d in reversed(range(1, count))]
    return [pieces[0]] + moved[::-1]


def chip_gather(pieces):
    along_x, along_y, across = [], [], []
    for i, piece in enumerate(pieces):
        along_x.append(swap_x(piece))
        along_y.append(swap_y(piece))
        across.append(swap_x(along_y[i]) if i % 2 else swap_y(along_x[i]))
    return [pieces, along_x, along_y, across]


def block(index, size):
    return pl.ds(pl.multiple_of(index * size, size), size)


def kernel_call(kernel, outs, scratch, vmem, *operands, flops=0):
    moved = sum(a.size * a.dtype.itemsize for a in operands)
    return pl.pallas_call(
        kernel,
        in_specs=[VMEM] * len(operands),
        out_specs=[VMEM] * len(outs),
        out_shape=[jax.ShapeDtypeStruct(shape, dtype) for shape, dtype in outs],
        scratch_shapes=scratch,
        compiler_params=pltpu.CompilerParams(vmem_limit_bytes=vmem * 2**20),
        cost_estimate=pl.CostEstimate(flops=flops, bytes_accessed=moved, transcendentals=0),
    )(*operands)


def deal_kernel(n_col, data_ref, *outs):
    _, col = place()
    part = data_ref.shape[1] // n_col
    for d in range(n_col):
        outs[d][...] = data_ref[:, block(col ^ d, part)]


def deal(data, n_col):
    piece = (data.shape[0], data.shape[1] // n_col)
    return kernel_call(functools.partial(deal_kernel, n_col), [(piece, data.dtype)] * n_col, [], 8, data)


def halve_kernel(noise_ref, own_ref, other_ref):
    row, _ = place()
    core = lax.rem(row, 2)
    half = own_ref.shape[1]
    own_ref[...] = noise_ref[:, block(core, half)]
    other_ref[...] = noise_ref[:, block(1 - core, half)]


def halve(noise):
    half = (noise.shape[0], noise.shape[1] // 2)
    return kernel_call(halve_kernel, [(half, noise.dtype)] * 2, [], 8, noise)


def deal_noise_kernel(n_col, own_ref, other_ref, *outs):
    _, col = place()
    part = own_ref.shape[1] // n_col
    for d in range(n_col):
        outs[d][0] = own_ref[:, block(col ^ d, part)]
        outs[d][1] = other_ref[:, block(col ^ d, part)]


def deal_noise(own, other, n_col):
    shape = (2, own.shape[0], own.shape[1] // n_col)
    return kernel_call(
        functools.partial(deal_noise_kernel, n_col), [(shape, own.dtype)] * n_col, [], 8, own, other
    )


def cost_kernel(n_col, n_chip, *refs):
    noise_refs, latent_refs = refs[:n_col], refs[n_col : n_col + n_chip * n_col]
    own_ref, other_ref, noise_all = refs[n_col + n_chip * n_col :]
    row, col = place()
    _, own, part = noise_refs[0].shape
    height = latent_refs[0].shape[0]
    for d in range(n_col):
        noise_all[(row // 2) ^ col ^ d] = noise_refs[d][...].reshape(2 * own, part)
    noise_norm = jnp.zeros((2 * own, 1), jnp.float32)
    for k in range(n_chip):
        values = noise_all[k].astype(jnp.float32)
        noise_norm += jnp.sum(values * values, axis=1, keepdims=True)
    for d in range(n_col):
        cross = jnp.zeros((2 * own, height), jnp.float32)
        squares = jnp.zeros((height, part), jnp.float32)
        for k in range(n_chip):
            rows = latent_refs[k * n_col + d][...]
            cross += lax.dot_general(noise_all[k], rows, CONTRACT, preferred_element_type=jnp.float32)
            values = rows.astype(jnp.float32)
            squares += values * values
        norm = jnp.sum(squares, axis=1, keepdims=True)
        norm = jnp.broadcast_to(norm, (height, WIDTH)).T[0:1, :]
        cost = (noise_norm + norm - 2.0 * cross) * (TO_LOG2 / LATENT)
        lanes = block(col ^ d, height)
        own_ref[:, lanes] = cost[:own]
        other_ref[:, lanes] = cost[own:]


def partial_cost(noise_pieces, latents):
    n_chip, n_col = len(latents), len(noise_pieces)
    _, own, part = noise_pieces[0].shape
    width = n_col * latents[0][0].shape[0]
    return kernel_call(
        functools.partial(cost_kernel, n_col, n_chip),
        [((own, width), jnp.float32)] * 2,
        [pltpu.VMEM((n_chip, 2 * own, part), jnp.bfloat16)],
        24,
        *noise_pieces,
        *[piece for group in latents for piece in group],
        flops=4 * own * width * n_chip * part,
    )


def core_sum_kernel(n_col, own_ref, other_ref, *outs):
    _, col = place()
    share = own_ref.shape[0] // n_col
    for d in range(n_col):
        rows = block(col ^ d, share)
        outs[d][...] = own_ref[rows, :] + other_ref[rows, :]


def core_sum(own, other, n_col):
    shape = (own.shape[0] // n_col, own.shape[1])
    return kernel_call(
        functools.partial(core_sum_kernel, n_col), [(shape, own.dtype)] * n_col, [], 8, own, other
    )


def rows_of(refs, b):
    lanes = slice(b * WIDTH, (b + 1) * WIDTH)
    parts = []
    for ref in refs:
        if len(ref.shape) == 2:
            parts.append(ref[:, lanes])
        else:
            parts += [ref[i, :, lanes] for i in reversed(range(ref.shape[0]))]
    return jnp.concatenate(parts)


def row_update(refs, g, log_noise):
    blocks = range(len(g))
    peak = functools.reduce(jnp.maximum, [g[b] - rows_of(refs, b) for b in blocks])
    peak = jnp.max(peak, axis=1, keepdims=True)
    total = functools.reduce(jnp.add, [jnp.exp2(g[b] - rows_of(refs, b) - peak) for b in blocks])
    total = jnp.sum(total, axis=1, keepdims=True)
    return -(log_noise + peak + jnp.log2(total))


def data_potentials(stats, wide):
    if not stats:
        return [jnp.zeros((1, WIDTH), jnp.float32)] * (wide // WIDTH)
    own, other = stats
    result = []
    for first in range(0, wide, WIDTH):
        lanes = slice(first, first + WIDTH)
        peak = jnp.maximum(own[0:1, lanes], other[0:1, lanes])
        total = own[1:2, lanes] * jnp.exp2(own[0:1, lanes] - peak)
        total += other[1:2, lanes] * jnp.exp2(other[0:1, lanes] - peak)
        result.append(-(math.log2(wide) + peak + jnp.log2(total)))
    return result


def iteration_kernel(n_groups, log_noise, *refs):
    *refs, out_ref = refs
    wide = out_ref.shape[1]
    chips = [refs[i : i + 3] for i in range(0, 3 * n_groups, 3)]
    g = data_potentials(refs[3 * n_groups :], wide)
    potentials = [row_update(chip, g, log_noise) for chip in chips]
    for b in range(len(g)):
        scores = [f - rows_of(chip, b) for f, chip in zip(potentials, chips)]
        peak = functools.reduce(jnp.maximum, [jnp.max(s, axis=0, keepdims=True) for s in scores])
        total = functools.reduce(jnp.add, [jnp.sum(jnp.exp2(s - peak), axis=0, keepdims=True) for s in scores])
        out_ref[0:1, b * WIDTH : (b + 1) * WIDTH] = peak
        out_ref[1:2, b * WIDTH : (b + 1) * WIDTH] = total


def iteration(tiles, stats, log_noise):
    wide = tiles[0][0].shape[1]
    operands = [piece for group in tiles for piece in group] + list(stats)
    (own,) = kernel_call(
        functools.partial(iteration_kernel, len(tiles), log_noise),
        [((2, wide), jnp.float32)],
        [],
        16,
        *operands,
        flops=16 * sum(piece.size for piece in operands),
    )
    return own, swap_core(own)


def target_kernel(n_col, n_chip, log_noise, *refs):
    tiles, stats, latent_refs = refs[:6], refs[6:8], refs[8 : 8 + n_chip * n_col]
    refs = refs[8 + n_chip * n_col :]
    target_refs, refs = refs[:n_col], refs[n_col:]
    noise_pot_ref, data_pot_ref, pots, weights = refs
    _, col = place()
    height, wide = weights.shape
    g = data_potentials(stats, wide)
    f = row_update(tiles, g, log_noise)
    for b in range(len(g)):
        lanes = slice(b * WIDTH, (b + 1) * WIDTH)
        pots[:, lanes] = g[b] * (1.0 / TO_LOG2)
        scores = (f + g[b] - rows_of(tiles, b)) + log_noise
        weights[:, lanes] = jnp.exp2(scores).astype(jnp.bfloat16)
    data_pot_ref[...] = pots[:, block(col, wide // n_col)]
    own = height // 2
    share = own // n_col
    f = jnp.broadcast_to(f[:own], (own, WIDTH)).T[0:1, :] * (1.0 / TO_LOG2)
    for d in range(n_col):
        noise_pot_ref[pl.ds(col ^ d, 1), :] = f[:, d * share : (d + 1) * share]

    rows_of_one, part = latent_refs[0].shape
    for k in range(n_chip):
        product = jnp.zeros((height, part), jnp.float32)
        for d in range(n_col):
            product += jnp.dot(
                weights[:, block(col ^ d, rows_of_one)],
                latent_refs[k * n_col + d][...],
                preferred_element_type=jnp.float32,
            )
        product = product.astype(jnp.bfloat16)
        for d in range(n_col):
            target_refs[d][0, k] = product[d * share : (d + 1) * share]
            target_refs[d][1, k] = product[own + d * share : own + (d + 1) * share]


def make_targets(own_tiles, other_tiles, stats, latents, n_col, log_noise):
    n_chip = len(latents)
    share, wide = own_tiles[0].shape
    own = n_col * share
    part = latents[0][0].shape[1]
    return kernel_call(
        functools.partial(target_kernel, n_col, n_chip, log_noise),
        [((2, n_chip, share, part), jnp.bfloat16)] * n_col
        + [((n_col, share), jnp.float32), ((1, wide // n_col), jnp.float32)],
        [pltpu.VMEM((1, wide), jnp.float32), pltpu.VMEM((2 * own, wide), jnp.bfloat16)],
        24,
        *own_tiles,
        *other_tiles,
        *stats,
        *[piece for group in latents for piece in group],
        flops=4 * own * wide * n_chip * part,
    )


def join_kernel(n_col, *refs):
    *pieces, out_ref = refs
    row, col = place()
    _, n_chip, _, part = pieces[0].shape
    for i, piece in enumerate(pieces):
        other, d = i // n_col, n_col - 1 - i % n_col
        for k in range(n_chip):
            out_ref[:, block((row ^ other ^ (2 * k)) * n_col + (col ^ d), part)] = piece[other, k]


def join(pieces, n_col):
    _, n_chip, share, part = pieces[0].shape
    shape = (share, n_chip * part * len(pieces))
    (out,) = kernel_call(
        functools.partial(join_kernel, n_col), [(shape, pieces[0].dtype)], [], 12, *pieces
    )
    return out


def per_device_local(noise, data):
    n_col = lax.axis_size("col")
    own, own_data = noise.shape[0], data.shape[0]
    data_0, *dealt = deal(data, n_col)
    own_half, other_half = halve(noise)
    data_1, data_2 = swap(dealt[0], "col", 1), swap(dealt[1], "col", 2)
    x_0, y_0 = swap_x(data_0), swap_y(data_0)
    noise_0, *dealt_noise = deal_noise(own_half, after(swap_core(other_half), x_0, y_0), n_col)
    data_3 = swap(dealt[2], "col", 3)
    across_0 = swap_y(after(x_0, noise_0))
    x_1, y_1 = swap_x(after(data_1, noise_0)), swap_y(after(data_1, noise_0))
    noise_1 = swap(after(dealt_noise[0], data_2), "col", 1)
    across_1 = swap_x(y_1)
    x_2, y_2 = swap_x(after(data_2, x_1)), swap_y(after(data_2, y_1, across_0))
    noise_2 = swap(after(dealt_noise[1], data_2), "col", 2)
    across_2 = swap_y(x_2)
    x_3, y_3 = swap_x(after(data_3, across_1, x_2, noise_1)), swap_y(after(data_3, y_2, noise_1))
    noise_3 = swap(after(dealt_noise[2], data_3, noise_1), "col", 3)
    across_3 = swap_x(y_3)
    noise_pieces = [noise_0, noise_1, noise_2, noise_3]
    latents = [
        [data_0, data_1, data_2, data_3],
        [x_0, x_1, x_2, x_3],
        [y_0, y_1, y_2, y_3],
        [across_0, across_1, across_2, across_3],
    ]
    own_part, other_part = partial_cost(noise_pieces, latents)
    parts = col_exchange(core_sum(own_part, swap_core(other_part), n_col))
    tile = functools.reduce(jnp.add, parts[::-1])
    tile_2, tile_1 = swap(tile, "col", 2), swap(tile, "col", 1)
    tile_3 = swap(tile_2, "col", 1)
    x_tile, y_tile = swap_x(tile), swap_y(tile)
    pair = jnp.stack([after(tile_2, y_tile), after(tile_1, x_tile)])
    x_pair, y_pair = swap_x(pair), swap_y(pair)
    x_last, y_last = swap_x(tile_3), swap_y(tile_3)
    tiles = [
        [tile, pair, tile_3],
        [x_tile, x_pair, x_last],
        [y_tile, y_pair, y_last],
        [swap_y(x_tile), swap_x(y_pair), swap_y(x_last)],
    ]
    other_tiles = [swap_core(piece) for piece in tiles[0]]
    log_noise = math.log2(own * lax.axis_size("row"))
    stats = ()
    for _ in range(ITERS):
        stats = iteration(tiles, stats, log_noise)
    *products, noise_pot, data_pot = make_targets(tiles[0], other_tiles, stats, latents, n_col, log_noise)
    products = col_exchange(products)
    products = products[::-1]
    targets = join(products + [swap_core(piece) for piece in products], n_col)
    return (targets, noise_pot.reshape((own,)), data_pot.reshape((own_data,)))


def per_device(noise, data):
    n_row, n_col = lax.axis_size("row"), lax.axis_size("col")
    whole = 4 * noise.shape[0] * n_row * data.shape[0] * n_col
    if whole <= LOCAL_COST_BYTES and n_row == 8 and n_col == 4:
        return per_device_local(noise, data)
    return per_device_tiled(noise, data)


def solution(mesh):
    placed = (P("row", "col"), P("col", "row"))
    return jax.shard_map(
        per_device,
        mesh=mesh,
        in_specs=placed,
        out_specs=(P(("row", "col"), None), P("row"), P("col")),
        check_vma=False,
    )
```

```python
import functools
import math

import jax
import jax.numpy as jnp
from jax import lax
from jax.experimental import pallas as pl
from jax.experimental.pallas import tpu as pltpu
from jax.sharding import PartitionSpec as P

LATENT = 16384
ITERS = 3
EPSILON = 0.64 / math.sqrt(LATENT)
LOG2E = math.log2(math.e)
TO_LOG2 = LOG2E / EPSILON
CONTRACT = (((1,), (1,)), ((), ()))
LOCAL_COST_BYTES = 8 * 2**20


def noise_update(cost_tile, data_pot, epsilon, log_count):
    scores = (data_pot[None, :] - cost_tile) / epsilon
    local_peak = jnp.max(scores, axis=1)
    highest = lax.pmax(local_peak, "col")
    summed = lax.psum(jnp.sum(jnp.exp(scores - highest[:, None]), axis=1), "col")
    return -epsilon * (log_count + highest + jnp.log(summed))


def data_update(cost_tile, noise_pot, epsilon, log_count):
    scores = (noise_pot[:, None] - cost_tile) / epsilon
    local_peak = jnp.max(scores, axis=0)
    highest = lax.pmax(local_peak, "row")
    summed = lax.psum(jnp.sum(jnp.exp(scores - highest[None, :]), axis=0), "row")
    return -epsilon * (log_count + highest + jnp.log(summed))


def per_device_tiled(noise, data):
    epsilon = EPSILON
    noise_full = lax.all_gather(noise, "col", axis=1, tiled=True)
    noise_norm = jnp.sum(jnp.square(noise_full.astype(jnp.float32)), axis=1) / LATENT
    noise_rows = noise.shape[0]
    data_rows = data.shape[0]
    data_full = lax.all_gather(data, "row", axis=1, tiled=True)
    data_norm = jnp.sum(jnp.square(data_full.astype(jnp.float32)), axis=1) / LATENT
    cross = lax.dot_general(noise_full, data_full, CONTRACT, preferred_element_type=jnp.float32)
    cost_tile = noise_norm[:, None] + data_norm[None, :] - 2.0 / LATENT * cross
    log_noise = math.log(noise_rows * lax.axis_size("row"))
    log_data = math.log(data_rows * lax.axis_size("col"))
    data_pot = jnp.zeros((data_rows,), jnp.float32)
    for step in range(ITERS):
        noise_pot = noise_update(cost_tile, data_pot, epsilon, log_noise)
        data_pot = data_update(cost_tile, noise_pot, epsilon, log_data)
    noise_pot = noise_update(cost_tile, data_pot, epsilon, log_noise)
    weights = jnp.exp(
        (noise_pot[:, None] + data_pot[None, :] - cost_tile) / epsilon + log_noise
    ).astype(jnp.bfloat16)
    targets = lax.psum_scatter(
        jnp.dot(weights, data_full, preferred_element_type=jnp.float32).astype(jnp.bfloat16),
        "col",
        scatter_dimension=0,
        tiled=True,
    )
    return (targets, noise_pot, data_pot)


VMEM = pl.BlockSpec(memory_space=pltpu.VMEM)
WIDTH = 128


def place():
    return lax.axis_index("row"), lax.axis_index("col")


def swap(array, axis, step):
    count = lax.axis_size(axis)
    return lax.ppermute(array, axis, [(i, i ^ step) for i in range(count)])


def swap_core(array):
    return swap(array, "row", 1)


def swap_x(array):
    return swap(array, "row", 2)


def swap_y(array):
    return swap(array, "row", 4)


def after(array, *others):
    return lax.optimization_barrier((array,) + others)[0]


def col_exchange(pieces):
    count = len(pieces)
    moved = [swap(pieces[d], "col", d) for d in reversed(range(1, count))]
    return [pieces[0]] + moved[::-1]


def chip_gather(pieces):
    along_x, along_y, across = [], [], []
    for i, piece in enumerate(pieces):
        along_x.append(swap_x(piece))
        along_y.append(swap_y(piece))
        across.append(swap_x(along_y[i]) if i % 2 else swap_y(along_x[i]))
    return [pieces, along_x, along_y, across]


def block(index, size):
    return pl.ds(pl.multiple_of(index * size, size), size)


def kernel_call(kernel, outs, scratch, vmem, *operands, flops=0):
    moved = sum(a.size * a.dtype.itemsize for a in operands)
    return pl.pallas_call(
        kernel,
        in_specs=[VMEM] * len(operands),
        out_specs=[VMEM] * len(outs),
        out_shape=[jax.ShapeDtypeStruct(shape, dtype) for shape, dtype in outs],
        scratch_shapes=scratch,
        compiler_params=pltpu.CompilerParams(vmem_limit_bytes=vmem * 2**20),
        cost_estimate=pl.CostEstimate(flops=flops, bytes_accessed=moved, transcendentals=0),
    )(*operands)


def deal_kernel(n_col, data_ref, *outs):
    _, col = place()
    part = data_ref.shape[1] // n_col
    for d in range(n_col):
        outs[d][...] = data_ref[:, block(col ^ d, part)]


def deal(data, n_col):
    piece = (data.shape[0], data.shape[1] // n_col)
    return kernel_call(functools.partial(deal_kernel, n_col), [(piece, data.dtype)] * n_col, [], 8, data)


def halve_kernel(noise_ref, own_ref, other_ref):
    row, _ = place()
    core = lax.rem(row, 2)
    half = own_ref.shape[1]
    own_ref[...] = noise_ref[:, block(core, half)]
    other_ref[...] = noise_ref[:, block(1 - core, half)]


def halve(noise):
    half = (noise.shape[0], noise.shape[1] // 2)
    return kernel_call(halve_kernel, [(half, noise.dtype)] * 2, [], 8, noise)


def deal_noise_kernel(n_col, own_ref, other_ref, *outs):
    _, col = place()
    part = own_ref.shape[1] // n_col
    for d in range(n_col):
        outs[d][0] = own_ref[:, block(col ^ d, part)]
        outs[d][1] = other_ref[:, block(col ^ d, part)]


def deal_noise(own, other, n_col):
    shape = (2, own.shape[0], own.shape[1] // n_col)
    return kernel_call(
        functools.partial(deal_noise_kernel, n_col), [(shape, own.dtype)] * n_col, [], 8, own, other
    )


def cost_kernel(n_col, n_chip, *refs):
    noise_refs, latent_refs = refs[:n_col], refs[n_col : n_col + n_chip * n_col]
    own_ref, other_ref, noise_all = refs[n_col + n_chip * n_col :]
    row, col = place()
    _, own, part = noise_refs[0].shape
    height = latent_refs[0].shape[0]
    for d in range(n_col):
        noise_all[(row // 2) ^ col ^ d] = noise_refs[d][...].reshape(2 * own, part)
    noise_norm = jnp.zeros((2 * own, 1), jnp.float32)
    for k in range(n_chip):
        values = noise_all[k].astype(jnp.float32)
        noise_norm += jnp.sum(values * values, axis=1, keepdims=True)
    for d in range(n_col):
        cross = jnp.zeros((2 * own, height), jnp.float32)
        squares = jnp.zeros((height, part), jnp.float32)
        for k in range(n_chip):
            rows = latent_refs[k * n_col + d][...]
            cross += lax.dot_general(noise_all[k], rows, CONTRACT, preferred_element_type=jnp.float32)
            values = rows.astype(jnp.float32)
            squares += values * values
        norm = jnp.sum(squares, axis=1, keepdims=True)
        norm = jnp.broadcast_to(norm, (height, WIDTH)).T[0:1, :]
        cost = (noise_norm + norm - 2.0 * cross) * (TO_LOG2 / LATENT)
        lanes = block(col ^ d, height)
        own_ref[:, lanes] = cost[:own]
        other_ref[:, lanes] = cost[own:]


def partial_cost(noise_pieces, latents):
    n_chip, n_col = len(latents), len(noise_pieces)
    _, own, part = noise_pieces[0].shape
    width = n_col * latents[0][0].shape[0]
    return kernel_call(
        functools.partial(cost_kernel, n_col, n_chip),
        [((own, width), jnp.float32)] * 2,
        [pltpu.VMEM((n_chip, 2 * own, part), jnp.bfloat16)],
        24,
        *noise_pieces,
        *[piece for group in latents for piece in group],
        flops=4 * own * width * n_chip * part,
    )


def core_sum_kernel(n_col, own_ref, other_ref, *outs):
    _, col = place()
    share = own_ref.shape[0] // n_col
    for d in range(n_col):
        rows = block(col ^ d, share)
        outs[d][...] = own_ref[rows, :] + other_ref[rows, :]


def core_sum(own, other, n_col):
    shape = (own.shape[0] // n_col, own.shape[1])
    return kernel_call(
        functools.partial(core_sum_kernel, n_col), [(shape, own.dtype)] * n_col, [], 8, own, other
    )


def rows_of(refs, b):
    lanes = slice(b * WIDTH, (b + 1) * WIDTH)
    parts = []
    for ref in refs:
        if len(ref.shape) == 2:
            parts.append(ref[:, lanes])
        else:
            parts += [ref[i, :, lanes] for i in reversed(range(ref.shape[0]))]
    return jnp.concatenate(parts)


def row_update(refs, g, log_noise):
    blocks = range(len(g))
    peak = functools.reduce(jnp.maximum, [g[b] - rows_of(refs, b) for b in blocks])
    peak = jnp.max(peak, axis=1, keepdims=True)
    total = functools.reduce(jnp.add, [jnp.exp2(g[b] - rows_of(refs, b) - peak) for b in blocks])
    total = jnp.sum(total, axis=1, keepdims=True)
    return -(log_noise + peak + jnp.log2(total))


def data_potentials(stats, wide):
    if not stats:
        return [jnp.zeros((1, WIDTH), jnp.float32)] * (wide // WIDTH)
    own, other = stats
    result = []
    for first in range(0, wide, WIDTH):
        lanes = slice(first, first + WIDTH)
        peak = jnp.maximum(own[0:1, lanes], other[0:1, lanes])
        total = own[1:2, lanes] * jnp.exp2(own[0:1, lanes] - peak)
        total += other[1:2, lanes] * jnp.exp2(other[0:1, lanes] - peak)
        result.append(-(math.log2(wide) + peak + jnp.log2(total)))
    return result


def iteration_kernel(n_groups, log_noise, *refs):
    *refs, out_ref = refs
    wide = out_ref.shape[1]
    chips = [refs[i : i + 3] for i in range(0, 3 * n_groups, 3)]
    g = data_potentials(refs[3 * n_groups :], wide)
    potentials = [row_update(chip, g, log_noise) for chip in chips]
    for b in range(len(g)):
        scores = [f - rows_of(chip, b) for f, chip in zip(potentials, chips)]
        peak = functools.reduce(jnp.maximum, [jnp.max(s, axis=0, keepdims=True) for s in scores])
        total = functools.reduce(jnp.add, [jnp.sum(jnp.exp2(s - peak), axis=0, keepdims=True) for s in scores])
        out_ref[0:1, b * WIDTH : (b + 1) * WIDTH] = peak
        out_ref[1:2, b * WIDTH : (b + 1) * WIDTH] = total


def iteration(tiles, stats, log_noise):
    wide = tiles[0][0].shape[1]
    operands = [piece for group in tiles for piece in group] + list(stats)
    (own,) = kernel_call(
        functools.partial(iteration_kernel, len(tiles), log_noise),
        [((2, wide), jnp.float32)],
        [],
        16,
        *operands,
        flops=16 * sum(piece.size for piece in operands),
    )
    return own, swap_y(own)


def target_kernel(n_col, n_chip, log_noise, *refs):
    tiles, stats, latent_refs = refs[:6], refs[6:8], refs[8 : 8 + n_chip * n_col]
    refs = refs[8 + n_chip * n_col :]
    target_refs, refs = refs[:n_col], refs[n_col:]
    noise_pot_ref, data_pot_ref, pots, weights = refs
    _, col = place()
    height, wide = weights.shape
    g = data_potentials(stats, wide)
    f = row_update(tiles, g, log_noise)
    for b in range(len(g)):
        lanes = slice(b * WIDTH, (b + 1) * WIDTH)
        pots[:, lanes] = g[b] * (1.0 / TO_LOG2)
        scores = (f + g[b] - rows_of(tiles, b)) + log_noise
        weights[:, lanes] = jnp.exp2(scores).astype(jnp.bfloat16)
    data_pot_ref[...] = pots[:, block(col, wide // n_col)]
    own = height // 2
    share = own // n_col
    f = jnp.broadcast_to(f[:own], (own, WIDTH)).T[0:1, :] * (1.0 / TO_LOG2)
    for d in range(n_col):
        noise_pot_ref[pl.ds(col ^ d, 1), :] = f[:, d * share : (d + 1) * share]

    rows_of_one, part = latent_refs[0].shape
    for k in range(n_chip):
        product = jnp.zeros((height, part), jnp.float32)
        for d in range(n_col):
            product += jnp.dot(
                weights[:, block(col ^ d, rows_of_one)],
                latent_refs[k * n_col + d][...],
                preferred_element_type=jnp.float32,
            )
        product = product.astype(jnp.bfloat16)
        for d in range(n_col):
            target_refs[d][0, k] = product[d * share : (d + 1) * share]
            target_refs[d][1, k] = product[own + d * share : own + (d + 1) * share]


def make_targets(own_tiles, other_tiles, stats, latents, n_col, log_noise):
    n_chip = len(latents)
    share, wide = own_tiles[0].shape
    own = n_col * share
    part = latents[0][0].shape[1]
    return kernel_call(
        functools.partial(target_kernel, n_col, n_chip, log_noise),
        [((2, n_chip, share, part), jnp.bfloat16)] * n_col
        + [((n_col, share), jnp.float32), ((1, wide // n_col), jnp.float32)],
        [pltpu.VMEM((1, wide), jnp.float32), pltpu.VMEM((2 * own, wide), jnp.bfloat16)],
        24,
        *own_tiles,
        *other_tiles,
        *stats,
        *[piece for group in latents for piece in group],
        flops=4 * own * wide * n_chip * part,
    )


def join_kernel(n_col, *refs):
    *pieces, out_ref = refs
    row, col = place()
    _, n_chip, _, part = pieces[0].shape
    for i, piece in enumerate(pieces):
        other, d = i // n_col, n_col - 1 - i % n_col
        for k in range(n_chip):
            out_ref[:, block((row ^ other ^ (2 * k)) * n_col + (col ^ d), part)] = piece[other, k]


def join(pieces, n_col):
    _, n_chip, share, part = pieces[0].shape
    shape = (share, n_chip * part * len(pieces))
    (out,) = kernel_call(
        functools.partial(join_kernel, n_col), [(shape, pieces[0].dtype)], [], 12, *pieces
    )
    return out


def per_device_local(noise, data):
    n_col = lax.axis_size("col")
    own, own_data = noise.shape[0], data.shape[0]
    data_0, *dealt = deal(data, n_col)
    own_half, other_half = halve(noise)
    data_1, data_2 = swap(dealt[0], "col", 1), swap(dealt[1], "col", 2)
    x_0, y_0 = swap_x(data_0), swap_y(data_0)
    noise_0, *dealt_noise = deal_noise(own_half, after(swap_core(other_half), x_0, y_0), n_col)
    data_3 = swap(dealt[2], "col", 3)
    across_0 = swap_y(after(x_0, noise_0))
    x_1, y_1 = swap_x(after(data_1, noise_0)), swap_y(after(data_1, noise_0))
    noise_1 = swap(after(dealt_noise[0], data_2), "col", 1)
    across_1 = swap_x(y_1)
    x_2, y_2 = swap_x(after(data_2, x_1)), swap_y(after(data_2, y_1, across_0))
    noise_2 = swap(after(dealt_noise[1], data_2), "col", 2)
    across_2 = swap_y(x_2)
    x_3, y_3 = swap_x(after(data_3, across_1, x_2, noise_1)), swap_y(after(data_3, y_2, noise_1))
    noise_3 = swap(after(dealt_noise[2], data_3, noise_1), "col", 3)
    across_3 = swap_x(y_3)
    noise_pieces = [noise_0, noise_1, noise_2, noise_3]
    latents = [
        [data_0, data_1, data_2, data_3],
        [x_0, x_1, x_2, x_3],
        [y_0, y_1, y_2, y_3],
        [across_0, across_1, across_2, across_3],
    ]
    own_part, other_part = partial_cost(noise_pieces, latents)
    parts = col_exchange(core_sum(own_part, swap_core(other_part), n_col))
    tile = functools.reduce(jnp.add, parts[::-1])
    tile_2, tile_1 = swap(tile, "col", 2), swap(tile, "col", 1)
    tile_3 = swap(tile_2, "col", 1)
    x_tile = swap_x(tile)
    pair = jnp.stack([after(tile_2, x_tile), tile_1])
    tiles = [[tile, pair, tile_3], [x_tile, swap_x(pair), swap_x(tile_3)]]
    other_tiles = [swap_core(piece) for piece in tiles[0]]
    tiles += [other_tiles, [swap_core(piece) for piece in tiles[1]]]
    log_noise = math.log2(own * lax.axis_size("row"))
    stats = ()
    for _ in range(ITERS):
        stats = iteration(tiles, stats, log_noise)
    *products, noise_pot, data_pot = make_targets(tiles[0], other_tiles, stats, latents, n_col, log_noise)
    products = col_exchange(products)
    products = products[::-1]
    targets = join(products + [swap_core(piece) for piece in products], n_col)
    return (targets, noise_pot.reshape((own,)), data_pot.reshape((own_data,)))


def per_device(noise, data):
    n_row, n_col = lax.axis_size("row"), lax.axis_size("col")
    whole = 4 * noise.shape[0] * n_row * data.shape[0] * n_col
    if whole <= LOCAL_COST_BYTES and n_row == 8 and n_col == 4:
        return per_device_local(noise, data)
    return per_device_tiled(noise, data)


def solution(mesh):
    placed = (P("row", "col"), P("col", "row"))
    return jax.shard_map(
        per_device,
        mesh=mesh,
        in_specs=placed,
        out_specs=(P(("row", "col"), None), P("row"), P("col")),
        check_vma=False,
    )
```

```python
import functools
import math

import jax
import jax.numpy as jnp
from jax import lax
from jax.experimental import pallas as pl
from jax.experimental.pallas import tpu as pltpu
from jax.sharding import PartitionSpec as P

LATENT = 16384
ITERS = 3
EPSILON = 0.64 / math.sqrt(LATENT)
LOG2E = math.log2(math.e)
TO_LOG2 = LOG2E / EPSILON
CONTRACT = (((1,), (1,)), ((), ()))
LOCAL_COST_BYTES = 8 * 2**20


def noise_update(cost_tile, data_pot, epsilon, log_count):
    scores = (data_pot[None, :] - cost_tile) / epsilon
    local_peak = jnp.max(scores, axis=1)
    highest = lax.pmax(local_peak, "col")
    summed = lax.psum(jnp.sum(jnp.exp(scores - highest[:, None]), axis=1), "col")
    return -epsilon * (log_count + highest + jnp.log(summed))


def data_update(cost_tile, noise_pot, epsilon, log_count):
    scores = (noise_pot[:, None] - cost_tile) / epsilon
    local_peak = jnp.max(scores, axis=0)
    highest = lax.pmax(local_peak, "row")
    summed = lax.psum(jnp.sum(jnp.exp(scores - highest[None, :]), axis=0), "row")
    return -epsilon * (log_count + highest + jnp.log(summed))


def per_device_tiled(noise, data):
    epsilon = EPSILON
    noise_full = lax.all_gather(noise, "col", axis=1, tiled=True)
    noise_norm = jnp.sum(jnp.square(noise_full.astype(jnp.float32)), axis=1) / LATENT
    noise_rows = noise.shape[0]
    data_rows = data.shape[0]
    data_full = lax.all_gather(data, "row", axis=1, tiled=True)
    data_norm = jnp.sum(jnp.square(data_full.astype(jnp.float32)), axis=1) / LATENT
    cross = lax.dot_general(noise_full, data_full, CONTRACT, preferred_element_type=jnp.float32)
    cost_tile = noise_norm[:, None] + data_norm[None, :] - 2.0 / LATENT * cross
    log_noise = math.log(noise_rows * lax.axis_size("row"))
    log_data = math.log(data_rows * lax.axis_size("col"))
    data_pot = jnp.zeros((data_rows,), jnp.float32)
    for step in range(ITERS):
        noise_pot = noise_update(cost_tile, data_pot, epsilon, log_noise)
        data_pot = data_update(cost_tile, noise_pot, epsilon, log_data)
    noise_pot = noise_update(cost_tile, data_pot, epsilon, log_noise)
    weights = jnp.exp(
        (noise_pot[:, None] + data_pot[None, :] - cost_tile) / epsilon + log_noise
    ).astype(jnp.bfloat16)
    targets = lax.psum_scatter(
        jnp.dot(weights, data_full, preferred_element_type=jnp.float32).astype(jnp.bfloat16),
        "col",
        scatter_dimension=0,
        tiled=True,
    )
    return (targets, noise_pot, data_pot)


VMEM = pl.BlockSpec(memory_space=pltpu.VMEM)
WIDTH = 128


def place():
    return lax.axis_index("row"), lax.axis_index("col")


def swap(array, axis, step):
    count = lax.axis_size(axis)
    return lax.ppermute(array, axis, [(i, i ^ step) for i in range(count)])


def swap_core(array):
    return swap(array, "row", 1)


def swap_x(array):
    return swap(array, "row", 2)


def swap_y(array):
    return swap(array, "row", 4)


def after(array, *others):
    return lax.optimization_barrier((array,) + others)[0]


def col_exchange(pieces):
    count = len(pieces)
    moved = [swap(pieces[d], "col", d) for d in reversed(range(1, count))]
    return [pieces[0]] + moved[::-1]


def chip_gather(pieces):
    along_x, along_y, across = [], [], []
    for i, piece in enumerate(pieces):
        along_x.append(swap_x(piece))
        along_y.append(swap_y(piece))
        across.append(swap_x(along_y[i]) if i % 2 else swap_y(along_x[i]))
    return [pieces, along_x, along_y, across]


def block(index, size):
    return pl.ds(pl.multiple_of(index * size, size), size)


def kernel_call(kernel, outs, scratch, vmem, *operands, flops=0):
    moved = sum(a.size * a.dtype.itemsize for a in operands)
    return pl.pallas_call(
        kernel,
        in_specs=[VMEM] * len(operands),
        out_specs=[VMEM] * len(outs),
        out_shape=[jax.ShapeDtypeStruct(shape, dtype) for shape, dtype in outs],
        scratch_shapes=scratch,
        compiler_params=pltpu.CompilerParams(vmem_limit_bytes=vmem * 2**20),
        cost_estimate=pl.CostEstimate(flops=flops, bytes_accessed=moved, transcendentals=0),
    )(*operands)


def deal_kernel(n_col, data_ref, *outs):
    _, col = place()
    part = data_ref.shape[1] // n_col
    for d in range(n_col):
        outs[d][...] = data_ref[:, block(col ^ d, part)]


def deal(data, n_col):
    piece = (data.shape[0], data.shape[1] // n_col)
    return kernel_call(functools.partial(deal_kernel, n_col), [(piece, data.dtype)] * n_col, [], 8, data)


def halve_kernel(noise_ref, own_ref, other_ref):
    row, _ = place()
    core = lax.rem(row, 2)
    half = own_ref.shape[1]
    own_ref[...] = noise_ref[:, block(core, half)]
    other_ref[...] = noise_ref[:, block(1 - core, half)]


def halve(noise):
    half = (noise.shape[0], noise.shape[1] // 2)
    return kernel_call(halve_kernel, [(half, noise.dtype)] * 2, [], 8, noise)


def deal_noise_kernel(n_col, own_ref, other_ref, *outs):
    _, col = place()
    part = own_ref.shape[1] // n_col
    for d in range(n_col):
        outs[d][0] = own_ref[:, block(col ^ d, part)]
        outs[d][1] = other_ref[:, block(col ^ d, part)]


def deal_noise(own, other, n_col):
    shape = (2, own.shape[0], own.shape[1] // n_col)
    return kernel_call(
        functools.partial(deal_noise_kernel, n_col), [(shape, own.dtype)] * n_col, [], 8, own, other
    )


def cost_kernel(n_col, n_chip, *refs):
    noise_refs, latent_refs = refs[:n_col], refs[n_col : n_col + n_chip * n_col]
    own_ref, other_ref, noise_all = refs[n_col + n_chip * n_col :]
    row, col = place()
    _, own, part = noise_refs[0].shape
    height = latent_refs[0].shape[0]
    for d in range(n_col):
        noise_all[(row // 2) ^ col ^ d] = noise_refs[d][...].reshape(2 * own, part)
    noise_norm = jnp.zeros((2 * own, 1), jnp.float32)
    for k in range(n_chip):
        values = noise_all[k].astype(jnp.float32)
        noise_norm += jnp.sum(values * values, axis=1, keepdims=True)
    for d in range(n_col):
        cross = jnp.zeros((2 * own, height), jnp.float32)
        squares = jnp.zeros((height, part), jnp.float32)
        for k in range(n_chip):
            rows = latent_refs[k * n_col + d][...]
            cross += lax.dot_general(noise_all[k], rows, CONTRACT, preferred_element_type=jnp.float32)
            values = rows.astype(jnp.float32)
            squares += values * values
        norm = jnp.sum(squares, axis=1, keepdims=True)
        norm = jnp.broadcast_to(norm, (height, WIDTH)).T[0:1, :]
        cost = (noise_norm + norm - 2.0 * cross) * (TO_LOG2 / LATENT)
        lanes = block(col ^ d, height)
        own_ref[:, lanes] = cost[:own]
        other_ref[:, lanes] = cost[own:]


def partial_cost(noise_pieces, latents):
    n_chip, n_col = len(latents), len(noise_pieces)
    _, own, part = noise_pieces[0].shape
    width = n_col * latents[0][0].shape[0]
    return kernel_call(
        functools.partial(cost_kernel, n_col, n_chip),
        [((own, width), jnp.float32)] * 2,
        [pltpu.VMEM((n_chip, 2 * own, part), jnp.bfloat16)],
        24,
        *noise_pieces,
        *[piece for group in latents for piece in group],
        flops=4 * own * width * n_chip * part,
    )


def core_sum_kernel(n_col, own_ref, other_ref, *outs):
    _, col = place()
    share = own_ref.shape[0] // n_col
    for d in range(n_col):
        rows = block(col ^ d, share)
        outs[d][...] = own_ref[rows, :] + other_ref[rows, :]


def core_sum(own, other, n_col):
    shape = (own.shape[0] // n_col, own.shape[1])
    return kernel_call(
        functools.partial(core_sum_kernel, n_col), [(shape, own.dtype)] * n_col, [], 8, own, other
    )


def rows_of(refs, b):
    lanes = slice(b * WIDTH, (b + 1) * WIDTH)
    parts = [ref[i, :, lanes] for ref in refs for i in (1, 0)]
    return jnp.concatenate(parts)


def row_update(refs, g, log_noise):
    blocks = range(len(g))
    peak = functools.reduce(jnp.maximum, [g[b] - rows_of(refs, b) for b in blocks])
    peak = jnp.max(peak, axis=1, keepdims=True)
    total = functools.reduce(jnp.add, [jnp.exp2(g[b] - rows_of(refs, b) - peak) for b in blocks])
    total = jnp.sum(total, axis=1, keepdims=True)
    return -(log_noise + peak + jnp.log2(total))


def data_potentials(stats, wide):
    if not stats:
        return [jnp.zeros((1, WIDTH), jnp.float32)] * (wide // WIDTH)
    own, other = stats
    result = []
    for first in range(0, wide, WIDTH):
        lanes = slice(first, first + WIDTH)
        peak = jnp.maximum(own[0:1, lanes], other[0:1, lanes])
        total = own[1:2, lanes] * jnp.exp2(own[0:1, lanes] - peak)
        total += other[1:2, lanes] * jnp.exp2(other[0:1, lanes] - peak)
        result.append(-(math.log2(wide) + peak + jnp.log2(total)))
    return result


def iteration_kernel(n_groups, log_noise, *refs):
    *refs, out_ref = refs
    wide = out_ref.shape[1]
    chips = [refs[i : i + 2] for i in range(0, 2 * n_groups, 2)]
    g = data_potentials(refs[2 * n_groups :], wide)
    potentials = [row_update(chip, g, log_noise) for chip in chips]
    for b in range(len(g)):
        scores = [f - rows_of(chip, b) for f, chip in zip(potentials, chips)]
        peak = functools.reduce(jnp.maximum, [jnp.max(s, axis=0, keepdims=True) for s in scores])
        total = functools.reduce(jnp.add, [jnp.sum(jnp.exp2(s - peak), axis=0, keepdims=True) for s in scores])
        out_ref[0:1, b * WIDTH : (b + 1) * WIDTH] = peak
        out_ref[1:2, b * WIDTH : (b + 1) * WIDTH] = total


def iteration(tiles, stats, log_noise):
    wide = tiles[0][0].shape[2]
    operands = [piece for group in tiles for piece in group] + list(stats)
    (own,) = kernel_call(
        functools.partial(iteration_kernel, len(tiles), log_noise),
        [((2, wide), jnp.float32)],
        [],
        16,
        *operands,
        flops=16 * sum(piece.size for piece in operands),
    )
    return own, swap_y(own)


def target_kernel(n_col, n_chip, log_noise, *refs):
    tiles, stats, latent_refs = refs[:4], refs[4:6], refs[6 : 6 + n_chip * n_col]
    refs = refs[6 + n_chip * n_col :]
    target_refs, refs = refs[:n_col], refs[n_col:]
    noise_pot_ref, data_pot_ref, pots, weights = refs
    _, col = place()
    height, wide = weights.shape
    g = data_potentials(stats, wide)
    f = row_update(tiles, g, log_noise)
    for b in range(len(g)):
        lanes = slice(b * WIDTH, (b + 1) * WIDTH)
        pots[:, lanes] = g[b] * (1.0 / TO_LOG2)
        scores = (f + g[b] - rows_of(tiles, b)) + log_noise
        weights[:, lanes] = jnp.exp2(scores).astype(jnp.bfloat16)
    data_pot_ref[...] = pots[:, block(col, wide // n_col)]
    own = height // 2
    share = own // n_col
    f = jnp.broadcast_to(f[:own], (own, WIDTH)).T[0:1, :] * (1.0 / TO_LOG2)
    for d in range(n_col):
        noise_pot_ref[pl.ds(col ^ d, 1), :] = f[:, d * share : (d + 1) * share]

    rows_of_one, part = latent_refs[0].shape
    for k in range(n_chip):
        product = jnp.zeros((height, part), jnp.float32)
        for d in range(n_col):
            product += jnp.dot(
                weights[:, block(col ^ d, rows_of_one)],
                latent_refs[k * n_col + d][...],
                preferred_element_type=jnp.float32,
            )
        product = product.astype(jnp.bfloat16)
        for d in range(n_col):
            target_refs[d][0, k] = product[d * share : (d + 1) * share]
            target_refs[d][1, k] = product[own + d * share : own + (d + 1) * share]


def make_targets(own_tiles, other_tiles, stats, latents, n_col, log_noise):
    n_chip = len(latents)
    _, share, wide = own_tiles[0].shape
    own = n_col * share
    part = latents[0][0].shape[1]
    return kernel_call(
        functools.partial(target_kernel, n_col, n_chip, log_noise),
        [((2, n_chip, share, part), jnp.bfloat16)] * n_col
        + [((n_col, share), jnp.float32), ((1, wide // n_col), jnp.float32)],
        [pltpu.VMEM((1, wide), jnp.float32), pltpu.VMEM((2 * own, wide), jnp.bfloat16)],
        24,
        *own_tiles,
        *other_tiles,
        *stats,
        *[piece for group in latents for piece in group],
        flops=4 * own * wide * n_chip * part,
    )


def join_kernel(n_col, *refs):
    *pieces, out_ref = refs
    row, col = place()
    _, n_chip, _, part = pieces[0].shape
    for i, piece in enumerate(pieces):
        other, d = i // n_col, n_col - 1 - i % n_col
        for k in range(n_chip):
            out_ref[:, block((row ^ other ^ (2 * k)) * n_col + (col ^ d), part)] = piece[other, k]


def join(pieces, n_col):
    _, n_chip, share, part = pieces[0].shape
    shape = (share, n_chip * part * len(pieces))
    (out,) = kernel_call(
        functools.partial(join_kernel, n_col), [(shape, pieces[0].dtype)], [], 12, *pieces
    )
    return out


def per_device_local(noise, data):
    n_col = lax.axis_size("col")
    own, own_data = noise.shape[0], data.shape[0]
    data_0, *dealt = deal(data, n_col)
    own_half, other_half = halve(noise)
    data_1, data_2 = swap(dealt[0], "col", 1), swap(dealt[1], "col", 2)
    x_0, y_0 = swap_x(data_0), swap_y(data_0)
    noise_0, *dealt_noise = deal_noise(own_half, after(swap_core(other_half), x_0, y_0), n_col)
    data_3 = swap(dealt[2], "col", 3)
    across_0 = swap_y(after(x_0, noise_0))
    x_1, y_1 = swap_x(after(data_1, noise_0)), swap_y(after(data_1, noise_0))
    noise_1 = swap(after(dealt_noise[0], data_2), "col", 1)
    across_1 = swap_x(y_1)
    x_2, y_2 = swap_x(after(data_2, x_1)), swap_y(after(data_2, y_1, across_0))
    noise_2 = swap(after(dealt_noise[1], data_2), "col", 2)
    across_2 = swap_y(x_2)
    x_3, y_3 = swap_x(after(data_3, across_1, x_2, noise_1)), swap_y(after(data_3, y_2, noise_1))
    noise_3 = swap(after(dealt_noise[2], data_3, noise_1), "col", 3)
    across_3 = swap_x(y_3)
    noise_pieces = [noise_0, noise_1, noise_2, noise_3]
    latents = [
        [data_0, data_1, data_2, data_3],
        [x_0, x_1, x_2, x_3],
        [y_0, y_1, y_2, y_3],
        [across_0, across_1, across_2, across_3],
    ]
    own_part, other_part = partial_cost(noise_pieces, latents)
    parts = col_exchange(core_sum(own_part, swap_core(other_part), n_col))
    tile = functools.reduce(jnp.add, parts[::-1])
    tile_3, tile_2, tile_1 = [swap(tile, "col", d) for d in (3, 2, 1)]
    near = jnp.stack([tile_1, tile])
    x_near = swap_x(near)
    far = jnp.stack([after(tile_3, x_near), tile_2])
    tiles = [[near, far], [x_near, swap_x(far)]]
    other_tiles = [swap_core(piece) for piece in tiles[0]]
    tiles += [other_tiles, [swap_core(piece) for piece in tiles[1]]]
    log_noise = math.log2(own * lax.axis_size("row"))
    stats = ()
    for _ in range(ITERS):
        stats = iteration(tiles, stats, log_noise)
    *products, noise_pot, data_pot = make_targets(tiles[0], other_tiles, stats, latents, n_col, log_noise)
    products = col_exchange(products)
    products = products[::-1]
    targets = join(products + [swap_core(piece) for piece in products], n_col)
    return (targets, noise_pot.reshape((own,)), data_pot.reshape((own_data,)))


def per_device(noise, data):
    n_row, n_col = lax.axis_size("row"), lax.axis_size("col")
    whole = 4 * noise.shape[0] * n_row * data.shape[0] * n_col
    if whole <= LOCAL_COST_BYTES and n_row == 8 and n_col == 4:
        return per_device_local(noise, data)
    return per_device_tiled(noise, data)


def solution(mesh):
    placed = (P("row", "col"), P("col", "row"))
    return jax.shard_map(
        per_device,
        mesh=mesh,
        in_specs=placed,
        out_specs=(P(("row", "col"), None), P("row"), P("col")),
        check_vma=False,
    )
```

```python
import functools
import math

import jax
import jax.numpy as jnp
from jax import lax
from jax.experimental import pallas as pl
from jax.experimental.pallas import tpu as pltpu
from jax.sharding import PartitionSpec as P

LATENT = 16384
ITERS = 3
EPSILON = 0.64 / math.sqrt(LATENT)
LOG2E = math.log2(math.e)
TO_LOG2 = LOG2E / EPSILON
CONTRACT = (((1,), (1,)), ((), ()))
LOCAL_COST_BYTES = 8 * 2**20


def noise_update(cost_tile, data_pot, epsilon, log_count):
    scores = (data_pot[None, :] - cost_tile) / epsilon
    local_peak = jnp.max(scores, axis=1)
    highest = lax.pmax(local_peak, "col")
    summed = lax.psum(jnp.sum(jnp.exp(scores - highest[:, None]), axis=1), "col")
    return -epsilon * (log_count + highest + jnp.log(summed))


def data_update(cost_tile, noise_pot, epsilon, log_count):
    scores = (noise_pot[:, None] - cost_tile) / epsilon
    local_peak = jnp.max(scores, axis=0)
    highest = lax.pmax(local_peak, "row")
    summed = lax.psum(jnp.sum(jnp.exp(scores - highest[None, :]), axis=0), "row")
    return -epsilon * (log_count + highest + jnp.log(summed))


def per_device_tiled(noise, data):
    epsilon = EPSILON
    noise_full = lax.all_gather(noise, "col", axis=1, tiled=True)
    noise_norm = jnp.sum(jnp.square(noise_full.astype(jnp.float32)), axis=1) / LATENT
    noise_rows = noise.shape[0]
    data_rows = data.shape[0]
    data_full = lax.all_gather(data, "row", axis=1, tiled=True)
    data_norm = jnp.sum(jnp.square(data_full.astype(jnp.float32)), axis=1) / LATENT
    cross = lax.dot_general(noise_full, data_full, CONTRACT, preferred_element_type=jnp.float32)
    cost_tile = noise_norm[:, None] + data_norm[None, :] - 2.0 / LATENT * cross
    log_noise = math.log(noise_rows * lax.axis_size("row"))
    log_data = math.log(data_rows * lax.axis_size("col"))
    data_pot = jnp.zeros((data_rows,), jnp.float32)
    for step in range(ITERS):
        noise_pot = noise_update(cost_tile, data_pot, epsilon, log_noise)
        data_pot = data_update(cost_tile, noise_pot, epsilon, log_data)
    noise_pot = noise_update(cost_tile, data_pot, epsilon, log_noise)
    weights = jnp.exp(
        (noise_pot[:, None] + data_pot[None, :] - cost_tile) / epsilon + log_noise
    ).astype(jnp.bfloat16)
    targets = lax.psum_scatter(
        jnp.dot(weights, data_full, preferred_element_type=jnp.float32).astype(jnp.bfloat16),
        "col",
        scatter_dimension=0,
        tiled=True,
    )
    return (targets, noise_pot, data_pot)


VMEM = pl.BlockSpec(memory_space=pltpu.VMEM)
WIDTH = 128


def place():
    return lax.axis_index("row"), lax.axis_index("col")


def swap(array, axis, step):
    count = lax.axis_size(axis)
    return lax.ppermute(array, axis, [(i, i ^ step) for i in range(count)])


def swap_core(array):
    return swap(array, "row", 1)


def swap_x(array):
    return swap(array, "row", 2)


def swap_y(array):
    return swap(array, "row", 4)


def after(array, *others):
    return lax.optimization_barrier((array,) + others)[0]


def col_exchange(pieces):
    count = len(pieces)
    moved = [swap(pieces[d], "col", d) for d in reversed(range(1, count))]
    return [pieces[0]] + moved[::-1]


def chip_gather(pieces):
    along_x, along_y, across = [], [], []
    for i, piece in enumerate(pieces):
        along_x.append(swap_x(piece))
        along_y.append(swap_y(piece))
        across.append(swap_x(along_y[i]) if i % 2 else swap_y(along_x[i]))
    return [pieces, along_x, along_y, across]


def block(index, size):
    return pl.ds(pl.multiple_of(index * size, size), size)


def kernel_call(kernel, outs, scratch, vmem, *operands, flops=0):
    moved = sum(a.size * a.dtype.itemsize for a in operands)
    return pl.pallas_call(
        kernel,
        in_specs=[VMEM] * len(operands),
        out_specs=[VMEM] * len(outs),
        out_shape=[jax.ShapeDtypeStruct(shape, dtype) for shape, dtype in outs],
        scratch_shapes=scratch,
        compiler_params=pltpu.CompilerParams(vmem_limit_bytes=vmem * 2**20),
        cost_estimate=pl.CostEstimate(flops=flops, bytes_accessed=moved, transcendentals=0),
    )(*operands)


def deal_kernel(n_col, data_ref, *outs):
    _, col = place()
    part = data_ref.shape[1] // n_col
    for d in range(n_col):
        outs[d][...] = data_ref[:, block(col ^ d, part)]


def deal(data, n_col):
    piece = (data.shape[0], data.shape[1] // n_col)
    return kernel_call(functools.partial(deal_kernel, n_col), [(piece, data.dtype)] * n_col, [], 8, data)


def halve_kernel(noise_ref, own_ref, other_ref):
    row, _ = place()
    core = lax.rem(row, 2)
    half = own_ref.shape[1]
    own_ref[...] = noise_ref[:, block(core, half)]
    other_ref[...] = noise_ref[:, block(1 - core, half)]


def halve(noise):
    half = (noise.shape[0], noise.shape[1] // 2)
    return kernel_call(halve_kernel, [(half, noise.dtype)] * 2, [], 8, noise)


def deal_noise_kernel(n_col, own_ref, other_ref, *outs):
    _, col = place()
    part = own_ref.shape[1] // n_col
    for d in range(n_col):
        outs[d][0] = own_ref[:, block(col ^ d, part)]
        outs[d][1] = other_ref[:, block(col ^ d, part)]


def deal_noise(own, other, n_col):
    shape = (2, own.shape[0], own.shape[1] // n_col)
    return kernel_call(
        functools.partial(deal_noise_kernel, n_col), [(shape, own.dtype)] * n_col, [], 8, own, other
    )


def cost_kernel(n_col, n_chip, *refs):
    noise_refs, latent_refs = refs[:n_col], refs[n_col : n_col + n_chip * n_col]
    own_ref, other_ref, noise_all = refs[n_col + n_chip * n_col :]
    row, col = place()
    _, own, part = noise_refs[0].shape
    height = latent_refs[0].shape[0]
    for d in range(n_col):
        noise_all[(row // 2) ^ col ^ d] = noise_refs[d][...].reshape(2 * own, part)
    noise_norm = jnp.zeros((2 * own, 1), jnp.float32)
    for k in range(n_chip):
        values = noise_all[k].astype(jnp.float32)
        noise_norm += jnp.sum(values * values, axis=1, keepdims=True)
    for d in range(n_col):
        cross = jnp.zeros((2 * own, height), jnp.float32)
        squares = jnp.zeros((height, part), jnp.float32)
        for k in range(n_chip):
            rows = latent_refs[k * n_col + d][...]
            cross += lax.dot_general(noise_all[k], rows, CONTRACT, preferred_element_type=jnp.float32)
            values = rows.astype(jnp.float32)
            squares += values * values
        norm = jnp.sum(squares, axis=1, keepdims=True)
        norm = jnp.broadcast_to(norm, (height, WIDTH)).T[0:1, :]
        cost = (noise_norm + norm - 2.0 * cross) * (TO_LOG2 / LATENT)
        lanes = block(col ^ d, height)
        own_ref[:, lanes] = cost[:own]
        other_ref[:, lanes] = cost[own:]


def partial_cost(noise_pieces, latents):
    n_chip, n_col = len(latents), len(noise_pieces)
    _, own, part = noise_pieces[0].shape
    width = n_col * latents[0][0].shape[0]
    return kernel_call(
        functools.partial(cost_kernel, n_col, n_chip),
        [((own, width), jnp.float32)] * 2,
        [pltpu.VMEM((n_chip, 2 * own, part), jnp.bfloat16)],
        24,
        *noise_pieces,
        *[piece for group in latents for piece in group],
        flops=4 * own * width * n_chip * part,
    )


def core_sum_kernel(n_col, own_ref, other_ref, *outs):
    _, col = place()
    share = own_ref.shape[0] // n_col
    for d in range(n_col):
        rows = block(col ^ d, share)
        outs[d][...] = own_ref[rows, :] + other_ref[rows, :]


def core_sum(own, other, n_col):
    shape = (own.shape[0] // n_col, own.shape[1])
    return kernel_call(
        functools.partial(core_sum_kernel, n_col), [(shape, own.dtype)] * n_col, [], 8, own, other
    )


def rows_of(refs, b):
    lanes = slice(b * WIDTH, (b + 1) * WIDTH)
    parts = []
    for ref in refs:
        if len(ref.shape) == 2:
            parts.append(ref[:, lanes])
        else:
            parts += [ref[i, :, lanes] for i in reversed(range(ref.shape[0]))]
    return jnp.concatenate(parts)


def row_update(refs, g, log_noise):
    blocks = range(len(g))
    peak = functools.reduce(jnp.maximum, [g[b] - rows_of(refs, b) for b in blocks])
    peak = jnp.max(peak, axis=1, keepdims=True)
    total = functools.reduce(jnp.add, [jnp.exp2(g[b] - rows_of(refs, b) - peak) for b in blocks])
    total = jnp.sum(total, axis=1, keepdims=True)
    return -(log_noise + peak + jnp.log2(total))


def data_potentials(stats, wide):
    if not stats:
        return [jnp.zeros((1, WIDTH), jnp.float32)] * (wide // WIDTH)
    own, other = stats
    result = []
    for first in range(0, wide, WIDTH):
        lanes = slice(first, first + WIDTH)
        peak = jnp.maximum(own[0:1, lanes], other[0:1, lanes])
        total = own[1:2, lanes] * jnp.exp2(own[0:1, lanes] - peak)
        total += other[1:2, lanes] * jnp.exp2(other[0:1, lanes] - peak)
        result.append(-(math.log2(wide) + peak + jnp.log2(total)))
    return result


def iteration_kernel(n_groups, log_noise, *refs):
    *refs, out_ref = refs
    wide = out_ref.shape[1]
    chips = [refs[i : i + 2] for i in range(0, 2 * n_groups, 2)]
    g = data_potentials(refs[2 * n_groups :], wide)
    potentials = [row_update(chip, g, log_noise) for chip in chips]
    for b in range(len(g)):
        scores = [f - rows_of(chip, b) for f, chip in zip(potentials, chips)]
        peak = functools.reduce(jnp.maximum, [jnp.max(s, axis=0, keepdims=True) for s in scores])
        total = functools.reduce(jnp.add, [jnp.sum(jnp.exp2(s - peak), axis=0, keepdims=True) for s in scores])
        out_ref[0:1, b * WIDTH : (b + 1) * WIDTH] = peak
        out_ref[1:2, b * WIDTH : (b + 1) * WIDTH] = total


def iteration(tiles, stats, log_noise):
    wide = tiles[0][0].shape[1]
    operands = [piece for group in tiles for piece in group] + list(stats)
    (own,) = kernel_call(
        functools.partial(iteration_kernel, len(tiles), log_noise),
        [((2, wide), jnp.float32)],
        [],
        16,
        *operands,
        flops=16 * sum(piece.size for piece in operands),
    )
    return own, swap_y(own)


def target_kernel(n_col, n_chip, log_noise, *refs):
    tiles, stats, latent_refs = refs[:4], refs[4:6], refs[6 : 6 + n_chip * n_col]
    refs = refs[6 + n_chip * n_col :]
    target_refs, refs = refs[:n_col], refs[n_col:]
    noise_pot_ref, data_pot_ref, pots, weights = refs
    _, col = place()
    height, wide = weights.shape
    g = data_potentials(stats, wide)
    f = row_update(tiles, g, log_noise)
    for b in range(len(g)):
        lanes = slice(b * WIDTH, (b + 1) * WIDTH)
        pots[:, lanes] = g[b] * (1.0 / TO_LOG2)
        scores = (f + g[b] - rows_of(tiles, b)) + log_noise
        weights[:, lanes] = jnp.exp2(scores).astype(jnp.bfloat16)
    data_pot_ref[...] = pots[:, block(col, wide // n_col)]
    own = height // 2
    share = own // n_col
    f = jnp.broadcast_to(f[:own], (own, WIDTH)).T[0:1, :] * (1.0 / TO_LOG2)
    for d in range(n_col):
        noise_pot_ref[pl.ds(col ^ d, 1), :] = f[:, d * share : (d + 1) * share]

    rows_of_one, part = latent_refs[0].shape
    for k in range(n_chip):
        product = jnp.zeros((height, part), jnp.float32)
        for d in range(n_col):
            product += jnp.dot(
                weights[:, block(col ^ d, rows_of_one)],
                latent_refs[k * n_col + d][...],
                preferred_element_type=jnp.float32,
            )
        product = product.astype(jnp.bfloat16)
        for d in range(n_col):
            target_refs[d][0, k] = product[d * share : (d + 1) * share]
            target_refs[d][1, k] = product[own + d * share : own + (d + 1) * share]


def make_targets(own_tiles, other_tiles, stats, latents, n_col, log_noise):
    n_chip = len(latents)
    share, wide = own_tiles[0].shape
    own = n_col * share
    part = latents[0][0].shape[1]
    return kernel_call(
        functools.partial(target_kernel, n_col, n_chip, log_noise),
        [((2, n_chip, share, part), jnp.bfloat16)] * n_col
        + [((n_col, share), jnp.float32), ((1, wide // n_col), jnp.float32)],
        [pltpu.VMEM((1, wide), jnp.float32), pltpu.VMEM((2 * own, wide), jnp.bfloat16)],
        24,
        *own_tiles,
        *other_tiles,
        *stats,
        *[piece for group in latents for piece in group],
        flops=4 * own * wide * n_chip * part,
    )


def join_kernel(n_col, *refs):
    *pieces, out_ref = refs
    row, col = place()
    _, n_chip, _, part = pieces[0].shape
    for i, piece in enumerate(pieces):
        other, d = i // n_col, n_col - 1 - i % n_col
        for k in range(n_chip):
            out_ref[:, block((row ^ other ^ (2 * k)) * n_col + (col ^ d), part)] = piece[other, k]


def join(pieces, n_col):
    _, n_chip, share, part = pieces[0].shape
    shape = (share, n_chip * part * len(pieces))
    (out,) = kernel_call(
        functools.partial(join_kernel, n_col), [(shape, pieces[0].dtype)], [], 12, *pieces
    )
    return out


def per_device_local(noise, data):
    n_col = lax.axis_size("col")
    own, own_data = noise.shape[0], data.shape[0]
    data_0, *dealt = deal(data, n_col)
    own_half, other_half = halve(noise)
    data_1, data_2 = swap(dealt[0], "col", 1), swap(dealt[1], "col", 2)
    x_0, y_0 = swap_x(data_0), swap_y(data_0)
    noise_0, *dealt_noise = deal_noise(own_half, after(swap_core(other_half), x_0, y_0), n_col)
    data_3 = swap(dealt[2], "col", 3)
    across_0 = swap_y(after(x_0, noise_0))
    x_1, y_1 = swap_x(after(data_1, noise_0)), swap_y(after(data_1, noise_0))
    noise_1 = swap(after(dealt_noise[0], data_2), "col", 1)
    across_1 = swap_x(y_1)
    x_2, y_2 = swap_x(after(data_2, x_1)), swap_y(after(data_2, y_1, across_0))
    noise_2 = swap(after(dealt_noise[1], data_2), "col", 2)
    across_2 = swap_y(x_2)
    x_3, y_3 = swap_x(after(data_3, across_1, x_2, noise_1)), swap_y(after(data_3, y_2, noise_1))
    noise_3 = swap(after(dealt_noise[2], data_3, noise_1), "col", 3)
    across_3 = swap_x(y_3)
    noise_pieces = [noise_0, noise_1, noise_2, noise_3]
    latents = [
        [data_0, data_1, data_2, data_3],
        [x_0, x_1, x_2, x_3],
        [y_0, y_1, y_2, y_3],
        [across_0, across_1, across_2, across_3],
    ]
    own_part, other_part = partial_cost(noise_pieces, latents)
    parts = col_exchange(core_sum(own_part, swap_core(other_part), n_col))
    tile = functools.reduce(jnp.add, parts[::-1])
    tile_3, tile_2, tile_1 = [swap(tile, "col", d) for d in (3, 2, 1)]
    x_tile = swap_x(tile)
    others = jnp.stack([after(tile_3, x_tile), tile_2, tile_1])
    tiles = [[tile, others], [x_tile, swap_x(others)]]
    other_tiles = [swap_core(piece) for piece in tiles[0]]
    tiles += [other_tiles, [swap_core(piece) for piece in tiles[1]]]
    log_noise = math.log2(own * lax.axis_size("row"))
    stats = ()
    for _ in range(ITERS):
        stats = iteration(tiles, stats, log_noise)
    *products, noise_pot, data_pot = make_targets(tiles[0], other_tiles, stats, latents, n_col, log_noise)
    products = col_exchange(products)
    products = products[::-1]
    targets = join(products + [swap_core(piece) for piece in products], n_col)
    return (targets, noise_pot.reshape((own,)), data_pot.reshape((own_data,)))


def per_device(noise, data):
    n_row, n_col = lax.axis_size("row"), lax.axis_size("col")
    whole = 4 * noise.shape[0] * n_row * data.shape[0] * n_col
    if whole <= LOCAL_COST_BYTES and n_row == 8 and n_col == 4:
        return per_device_local(noise, data)
    return per_device_tiled(noise, data)


def solution(mesh):
    placed = (P("row", "col"), P("col", "row"))
    return jax.shard_map(
        per_device,
        mesh=mesh,
        in_specs=placed,
        out_specs=(P(("row", "col"), None), P("row"), P("col")),
        check_vma=False,
    )
```

```python
import functools
import math

import jax
import jax.numpy as jnp
from jax import lax
from jax.experimental import pallas as pl
from jax.experimental.pallas import tpu as pltpu
from jax.sharding import PartitionSpec as P

LATENT = 16384
ITERS = 3
EPSILON = 0.64 / math.sqrt(LATENT)
LOG2E = math.log2(math.e)
TO_LOG2 = LOG2E / EPSILON
CONTRACT = (((1,), (1,)), ((), ()))
LOCAL_COST_BYTES = 8 * 2**20


def noise_update(cost_tile, data_pot, epsilon, log_count):
    scores = (data_pot[None, :] - cost_tile) / epsilon
    local_peak = jnp.max(scores, axis=1)
    highest = lax.pmax(local_peak, "col")
    summed = lax.psum(jnp.sum(jnp.exp(scores - highest[:, None]), axis=1), "col")
    return -epsilon * (log_count + highest + jnp.log(summed))


def data_update(cost_tile, noise_pot, epsilon, log_count):
    scores = (noise_pot[:, None] - cost_tile) / epsilon
    local_peak = jnp.max(scores, axis=0)
    highest = lax.pmax(local_peak, "row")
    summed = lax.psum(jnp.sum(jnp.exp(scores - highest[None, :]), axis=0), "row")
    return -epsilon * (log_count + highest + jnp.log(summed))


def per_device_tiled(noise, data):
    epsilon = EPSILON
    noise_full = lax.all_gather(noise, "col", axis=1, tiled=True)
    noise_norm = jnp.sum(jnp.square(noise_full.astype(jnp.float32)), axis=1) / LATENT
    noise_rows = noise.shape[0]
    data_rows = data.shape[0]
    data_full = lax.all_gather(data, "row", axis=1, tiled=True)
    data_norm = jnp.sum(jnp.square(data_full.astype(jnp.float32)), axis=1) / LATENT
    cross = lax.dot_general(noise_full, data_full, CONTRACT, preferred_element_type=jnp.float32)
    cost_tile = noise_norm[:, None] + data_norm[None, :] - 2.0 / LATENT * cross
    log_noise = math.log(noise_rows * lax.axis_size("row"))
    log_data = math.log(data_rows * lax.axis_size("col"))
    data_pot = jnp.zeros((data_rows,), jnp.float32)
    for step in range(ITERS):
        noise_pot = noise_update(cost_tile, data_pot, epsilon, log_noise)
        data_pot = data_update(cost_tile, noise_pot, epsilon, log_data)
    noise_pot = noise_update(cost_tile, data_pot, epsilon, log_noise)
    weights = jnp.exp(
        (noise_pot[:, None] + data_pot[None, :] - cost_tile) / epsilon + log_noise
    ).astype(jnp.bfloat16)
    targets = lax.psum_scatter(
        jnp.dot(weights, data_full, preferred_element_type=jnp.float32).astype(jnp.bfloat16),
        "col",
        scatter_dimension=0,
        tiled=True,
    )
    return (targets, noise_pot, data_pot)


VMEM = pl.BlockSpec(memory_space=pltpu.VMEM)
WIDTH = 128


def place():
    return lax.axis_index("row"), lax.axis_index("col")


def swap(array, axis, step):
    count = lax.axis_size(axis)
    return lax.ppermute(array, axis, [(i, i ^ step) for i in range(count)])


def swap_core(array):
    return swap(array, "row", 1)


def swap_x(array):
    return swap(array, "row", 2)


def swap_y(array):
    return swap(array, "row", 4)


def after(array, *others):
    return lax.optimization_barrier((array,) + others)[0]


def col_exchange(pieces):
    count = len(pieces)
    moved = [swap(pieces[d], "col", d) for d in reversed(range(1, count))]
    return [pieces[0]] + moved[::-1]


def chip_gather(pieces):
    along_x, along_y, across = [], [], []
    for i, piece in enumerate(pieces):
        along_x.append(swap_x(piece))
        along_y.append(swap_y(piece))
        across.append(swap_x(along_y[i]) if i % 2 else swap_y(along_x[i]))
    return [pieces, along_x, along_y, across]


def block(index, size):
    return pl.ds(pl.multiple_of(index * size, size), size)


def kernel_call(kernel, outs, scratch, vmem, *operands, flops=0):
    moved = sum(a.size * a.dtype.itemsize for a in operands)
    return pl.pallas_call(
        kernel,
        in_specs=[VMEM] * len(operands),
        out_specs=[VMEM] * len(outs),
        out_shape=[jax.ShapeDtypeStruct(shape, dtype) for shape, dtype in outs],
        scratch_shapes=scratch,
        compiler_params=pltpu.CompilerParams(vmem_limit_bytes=vmem * 2**20),
        cost_estimate=pl.CostEstimate(flops=flops, bytes_accessed=moved, transcendentals=0),
    )(*operands)


def deal_kernel(n_col, data_ref, *outs):
    _, col = place()
    part = data_ref.shape[1] // n_col
    for d in range(n_col):
        outs[d][...] = data_ref[:, block(col ^ d, part)]


def deal(data, n_col):
    piece = (data.shape[0], data.shape[1] // n_col)
    return kernel_call(functools.partial(deal_kernel, n_col), [(piece, data.dtype)] * n_col, [], 8, data)


def halve_kernel(noise_ref, own_ref, other_ref):
    row, _ = place()
    core = lax.rem(row, 2)
    half = own_ref.shape[1]
    own_ref[...] = noise_ref[:, block(core, half)]
    other_ref[...] = noise_ref[:, block(1 - core, half)]


def halve(noise):
    half = (noise.shape[0], noise.shape[1] // 2)
    return kernel_call(halve_kernel, [(half, noise.dtype)] * 2, [], 8, noise)


def deal_noise_kernel(n_col, own_ref, other_ref, *outs):
    _, col = place()
    part = own_ref.shape[1] // n_col
    for d in range(n_col):
        outs[d][0] = own_ref[:, block(col ^ d, part)]
        outs[d][1] = other_ref[:, block(col ^ d, part)]


def deal_noise(own, other, n_col):
    shape = (2, own.shape[0], own.shape[1] // n_col)
    return kernel_call(
        functools.partial(deal_noise_kernel, n_col), [(shape, own.dtype)] * n_col, [], 8, own, other
    )


def cost_kernel(n_col, n_chip, *refs):
    noise_refs, latent_refs = refs[:n_col], refs[n_col : n_col + n_chip * n_col]
    own_ref, other_ref, noise_all = refs[n_col + n_chip * n_col :]
    row, col = place()
    _, own, part = noise_refs[0].shape
    height = latent_refs[0].shape[0]
    for d in range(n_col):
        noise_all[(row // 2) ^ col ^ d] = noise_refs[d][...].reshape(2 * own, part)
    noise_norm = jnp.zeros((2 * own, 1), jnp.float32)
    for k in range(n_chip):
        values = noise_all[k].astype(jnp.float32)
        noise_norm += jnp.sum(values * values, axis=1, keepdims=True)
    for d in range(n_col):
        cross = jnp.zeros((2 * own, height), jnp.float32)
        squares = jnp.zeros((height, part), jnp.float32)
        for k in range(n_chip):
            rows = latent_refs[k * n_col + d][...]
            cross += lax.dot_general(noise_all[k], rows, CONTRACT, preferred_element_type=jnp.float32)
            values = rows.astype(jnp.float32)
            squares += values * values
        norm = jnp.sum(squares, axis=1, keepdims=True)
        norm = jnp.broadcast_to(norm, (height, WIDTH)).T[0:1, :]
        cost = (noise_norm + norm - 2.0 * cross) * (TO_LOG2 / LATENT)
        lanes = block(col ^ d, height)
        own_ref[:, lanes] = cost[:own]
        other_ref[:, lanes] = cost[own:]


def partial_cost(noise_pieces, latents):
    n_chip, n_col = len(latents), len(noise_pieces)
    _, own, part = noise_pieces[0].shape
    width = n_col * latents[0][0].shape[0]
    return kernel_call(
        functools.partial(cost_kernel, n_col, n_chip),
        [((own, width), jnp.float32)] * 2,
        [pltpu.VMEM((n_chip, 2 * own, part), jnp.bfloat16)],
        24,
        *noise_pieces,
        *[piece for group in latents for piece in group],
        flops=4 * own * width * n_chip * part,
    )


def core_sum_kernel(n_col, own_ref, other_ref, *outs):
    _, col = place()
    share = own_ref.shape[0] // n_col
    for d in range(n_col):
        rows = block(col ^ d, share)
        outs[d][...] = own_ref[rows, :] + other_ref[rows, :]


def core_sum(own, other, n_col):
    shape = (own.shape[0] // n_col, own.shape[1])
    return kernel_call(
        functools.partial(core_sum_kernel, n_col), [(shape, own.dtype)] * n_col, [], 8, own, other
    )


def rows_of(refs, b):
    lanes = slice(b * WIDTH, (b + 1) * WIDTH)
    parts = []
    for ref in refs:
        if len(ref.shape) == 2:
            parts.append(ref[:, lanes])
        else:
            parts += [ref[i, :, lanes] for i in reversed(range(ref.shape[0]))]
    return jnp.concatenate(parts)


def row_update(refs, g, log_noise):
    blocks = range(len(g))
    peak = functools.reduce(jnp.maximum, [g[b] - rows_of(refs, b) for b in blocks])
    peak = jnp.max(peak, axis=1, keepdims=True)
    total = functools.reduce(jnp.add, [jnp.exp2(g[b] - rows_of(refs, b) - peak) for b in blocks])
    total = jnp.sum(total, axis=1, keepdims=True)
    return -(log_noise + peak + jnp.log2(total))


def data_potentials(stats, wide):
    if not stats:
        return [jnp.zeros((1, WIDTH), jnp.float32)] * (wide // WIDTH)
    own, other = stats
    result = []
    for first in range(0, wide, WIDTH):
        lanes = slice(first, first + WIDTH)
        peak = jnp.maximum(own[0:1, lanes], other[0:1, lanes])
        total = own[1:2, lanes] * jnp.exp2(own[0:1, lanes] - peak)
        total += other[1:2, lanes] * jnp.exp2(other[0:1, lanes] - peak)
        result.append(-(math.log2(wide) + peak + jnp.log2(total)))
    return result


def iteration_kernel(n_groups, log_noise, *refs):
    *refs, out_ref = refs
    wide = out_ref.shape[1]
    chips = [refs[i : i + 3] for i in range(0, 3 * n_groups, 3)]
    g = data_potentials(refs[3 * n_groups :], wide)
    potentials = [row_update(chip, g, log_noise) for chip in chips]
    for b in range(len(g)):
        scores = [f - rows_of(chip, b) for f, chip in zip(potentials, chips)]
        peak = functools.reduce(jnp.maximum, [jnp.max(s, axis=0, keepdims=True) for s in scores])
        total = functools.reduce(jnp.add, [jnp.sum(jnp.exp2(s - peak), axis=0, keepdims=True) for s in scores])
        out_ref[0:1, b * WIDTH : (b + 1) * WIDTH] = peak
        out_ref[1:2, b * WIDTH : (b + 1) * WIDTH] = total


def iteration(tiles, stats, log_noise):
    wide = tiles[0][0].shape[1]
    operands = [piece for group in tiles for piece in group] + list(stats)
    (own,) = kernel_call(
        functools.partial(iteration_kernel, len(tiles), log_noise),
        [((2, wide), jnp.float32)],
        [],
        16,
        *operands,
        flops=16 * sum(piece.size for piece in operands),
    )
    return own, swap_y(own)


def target_kernel(n_col, n_chip, log_noise, *refs):
    tiles, stats, latent_refs = refs[:6], refs[6:8], refs[8 : 8 + n_chip * n_col]
    refs = refs[8 + n_chip * n_col :]
    target_refs, refs = refs[:n_col], refs[n_col:]
    noise_pot_ref, data_pot_ref, pots, weights = refs
    _, col = place()
    height, wide = weights.shape
    g = data_potentials(stats, wide)
    f = row_update(tiles, g, log_noise)
    for b in range(len(g)):
        lanes = slice(b * WIDTH, (b + 1) * WIDTH)
        pots[:, lanes] = g[b] * (1.0 / TO_LOG2)
        scores = (f + g[b] - rows_of(tiles, b)) + log_noise
        weights[:, lanes] = jnp.exp2(scores).astype(jnp.bfloat16)
    data_pot_ref[...] = pots[:, block(col, wide // n_col)]
    own = height // 2
    share = own // n_col
    f = jnp.broadcast_to(f[:own], (own, WIDTH)).T[0:1, :] * (1.0 / TO_LOG2)
    for d in range(n_col):
        noise_pot_ref[pl.ds(col ^ d, 1), :] = f[:, d * share : (d + 1) * share]

    rows_of_one, part = latent_refs[0].shape
    for k in range(n_chip):
        product = jnp.zeros((height, part), jnp.float32)
        for d in range(n_col):
            product += jnp.dot(
                weights[:, block(col ^ d, rows_of_one)],
                latent_refs[k * n_col + d][...],
                preferred_element_type=jnp.float32,
            )
        product = product.astype(jnp.bfloat16)
        for d in range(n_col):
            target_refs[d][0, k] = product[d * share : (d + 1) * share]
            target_refs[d][1, k] = product[own + d * share : own + (d + 1) * share]


def make_targets(own_tiles, other_tiles, stats, latents, n_col, log_noise):
    n_chip = len(latents)
    share, wide = own_tiles[0].shape
    own = n_col * share
    part = latents[0][0].shape[1]
    return kernel_call(
        functools.partial(target_kernel, n_col, n_chip, log_noise),
        [((2, n_chip, share, part), jnp.bfloat16)] * n_col
        + [((n_col, share), jnp.float32), ((1, wide // n_col), jnp.float32)],
        [pltpu.VMEM((1, wide), jnp.float32), pltpu.VMEM((2 * own, wide), jnp.bfloat16)],
        24,
        *own_tiles,
        *other_tiles,
        *stats,
        *[piece for group in latents for piece in group],
        flops=4 * own * wide * n_chip * part,
    )


def join_kernel(n_col, *refs):
    *pieces, out_ref = refs
    row, col = place()
    _, n_chip, _, part = pieces[0].shape
    for i, piece in enumerate(pieces):
        other, d = i // n_col, n_col - 1 - i % n_col
        for k in range(n_chip):
            out_ref[:, block((row ^ other ^ (2 * k)) * n_col + (col ^ d), part)] = piece[other, k]


def join(pieces, n_col):
    _, n_chip, share, part = pieces[0].shape
    shape = (share, n_chip * part * len(pieces))
    (out,) = kernel_call(
        functools.partial(join_kernel, n_col), [(shape, pieces[0].dtype)], [], 12, *pieces
    )
    return out


def per_device_local(noise, data):
    n_col = lax.axis_size("col")
    own, own_data = noise.shape[0], data.shape[0]
    data_0, *dealt = deal(data, n_col)
    own_half, other_half = halve(noise)
    data_1, data_2 = swap(dealt[0], "col", 1), swap(dealt[1], "col", 2)
    x_0, y_0 = swap_x(data_0), swap_y(data_0)
    noise_0, *dealt_noise = deal_noise(own_half, after(swap_core(other_half), x_0, y_0), n_col)
    data_3 = swap(dealt[2], "col", 3)
    across_0 = swap_y(after(x_0, noise_0))
    x_1, y_1 = swap_x(after(data_1, noise_0)), swap_y(after(data_1, noise_0))
    noise_1 = swap(after(dealt_noise[0], data_2), "col", 1)
    across_1 = swap_x(y_1)
    x_2, y_2 = swap_x(after(data_2, x_1)), swap_y(after(data_2, y_1, across_0))
    noise_2 = swap(after(dealt_noise[1], data_2), "col", 2)
    across_2 = swap_y(x_2)
    x_3, y_3 = swap_x(after(data_3, across_1, x_2, noise_1)), swap_y(after(data_3, y_2, noise_1))
    noise_3 = swap(after(dealt_noise[2], data_3, noise_1), "col", 3)
    across_3 = swap_x(y_3)
    noise_pieces = [noise_0, noise_1, noise_2, noise_3]
    latents = [
        [data_0, data_1, data_2, data_3],
        [x_0, x_1, x_2, x_3],
        [y_0, y_1, y_2, y_3],
        [across_0, across_1, across_2, across_3],
    ]
    own_part, other_part = partial_cost(noise_pieces, latents)
    parts = col_exchange(core_sum(own_part, swap_core(other_part), n_col))
    tile = functools.reduce(jnp.add, parts[::-1])
    tile_2, tile_1 = swap(tile, "col", 2), swap(tile, "col", 1)
    tile_3 = swap(tile_2, "col", 1)
    x_tile = swap_x(tile)
    pair = after(jnp.stack([tile_2, tile_1]), x_tile)
    tiles = [[tile, pair, tile_3], [x_tile, swap_x(pair), swap_x(tile_3)]]
    other_tiles = [swap_core(piece) for piece in tiles[0]]
    tiles += [other_tiles, [swap_core(piece) for piece in tiles[1]]]
    log_noise = math.log2(own * lax.axis_size("row"))
    stats = ()
    for _ in range(ITERS):
        stats = iteration(tiles, stats, log_noise)
    *products, noise_pot, data_pot = make_targets(tiles[0], other_tiles, stats, latents, n_col, log_noise)
    products = col_exchange(products)
    products = products[::-1]
    targets = join(products + [swap_core(piece) for piece in products], n_col)
    return (targets, noise_pot.reshape((own,)), data_pot.reshape((own_data,)))


def per_device(noise, data):
    n_row, n_col = lax.axis_size("row"), lax.axis_size("col")
    whole = 4 * noise.shape[0] * n_row * data.shape[0] * n_col
    if whole <= LOCAL_COST_BYTES and n_row == 8 and n_col == 4:
        return per_device_local(noise, data)
    return per_device_tiled(noise, data)


def solution(mesh):
    placed = (P("row", "col"), P("col", "row"))
    return jax.shard_map(
        per_device,
        mesh=mesh,
        in_specs=placed,
        out_specs=(P(("row", "col"), None), P("row"), P("col")),
        check_vma=False,
    )
```

```python
import functools
import math

import jax
import jax.numpy as jnp
from jax import lax
from jax.experimental import pallas as pl
from jax.experimental.pallas import tpu as pltpu
from jax.sharding import PartitionSpec as P

LATENT = 16384
ITERS = 3
EPSILON = 0.64 / math.sqrt(LATENT)
LOG2E = math.log2(math.e)
TO_LOG2 = LOG2E / EPSILON
CONTRACT = (((1,), (1,)), ((), ()))
LOCAL_COST_BYTES = 8 * 2**20


def noise_update(cost_tile, data_pot, epsilon, log_count):
    scores = (data_pot[None, :] - cost_tile) / epsilon
    local_peak = jnp.max(scores, axis=1)
    highest = lax.pmax(local_peak, "col")
    summed = lax.psum(jnp.sum(jnp.exp(scores - highest[:, None]), axis=1), "col")
    return -epsilon * (log_count + highest + jnp.log(summed))


def data_update(cost_tile, noise_pot, epsilon, log_count):
    scores = (noise_pot[:, None] - cost_tile) / epsilon
    local_peak = jnp.max(scores, axis=0)
    highest = lax.pmax(local_peak, "row")
    summed = lax.psum(jnp.sum(jnp.exp(scores - highest[None, :]), axis=0), "row")
    return -epsilon * (log_count + highest + jnp.log(summed))


def per_device_tiled(noise, data):
    epsilon = EPSILON
    noise_full = lax.all_gather(noise, "col", axis=1, tiled=True)
    noise_norm = jnp.sum(jnp.square(noise_full.astype(jnp.float32)), axis=1) / LATENT
    noise_rows = noise.shape[0]
    data_rows = data.shape[0]
    data_full = lax.all_gather(data, "row", axis=1, tiled=True)
    data_norm = jnp.sum(jnp.square(data_full.astype(jnp.float32)), axis=1) / LATENT
    cross = lax.dot_general(noise_full, data_full, CONTRACT, preferred_element_type=jnp.float32)
    cost_tile = noise_norm[:, None] + data_norm[None, :] - 2.0 / LATENT * cross
    log_noise = math.log(noise_rows * lax.axis_size("row"))
    log_data = math.log(data_rows * lax.axis_size("col"))
    data_pot = jnp.zeros((data_rows,), jnp.float32)
    for step in range(ITERS):
        noise_pot = noise_update(cost_tile, data_pot, epsilon, log_noise)
        data_pot = data_update(cost_tile, noise_pot, epsilon, log_data)
    noise_pot = noise_update(cost_tile, data_pot, epsilon, log_noise)
    weights = jnp.exp(
        (noise_pot[:, None] + data_pot[None, :] - cost_tile) / epsilon + log_noise
    ).astype(jnp.bfloat16)
    targets = lax.psum_scatter(
        jnp.dot(weights, data_full, preferred_element_type=jnp.float32).astype(jnp.bfloat16),
        "col",
        scatter_dimension=0,
        tiled=True,
    )
    return (targets, noise_pot, data_pot)


VMEM = pl.BlockSpec(memory_space=pltpu.VMEM)
WIDTH = 128


def place():
    return lax.axis_index("row"), lax.axis_index("col")


def swap(array, axis, step):
    count = lax.axis_size(axis)
    return lax.ppermute(array, axis, [(i, i ^ step) for i in range(count)])


def swap_core(array):
    return swap(array, "row", 1)


def swap_x(array):
    return swap(array, "row", 2)


def swap_y(array):
    return swap(array, "row", 4)


def after(array, *others):
    return lax.optimization_barrier((array,) + others)[0]


def col_exchange(pieces):
    count = len(pieces)
    moved = [swap(pieces[d], "col", d) for d in reversed(range(1, count))]
    return [pieces[0]] + moved[::-1]


def chip_gather(pieces):
    along_x, along_y, across = [], [], []
    for i, piece in enumerate(pieces):
        along_x.append(swap_x(piece))
        along_y.append(swap_y(piece))
        across.append(swap_x(along_y[i]) if i % 2 else swap_y(along_x[i]))
    return [pieces, along_x, along_y, across]


def block(index, size):
    return pl.ds(pl.multiple_of(index * size, size), size)


def kernel_call(kernel, outs, scratch, vmem, *operands, flops=0):
    moved = sum(a.size * a.dtype.itemsize for a in operands)
    return pl.pallas_call(
        kernel,
        in_specs=[VMEM] * len(operands),
        out_specs=[VMEM] * len(outs),
        out_shape=[jax.ShapeDtypeStruct(shape, dtype) for shape, dtype in outs],
        scratch_shapes=scratch,
        compiler_params=pltpu.CompilerParams(vmem_limit_bytes=vmem * 2**20),
        cost_estimate=pl.CostEstimate(flops=flops, bytes_accessed=moved, transcendentals=0),
    )(*operands)


def deal_kernel(n_col, data_ref, *outs):
    _, col = place()
    part = data_ref.shape[1] // n_col
    for d in range(n_col):
        outs[d][...] = data_ref[:, block(col ^ d, part)]


def deal(data, n_col):
    piece = (data.shape[0], data.shape[1] // n_col)
    return kernel_call(functools.partial(deal_kernel, n_col), [(piece, data.dtype)] * n_col, [], 8, data)


def halve_kernel(noise_ref, own_ref, other_ref):
    row, _ = place()
    core = lax.rem(row, 2)
    half = own_ref.shape[1]
    own_ref[...] = noise_ref[:, block(core, half)]
    other_ref[...] = noise_ref[:, block(1 - core, half)]


def halve(noise):
    half = (noise.shape[0], noise.shape[1] // 2)
    return kernel_call(halve_kernel, [(half, noise.dtype)] * 2, [], 8, noise)


def deal_noise_kernel(n_col, own_ref, other_ref, *outs):
    _, col = place()
    part = own_ref.shape[1] // n_col
    for d in range(n_col):
        outs[d][0] = own_ref[:, block(col ^ d, part)]
        outs[d][1] = other_ref[:, block(col ^ d, part)]


def deal_noise(own, other, n_col):
    shape = (2, own.shape[0], own.shape[1] // n_col)
    return kernel_call(
        functools.partial(deal_noise_kernel, n_col), [(shape, own.dtype)] * n_col, [], 8, own, other
    )


def cost_kernel(n_col, n_chip, *refs):
    noise_refs, latent_refs = refs[:n_col], refs[n_col : n_col + n_chip * n_col]
    own_ref, other_ref, noise_all = refs[n_col + n_chip * n_col :]
    row, col = place()
    _, own, part = noise_refs[0].shape
    height = latent_refs[0].shape[0]
    for d in range(n_col):
        noise_all[(row // 2) ^ col ^ d] = noise_refs[-d % n_col][...].reshape(2 * own, part)
    noise_norm = jnp.zeros((2 * own, 1), jnp.float32)
    for k in range(n_chip):
        values = noise_all[k].astype(jnp.float32)
        noise_norm += jnp.sum(values * values, axis=1, keepdims=True)
    for d in range(n_col):
        cross = jnp.zeros((2 * own, height), jnp.float32)
        squares = jnp.zeros((height, part), jnp.float32)
        for k in range(n_chip):
            rows = latent_refs[k * n_col + d][...]
            cross += lax.dot_general(noise_all[k], rows, CONTRACT, preferred_element_type=jnp.float32)
            values = rows.astype(jnp.float32)
            squares += values * values
        norm = jnp.sum(squares, axis=1, keepdims=True)
        norm = jnp.broadcast_to(norm, (height, WIDTH)).T[0:1, :]
        cost = (noise_norm + norm - 2.0 * cross) * (TO_LOG2 / LATENT)
        lanes = block(col ^ d, height)
        own_ref[:, lanes] = cost[:own]
        other_ref[:, lanes] = cost[own:]


def partial_cost(noise_pieces, latents):
    n_chip, n_col = len(latents), len(noise_pieces)
    _, own, part = noise_pieces[0].shape
    width = n_col * latents[0][0].shape[0]
    return kernel_call(
        functools.partial(cost_kernel, n_col, n_chip),
        [((own, width), jnp.float32)] * 2,
        [pltpu.VMEM((n_chip, 2 * own, part), jnp.bfloat16)],
        24,
        *[noise_pieces[-i] for i in range(n_col)],
        *[piece for group in latents for piece in group],
        flops=4 * own * width * n_chip * part,
    )


def core_sum_kernel(n_col, own_ref, other_ref, *outs):
    _, col = place()
    share = own_ref.shape[0] // n_col
    for d in range(n_col):
        rows = block(col ^ d, share)
        outs[d][...] = own_ref[rows, :] + other_ref[rows, :]


def core_sum(own, other, n_col):
    shape = (own.shape[0] // n_col, own.shape[1])
    return kernel_call(
        functools.partial(core_sum_kernel, n_col), [(shape, own.dtype)] * n_col, [], 8, own, other
    )


def rows_of(refs, b):
    lanes = slice(b * WIDTH, (b + 1) * WIDTH)
    parts = []
    for ref in refs:
        if len(ref.shape) == 2:
            parts.append(ref[:, lanes])
        else:
            parts += [ref[i, :, lanes] for i in reversed(range(ref.shape[0]))]
    return jnp.concatenate(parts)


def row_update(refs, g, log_noise):
    blocks = range(len(g))
    peak = functools.reduce(jnp.maximum, [g[b] - rows_of(refs, b) for b in blocks])
    peak = jnp.max(peak, axis=1, keepdims=True)
    total = functools.reduce(jnp.add, [jnp.exp2(g[b] - rows_of(refs, b) - peak) for b in blocks])
    total = jnp.sum(total, axis=1, keepdims=True)
    return -(log_noise + peak + jnp.log2(total))


def data_potentials(stats, wide):
    if not stats:
        return [jnp.zeros((1, WIDTH), jnp.float32)] * (wide // WIDTH)
    own, other = stats
    result = []
    for first in range(0, wide, WIDTH):
        lanes = slice(first, first + WIDTH)
        peak = jnp.maximum(own[0:1, lanes], other[0:1, lanes])
        total = own[1:2, lanes] * jnp.exp2(own[0:1, lanes] - peak)
        total += other[1:2, lanes] * jnp.exp2(other[0:1, lanes] - peak)
        result.append(-(math.log2(wide) + peak + jnp.log2(total)))
    return result


def iteration_kernel(n_groups, log_noise, *refs):
    *refs, out_ref = refs
    wide = out_ref.shape[1]
    chips = [refs[i : i + 3] for i in range(0, 3 * n_groups, 3)]
    g = data_potentials(refs[3 * n_groups :], wide)
    potentials = [row_update(chip, g, log_noise) for chip in chips]
    for b in range(len(g)):
        scores = [f - rows_of(chip, b) for f, chip in zip(potentials, chips)]
        peak = functools.reduce(jnp.maximum, [jnp.max(s, axis=0, keepdims=True) for s in scores])
        total = functools.reduce(jnp.add, [jnp.sum(jnp.exp2(s - peak), axis=0, keepdims=True) for s in scores])
        out_ref[0:1, b * WIDTH : (b + 1) * WIDTH] = peak
        out_ref[1:2, b * WIDTH : (b + 1) * WIDTH] = total


def iteration(tiles, stats, log_noise):
    wide = tiles[0][0].shape[1]
    operands = [piece for group in tiles for piece in group] + list(stats)
    (own,) = kernel_call(
        functools.partial(iteration_kernel, len(tiles), log_noise),
        [((2, wide), jnp.float32)],
        [],
        16,
        *operands,
        flops=16 * sum(piece.size for piece in operands),
    )
    return own, swap_y(own)


def target_kernel(n_col, n_chip, log_noise, *refs):
    tiles, stats, latent_refs = refs[:6], refs[6:8], refs[8 : 8 + n_chip * n_col]
    refs = refs[8 + n_chip * n_col :]
    target_refs, refs = refs[:n_col], refs[n_col:]
    noise_pot_ref, data_pot_ref, pots, weights = refs
    _, col = place()
    height, wide = weights.shape
    g = data_potentials(stats, wide)
    f = row_update(tiles, g, log_noise)
    for b in range(len(g)):
        lanes = slice(b * WIDTH, (b + 1) * WIDTH)
        pots[:, lanes] = g[b] * (1.0 / TO_LOG2)
        scores = (f + g[b] - rows_of(tiles, b)) + log_noise
        weights[:, lanes] = jnp.exp2(scores).astype(jnp.bfloat16)
    data_pot_ref[...] = pots[:, block(col, wide // n_col)]
    own = height // 2
    share = own // n_col
    f = jnp.broadcast_to(f[:own], (own, WIDTH)).T[0:1, :] * (1.0 / TO_LOG2)
    for d in range(n_col):
        noise_pot_ref[pl.ds(col ^ d, 1), :] = f[:, d * share : (d + 1) * share]

    rows_of_one, part = latent_refs[0].shape
    for k in range(n_chip):
        product = jnp.zeros((height, part), jnp.float32)
        for d in range(n_col):
            product += jnp.dot(
                weights[:, block(col ^ d, rows_of_one)],
                latent_refs[k * n_col + d][...],
                preferred_element_type=jnp.float32,
            )
        product = product.astype(jnp.bfloat16)
        for d in range(n_col):
            target_refs[d][0, k] = product[d * share : (d + 1) * share]
            target_refs[d][1, k] = product[own + d * share : own + (d + 1) * share]


def make_targets(own_tiles, other_tiles, stats, latents, n_col, log_noise):
    n_chip = len(latents)
    share, wide = own_tiles[0].shape
    own = n_col * share
    part = latents[0][0].shape[1]
    return kernel_call(
        functools.partial(target_kernel, n_col, n_chip, log_noise),
        [((2, n_chip, share, part), jnp.bfloat16)] * n_col
        + [((n_col, share), jnp.float32), ((1, wide // n_col), jnp.float32)],
        [pltpu.VMEM((1, wide), jnp.float32), pltpu.VMEM((2 * own, wide), jnp.bfloat16)],
        24,
        *own_tiles,
        *other_tiles,
        *stats,
        *[piece for group in latents for piece in group],
        flops=4 * own * wide * n_chip * part,
    )


def join_kernel(n_col, *refs):
    *pieces, out_ref = refs
    row, col = place()
    _, n_chip, _, part = pieces[0].shape
    for i, piece in enumerate(pieces):
        other, d = i // n_col, n_col - 1 - i % n_col
        for k in range(n_chip):
            out_ref[:, block((row ^ other ^ (2 * k)) * n_col + (col ^ d), part)] = piece[other, k]


def join(pieces, n_col):
    _, n_chip, share, part = pieces[0].shape
    shape = (share, n_chip * part * len(pieces))
    (out,) = kernel_call(
        functools.partial(join_kernel, n_col), [(shape, pieces[0].dtype)], [], 12, *pieces
    )
    return out


def per_device_local(noise, data):
    n_col = lax.axis_size("col")
    own, own_data = noise.shape[0], data.shape[0]
    data_0, *dealt = deal(data, n_col)
    own_half, other_half = halve(noise)
    data_1, data_2 = swap(dealt[0], "col", 1), swap(dealt[1], "col", 2)
    x_0, y_0 = swap_x(data_0), swap_y(data_0)
    noise_0, *dealt_noise = deal_noise(own_half, after(swap_core(other_half), x_0, y_0), n_col)
    data_3 = swap(dealt[2], "col", 3)
    across_0 = swap_y(after(x_0, noise_0))
    x_1, y_1 = swap_x(after(data_1, noise_0)), swap_y(after(data_1, noise_0))
    noise_1 = swap(after(dealt_noise[0], data_2), "col", 1)
    across_1 = swap_x(y_1)
    x_2, y_2 = swap_x(after(data_2, x_1)), swap_y(after(data_2, y_1, across_0))
    noise_2 = swap(after(dealt_noise[1], data_3, noise_1), "col", 2)
    across_2 = swap_y(x_2)
    x_3, y_3 = swap_x(after(data_3, across_1, x_2, noise_1)), swap_y(after(data_3, y_2, noise_1))
    noise_3 = swap(after(dealt_noise[2], data_3, noise_1), "col", 3)
    across_3 = swap_x(y_3)
    noise_pieces = [noise_0, noise_1, noise_2, noise_3]
    latents = [
        [data_0, data_1, data_2, data_3],
        [x_0, x_1, x_2, x_3],
        [y_0, y_1, y_2, y_3],
        [across_0, across_1, across_2, across_3],
    ]
    own_part, other_part = partial_cost(noise_pieces, latents)
    parts = col_exchange(core_sum(own_part, swap_core(other_part), n_col))
    tile = functools.reduce(jnp.add, parts[::-1])
    tile_2, tile_1 = swap(tile, "col", 2), swap(tile, "col", 1)
    tile_3 = swap(tile_2, "col", 1)
    x_tile = swap_x(tile)
    pair = after(jnp.stack([tile_2, tile_1]), x_tile)
    tiles = [[tile, pair, tile_3], [x_tile, swap_x(pair), swap_x(tile_3)]]
    other_tiles = [swap_core(piece) for piece in tiles[0]]
    tiles += [other_tiles, [swap_core(piece) for piece in tiles[1]]]
    log_noise = math.log2(own * lax.axis_size("row"))
    stats = ()
    for _ in range(ITERS):
        stats = iteration(tiles, stats, log_noise)
    *products, noise_pot, data_pot = make_targets(tiles[0], other_tiles, stats, latents, n_col, log_noise)
    products = col_exchange(products)
    products = products[::-1]
    targets = join(products + [swap_core(piece) for piece in products], n_col)
    return (targets, noise_pot.reshape((own,)), data_pot.reshape((own_data,)))


def per_device(noise, data):
    n_row, n_col = lax.axis_size("row"), lax.axis_size("col")
    whole = 4 * noise.shape[0] * n_row * data.shape[0] * n_col
    if whole <= LOCAL_COST_BYTES and n_row == 8 and n_col == 4:
        return per_device_local(noise, data)
    return per_device_tiled(noise, data)


def solution(mesh):
    placed = (P("row", "col"), P("col", "row"))
    return jax.shard_map(
        per_device,
        mesh=mesh,
        in_specs=placed,
        out_specs=(P(("row", "col"), None), P("row"), P("col")),
        check_vma=False,
    )
```

```python
import functools
import math

import jax
import jax.numpy as jnp
from jax import lax
from jax.experimental import pallas as pl
from jax.experimental.pallas import tpu as pltpu
from jax.sharding import PartitionSpec as P

LATENT = 16384
ITERS = 3
EPSILON = 0.64 / math.sqrt(LATENT)
LOG2E = math.log2(math.e)
TO_LOG2 = LOG2E / EPSILON
CONTRACT = (((1,), (1,)), ((), ()))
LOCAL_COST_BYTES = 8 * 2**20


def noise_update(cost_tile, data_pot, epsilon, log_count):
    scores = (data_pot[None, :] - cost_tile) / epsilon
    local_peak = jnp.max(scores, axis=1)
    highest = lax.pmax(local_peak, "col")
    summed = lax.psum(jnp.sum(jnp.exp(scores - highest[:, None]), axis=1), "col")
    return -epsilon * (log_count + highest + jnp.log(summed))


def data_update(cost_tile, noise_pot, epsilon, log_count):
    scores = (noise_pot[:, None] - cost_tile) / epsilon
    local_peak = jnp.max(scores, axis=0)
    highest = lax.pmax(local_peak, "row")
    summed = lax.psum(jnp.sum(jnp.exp(scores - highest[None, :]), axis=0), "row")
    return -epsilon * (log_count + highest + jnp.log(summed))


def per_device_tiled(noise, data):
    epsilon = EPSILON
    noise_full = lax.all_gather(noise, "col", axis=1, tiled=True)
    noise_norm = jnp.sum(jnp.square(noise_full.astype(jnp.float32)), axis=1) / LATENT
    noise_rows = noise.shape[0]
    data_rows = data.shape[0]
    data_full = lax.all_gather(data, "row", axis=1, tiled=True)
    data_norm = jnp.sum(jnp.square(data_full.astype(jnp.float32)), axis=1) / LATENT
    cross = lax.dot_general(noise_full, data_full, CONTRACT, preferred_element_type=jnp.float32)
    cost_tile = noise_norm[:, None] + data_norm[None, :] - 2.0 / LATENT * cross
    log_noise = math.log(noise_rows * lax.axis_size("row"))
    log_data = math.log(data_rows * lax.axis_size("col"))
    data_pot = jnp.zeros((data_rows,), jnp.float32)
    for step in range(ITERS):
        noise_pot = noise_update(cost_tile, data_pot, epsilon, log_noise)
        data_pot = data_update(cost_tile, noise_pot, epsilon, log_data)
    noise_pot = noise_update(cost_tile, data_pot, epsilon, log_noise)
    weights = jnp.exp(
        (noise_pot[:, None] + data_pot[None, :] - cost_tile) / epsilon + log_noise
    ).astype(jnp.bfloat16)
    targets = lax.psum_scatter(
        jnp.dot(weights, data_full, preferred_element_type=jnp.float32).astype(jnp.bfloat16),
        "col",
        scatter_dimension=0,
        tiled=True,
    )
    return (targets, noise_pot, data_pot)


VMEM = pl.BlockSpec(memory_space=pltpu.VMEM)
WIDTH = 128


def place():
    return lax.axis_index("row"), lax.axis_index("col")


def swap(array, axis, step):
    count = lax.axis_size(axis)
    return lax.ppermute(array, axis, [(i, i ^ step) for i in range(count)])


def swap_core(array):
    return swap(array, "row", 1)


def swap_x(array):
    return swap(array, "row", 2)


def swap_y(array):
    return swap(array, "row", 4)


def after(array, *others):
    return lax.optimization_barrier((array,) + others)[0]


def col_exchange(pieces):
    count = len(pieces)
    moved = [swap(pieces[d], "col", d) for d in reversed(range(1, count))]
    return [pieces[0]] + moved[::-1]


def chip_gather(pieces):
    along_x, along_y, across = [], [], []
    for i, piece in enumerate(pieces):
        along_x.append(swap_x(piece))
        along_y.append(swap_y(piece))
        across.append(swap_x(along_y[i]) if i % 2 else swap_y(along_x[i]))
    return [pieces, along_x, along_y, across]


def block(index, size):
    return pl.ds(pl.multiple_of(index * size, size), size)


def kernel_call(kernel, outs, scratch, vmem, *operands, flops=0):
    moved = sum(a.size * a.dtype.itemsize for a in operands)
    return pl.pallas_call(
        kernel,
        in_specs=[VMEM] * len(operands),
        out_specs=[VMEM] * len(outs),
        out_shape=[jax.ShapeDtypeStruct(shape, dtype) for shape, dtype in outs],
        scratch_shapes=scratch,
        compiler_params=pltpu.CompilerParams(vmem_limit_bytes=vmem * 2**20),
        cost_estimate=pl.CostEstimate(flops=flops, bytes_accessed=moved, transcendentals=0),
    )(*operands)


def deal_kernel(n_col, data_ref, *outs):
    _, col = place()
    part = data_ref.shape[1] // n_col
    for d in range(n_col):
        outs[d][...] = data_ref[:, block(col ^ d, part)]


def deal(data, n_col):
    piece = (data.shape[0], data.shape[1] // n_col)
    return kernel_call(functools.partial(deal_kernel, n_col), [(piece, data.dtype)] * n_col, [], 8, data)


def halve_kernel(noise_ref, own_ref, other_ref):
    row, _ = place()
    core = lax.rem(row, 2)
    half = own_ref.shape[1]
    own_ref[...] = noise_ref[:, block(core, half)]
    other_ref[...] = noise_ref[:, block(1 - core, half)]


def halve(noise):
    half = (noise.shape[0], noise.shape[1] // 2)
    return kernel_call(halve_kernel, [(half, noise.dtype)] * 2, [], 8, noise)


def deal_noise_kernel(n_col, own_ref, other_ref, *outs):
    _, col = place()
    part = own_ref.shape[1] // n_col
    for d in range(n_col):
        outs[d][0] = own_ref[:, block(col ^ d, part)]
        outs[d][1] = other_ref[:, block(col ^ d, part)]


def deal_noise(own, other, n_col):
    shape = (2, own.shape[0], own.shape[1] // n_col)
    return kernel_call(
        functools.partial(deal_noise_kernel, n_col), [(shape, own.dtype)] * n_col, [], 8, own, other
    )


def cost_kernel(n_col, n_chip, *refs):
    noise_refs, latent_refs = refs[:n_col], refs[n_col : n_col + n_chip * n_col]
    own_ref, other_ref, noise_all = refs[n_col + n_chip * n_col :]
    row, col = place()
    _, own, part = noise_refs[0].shape
    height = latent_refs[0].shape[0]
    for d in range(n_col):
        noise_all[(row // 2) ^ col ^ d] = noise_refs[d][...].reshape(2 * own, part)
    noise_norm = jnp.zeros((2 * own, 1), jnp.float32)
    for k in range(n_chip):
        values = noise_all[k].astype(jnp.float32)
        noise_norm += jnp.sum(values * values, axis=1, keepdims=True)
    for d in range(n_col):
        cross = jnp.zeros((2 * own, height), jnp.float32)
        squares = jnp.zeros((height, part), jnp.float32)
        for k in range(n_chip):
            rows = latent_refs[k * n_col + d][...]
            cross += lax.dot_general(noise_all[k], rows, CONTRACT, preferred_element_type=jnp.float32)
            values = rows.astype(jnp.float32)
            squares += values * values
        norm = jnp.sum(squares, axis=1, keepdims=True)
        norm = jnp.broadcast_to(norm, (height, WIDTH)).T[0:1, :]
        cost = (noise_norm + norm - 2.0 * cross) * (TO_LOG2 / LATENT)
        lanes = block(col ^ d, height)
        own_ref[:, lanes] = cost[:own]
        other_ref[:, lanes] = cost[own:]


def partial_cost(noise_pieces, latents):
    n_chip, n_col = len(latents), len(noise_pieces)
    _, own, part = noise_pieces[0].shape
    width = n_col * latents[0][0].shape[0]
    return kernel_call(
        functools.partial(cost_kernel, n_col, n_chip),
        [((own, width), jnp.float32)] * 2,
        [pltpu.VMEM((n_chip, 2 * own, part), jnp.bfloat16)],
        24,
        *noise_pieces,
        *[piece for group in latents for piece in group],
        flops=4 * own * width * n_chip * part,
    )


def core_sum_kernel(n_col, own_ref, other_ref, *outs):
    _, col = place()
    share = own_ref.shape[0] // n_col
    for d in range(n_col):
        rows = block(col ^ d, share)
        outs[d][...] = own_ref[rows, :] + other_ref[rows, :]


def core_sum(own, other, n_col):
    shape = (own.shape[0] // n_col, own.shape[1])
    return kernel_call(
        functools.partial(core_sum_kernel, n_col), [(shape, own.dtype)] * n_col, [], 8, own, other
    )


def rows_of(refs, b):
    lanes = slice(b * WIDTH, (b + 1) * WIDTH)
    parts = []
    for ref in refs:
        if len(ref.shape) == 2:
            parts.append(ref[:, lanes])
        else:
            parts += [ref[i, :, lanes] for i in range(ref.shape[0])]
    return jnp.concatenate(parts)


def row_update(refs, g, log_noise):
    blocks = range(len(g))
    peak = functools.reduce(jnp.maximum, [g[b] - rows_of(refs, b) for b in blocks])
    peak = jnp.max(peak, axis=1, keepdims=True)
    total = functools.reduce(jnp.add, [jnp.exp2(g[b] - rows_of(refs, b) - peak) for b in blocks])
    total = jnp.sum(total, axis=1, keepdims=True)
    return -(log_noise + peak + jnp.log2(total))


def data_potentials(stats, wide):
    if not stats:
        return [jnp.zeros((1, WIDTH), jnp.float32)] * (wide // WIDTH)
    own, other = stats
    result = []
    for first in range(0, wide, WIDTH):
        lanes = slice(first, first + WIDTH)
        peak = jnp.maximum(own[0:1, lanes], other[0:1, lanes])
        total = own[1:2, lanes] * jnp.exp2(own[0:1, lanes] - peak)
        total += other[1:2, lanes] * jnp.exp2(other[0:1, lanes] - peak)
        result.append(-(math.log2(wide) + peak + jnp.log2(total)))
    return result


def iteration_kernel(n_groups, log_noise, *refs):
    *refs, out_ref = refs
    wide = out_ref.shape[1]
    chips = [refs[i : i + 3] for i in range(0, 3 * n_groups, 3)]
    g = data_potentials(refs[3 * n_groups :], wide)
    potentials = [row_update(chip, g, log_noise) for chip in chips]
    for b in range(len(g)):
        scores = [f - rows_of(chip, b) for f, chip in zip(potentials, chips)]
        peak = functools.reduce(jnp.maximum, [jnp.max(s, axis=0, keepdims=True) for s in scores])
        total = functools.reduce(jnp.add, [jnp.sum(jnp.exp2(s - peak), axis=0, keepdims=True) for s in scores])
        out_ref[0:1, b * WIDTH : (b + 1) * WIDTH] = peak
        out_ref[1:2, b * WIDTH : (b + 1) * WIDTH] = total


def iteration(tiles, stats, log_noise):
    wide = tiles[0][0].shape[1]
    operands = [piece for group in tiles for piece in group] + list(stats)
    (own,) = kernel_call(
        functools.partial(iteration_kernel, len(tiles), log_noise),
        [((2, wide), jnp.float32)],
        [],
        16,
        *operands,
        flops=16 * sum(piece.size for piece in operands),
    )
    return own, swap_y(own)


def target_kernel(n_col, n_chip, log_noise, *refs):
    tiles, stats, latent_refs = refs[:6], refs[6:8], refs[8 : 8 + n_chip * n_col]
    refs = refs[8 + n_chip * n_col :]
    target_refs, refs = refs[:n_col], refs[n_col:]
    noise_pot_ref, data_pot_ref, pots, weights = refs
    _, col = place()
    height, wide = weights.shape
    g = data_potentials(stats, wide)
    f = row_update(tiles, g, log_noise)
    for b in range(len(g)):
        lanes = slice(b * WIDTH, (b + 1) * WIDTH)
        pots[:, lanes] = g[b] * (1.0 / TO_LOG2)
        scores = (f + g[b] - rows_of(tiles, b)) + log_noise
        weights[:, lanes] = jnp.exp2(scores).astype(jnp.bfloat16)
    data_pot_ref[...] = pots[:, block(col, wide // n_col)]
    own = height // 2
    share = own // n_col
    f = jnp.broadcast_to(f[:own], (own, WIDTH)).T[0:1, :] * (1.0 / TO_LOG2)
    for d in range(n_col):
        noise_pot_ref[pl.ds(col ^ d, 1), :] = f[:, d * share : (d + 1) * share]

    rows_of_one, part = latent_refs[0].shape
    for k in range(n_chip):
        product = jnp.zeros((height, part), jnp.float32)
        for d in range(n_col):
            product += jnp.dot(
                weights[:, block(col ^ d, rows_of_one)],
                latent_refs[k * n_col + d][...],
                preferred_element_type=jnp.float32,
            )
        product = product.astype(jnp.bfloat16)
        for d in range(n_col):
            target_refs[d][0, k] = product[d * share : (d + 1) * share]
            target_refs[d][1, k] = product[own + d * share : own + (d + 1) * share]


def make_targets(own_tiles, other_tiles, stats, latents, n_col, log_noise):
    n_chip = len(latents)
    share, wide = own_tiles[0].shape
    own = n_col * share
    part = latents[0][0].shape[1]
    return kernel_call(
        functools.partial(target_kernel, n_col, n_chip, log_noise),
        [((2, n_chip, share, part), jnp.bfloat16)] * n_col
        + [((n_col, share), jnp.float32), ((1, wide // n_col), jnp.float32)],
        [pltpu.VMEM((1, wide), jnp.float32), pltpu.VMEM((2 * own, wide), jnp.bfloat16)],
        24,
        *own_tiles,
        *other_tiles,
        *stats,
        *[piece for group in latents for piece in group],
        flops=4 * own * wide * n_chip * part,
    )


def join_kernel(n_col, *refs):
    *pieces, out_ref = refs
    row, col = place()
    _, n_chip, _, part = pieces[0].shape
    for i, piece in enumerate(pieces):
        other, d = i // n_col, n_col - 1 - i % n_col
        for k in range(n_chip):
            out_ref[:, block((row ^ other ^ (2 * k)) * n_col + (col ^ d), part)] = piece[other, k]


def join(pieces, n_col):
    _, n_chip, share, part = pieces[0].shape
    shape = (share, n_chip * part * len(pieces))
    (out,) = kernel_call(
        functools.partial(join_kernel, n_col), [(shape, pieces[0].dtype)], [], 12, *pieces
    )
    return out


def per_device_local(noise, data):
    n_col = lax.axis_size("col")
    own, own_data = noise.shape[0], data.shape[0]
    data_0, *dealt = deal(data, n_col)
    own_half, other_half = halve(noise)
    data_1, data_2 = swap(dealt[0], "col", 1), swap(dealt[1], "col", 2)
    x_0, y_0 = swap_x(data_0), swap_y(data_0)
    noise_0, *dealt_noise = deal_noise(own_half, after(swap_core(other_half), x_0, y_0), n_col)
    data_3 = swap(dealt[2], "col", 3)
    across_0 = swap_y(after(x_0, noise_0))
    x_1, y_1 = swap_x(after(data_1, noise_0)), swap_y(after(data_1, noise_0))
    noise_1 = swap(after(dealt_noise[0], data_2), "col", 1)
    across_1 = swap_x(y_1)
    x_2, y_2 = swap_x(after(data_2, x_1)), swap_y(after(data_2, y_1, across_0))
    noise_2 = swap(after(dealt_noise[1], data_2), "col", 2)
    across_2 = swap_y(x_2)
    x_3, y_3 = swap_x(after(data_3, across_1, x_2, noise_1)), swap_y(after(data_3, y_2, noise_1))
    noise_3 = swap(after(dealt_noise[2], data_3, noise_1), "col", 3)
    across_3 = swap_x(y_3)
    noise_pieces = [noise_0, noise_1, noise_2, noise_3]
    latents = [
        [data_0, data_1, data_2, data_3],
        [x_0, x_1, x_2, x_3],
        [y_0, y_1, y_2, y_3],
        [across_0, across_1, across_2, across_3],
    ]
    own_part, other_part = partial_cost(noise_pieces, latents)
    parts = col_exchange(core_sum(own_part, swap_core(other_part), n_col))
    tile = functools.reduce(jnp.add, parts[::-1])
    tile_2, tile_1 = swap(tile, "col", 2), swap(tile, "col", 1)
    tile_3 = swap(tile_2, "col", 1)
    x_tile = swap_x(tile)
    pair = after(jnp.stack([tile_1, tile_2]), x_tile)
    tiles = [[tile, pair, tile_3], [x_tile, swap_x(pair), swap_x(tile_3)]]
    other_tiles = [swap_core(piece) for piece in tiles[0]]
    tiles += [other_tiles, [swap_core(piece) for piece in tiles[1]]]
    log_noise = math.log2(own * lax.axis_size("row"))
    stats = ()
    for _ in range(ITERS):
        stats = iteration(tiles, stats, log_noise)
    *products, noise_pot, data_pot = make_targets(tiles[0], other_tiles, stats, latents, n_col, log_noise)
    products = col_exchange(products)
    products = products[::-1]
    targets = join(products + [swap_core(piece) for piece in products], n_col)
    return (targets, noise_pot.reshape((own,)), data_pot.reshape((own_data,)))


def per_device(noise, data):
    n_row, n_col = lax.axis_size("row"), lax.axis_size("col")
    whole = 4 * noise.shape[0] * n_row * data.shape[0] * n_col
    if whole <= LOCAL_COST_BYTES and n_row == 8 and n_col == 4:
        return per_device_local(noise, data)
    return per_device_tiled(noise, data)


def solution(mesh):
    placed = (P("row", "col"), P("col", "row"))
    return jax.shard_map(
        per_device,
        mesh=mesh,
        in_specs=placed,
        out_specs=(P(("row", "col"), None), P("row"), P("col")),
        check_vma=False,
    )
```
